128 devices in a mesh: grp: 4 (over z), env: 32 (over x, y, core).
Axes of the slice: x: 4, y: 4, z: 4, core: 2. Of those that a mesh axis runs over, the one named last changes fastest.
Arguments:
- images: bfloat16 [256, 4, 36, 768], P(('grp', 'env')), may hold values from -6 to 6
- camera_counts: int32 [256], P(('grp', 'env')), may hold values from 1 to 4, as said below
- slot_of: int32 [256], replicated, may hold values from 0 to 255, each once
- patch_weight: bfloat16 [768, 384], replicated, may hold values from -0.21875 to 0.21875
- pos_embed: bfloat16 [36, 384], replicated, may hold values from -3 to 3
- attn_gain: float32 [2, 384], replicated, may hold values from 0.25 to 1.75
- qkv_weight: bfloat16 [2, 384, 1152], replicated, may hold values from -0.3125 to 0.3125
- proj_weight: bfloat16 [2, 384, 384], replicated, may hold values from -0.3125 to 0.3125
- mlp_gain: float32 [2, 384], replicated, may hold values from 0.25 to 1.75
- up_weight: bfloat16 [2, 384, 1536], replicated, may hold values from -0.3125 to 0.3125
- down_weight: bfloat16 [2, 1536, 384], replicated, may hold values from -0.15625 to 0.15625
- final_gain: float32 [384], replicated, may hold values from 0.25 to 1.75
- cotangent: bfloat16 [256, 384], P(('grp', 'env')), may hold values from -6 to 6
Outputs:
- learner_tokens: bfloat16 [256, 384], P(('grp', 'env'))
- grad_patch: float32 [768, 384], P(('grp', 'env'))
- grad_qkv: float32 [2, 384, 1152], P(None, ('grp', 'env'))
- grad_proj: float32 [2, 384, 384], P(None, ('grp', 'env'))
- grad_up: float32 [2, 384, 1536], P(None, ('grp', 'env'))
- grad_down: float32 [2, 1536, 384], P(None, ('grp', 'env'))
The draws below stay inside these ranges and needn't reach their ends.
Inputs may be any that keep to these rules, and one draw needn't show every extreme that they name: `camera_counts`: split the environments into aligned blocks of 2. No block holds more than 7 cameras, and blocks b and b + 16 within the same run of 32 blocks (runs aligned) hold together at most 10 cameras; in every run both bounds are reached.
All inputs are finite; a program needn't handle non-finite values.
Results may differ from the reference program's by a relative error of at most 0.018.
Values may be sent and summed in bfloat16 or wider, within the bound.
No kernel may reach another device: no remote copies, remote signals or barrier semaphores. Data moves between devices by JAX's collectives and lax.ppermute only.
A program may use at most 128 MiB of HBM per device.

```python
from functools import partial
import jax
import jax.numpy as jnp
from jax import lax

D = 384
HEADS = 6
HEAD_DIM = 64
FF = 1536
PATCH_DIM = 768
PATCHES = 36
CAMS = 4
LAYERS = 2
ENV_DEV = 2
BAL_CAP = 5
CAM_MOST = 7
TOTAL_ENVS = 256
N_GRP = 4
N_ENV = 32


def draw_camera_counts(key, part):
    key = jax.random.fold_in(key, 11)
    key_heavy, key_light, key_side, key_slots = jax.random.split(key, 4)
    half_env = N_ENV // 2
    heavy_load = jax.random.randint(key_heavy, (N_GRP, half_env), BAL_CAP, CAM_MOST + 1)
    heavy_load = heavy_load.at[:, 0].set(CAM_MOST)
    room_left = 2 * BAL_CAP - heavy_load
    light_load = ENV_DEV + jax.random.randint(key_light, (N_GRP, half_env), 0, 1 << 20) % (room_left - ENV_DEV + 1)
    light_load = light_load.at[:, 0].set(room_left[:, 0])
    flip_side = jax.random.randint(key_side, (N_GRP, half_env), 0, 2)
    first_half = jnp.where(flip_side == 1, heavy_load, light_load)
    second_half = jnp.where(flip_side == 1, light_load, heavy_load)
    device_loads = jnp.concatenate([first_half, second_half], axis=1)
    extra_units = device_loads - ENV_DEV
    scores = jax.random.randint(key_slots, (N_GRP, N_ENV, 3 * ENV_DEV), 0, 1 << 20) * (3 * ENV_DEV) + jnp.arange(3 * ENV_DEV, dtype=jnp.int32)
    slot_ranks = jnp.argsort(jnp.argsort(scores, axis=-1), axis=-1)
    picked = (slot_ranks < extra_units[:, :, None]).astype(jnp.int32)
    per_env = 1 + jnp.sum(picked.reshape(N_GRP, N_ENV, ENV_DEV, 3), axis=-1)
    return per_env.reshape(-1).astype(jnp.int32)


def level_of(stream_key, extent, pieces, smallest, top_value):
    gain = 1.0
    for axis_at, shards_of in pieces:
        steps = jax.random.uniform(jax.random.fold_in(jax.random.fold_in(stream_key, 6), axis_at), (shards_of,), jnp.float32, smallest / len(pieces), top_value / len(pieces))
        gain = gain * jnp.repeat(jnp.exp(steps), extent[axis_at] // shards_of).reshape((-1,) + (1,) * (len(extent) - 1 - axis_at))
    return gain


def normal_values(stream_key, shape, width, limit, cuts=(), held_as=jnp.bfloat16):
    gain = level_of(stream_key, shape, cuts, -0.22, 0.18) if cuts else 1.0
    values = jax.random.normal(stream_key, shape, jnp.float32) * width * gain
    return jnp.minimum(jnp.maximum(values, -limit), limit).astype(held_as)


def setup_inputs(seed: int = 0) -> dict:
    key_list = jax.random.split(jax.random.key(seed), 14)
    return {
        "images": normal_values(key_list[0], (TOTAL_ENVS, CAMS, PATCHES, PATCH_DIM), 1.0, 6.0, ((0, 128),)),
        "camera_counts": draw_camera_counts(jax.random.fold_in(key_list[13], 71), 0),
        "slot_of": jax.random.permutation(key_list[2], TOTAL_ENVS).astype(jnp.int32),
        "patch_weight": normal_values(key_list[3], (PATCH_DIM, D), PATCH_DIM ** -0.5, 0.21875),
        "pos_embed": normal_values(key_list[4], (PATCHES, D), 0.5, 3.0),
        "attn_gain": jnp.clip(1.0 + 0.15 * jax.random.normal(key_list[5], (LAYERS, D), jnp.float32), 0.25, 1.75),
        "qkv_weight": normal_values(key_list[6], (LAYERS, D, 3 * D), D ** -0.5, 0.3125),
        "proj_weight": normal_values(key_list[7], (LAYERS, D, D), D ** -0.5, 0.3125),
        "mlp_gain": jnp.clip(1.0 + 0.15 * jax.random.normal(key_list[8], (LAYERS, D), jnp.float32), 0.25, 1.75),
        "up_weight": normal_values(key_list[9], (LAYERS, D, FF), D ** -0.5, 0.3125),
        "down_weight": normal_values(key_list[10], (LAYERS, FF, D), FF ** -0.5, 0.15625),
        "final_gain": jnp.clip(1.0 + 0.15 * jax.random.normal(key_list[11], (D,), jnp.float32), 0.25, 1.75),
        "cotangent": normal_values(key_list[12], (TOTAL_ENVS, D), 1.0, 6.0, ((0, 128),)),
    }


def norm_rows(values, gain_row):
    centered = values - lax.optimization_barrier(jnp.mean(values, axis=-1, keepdims=True))
    spread = lax.optimization_barrier(jnp.mean(centered * centered, axis=-1, keepdims=True))
    return centered * lax.rsqrt(spread + 1e-06) * gain_row

def cross_rows(left, right):
    return lax.dot_general(left, right, (((0,), (0,)), ((), ())), preferred_element_type=jnp.float32)

def cross_cols(left, right):
    return lax.dot_general(left, right, (((1,), (1,)), ((), ())), preferred_element_type=jnp.float32)

def attend(triple, cameras):
    shaped = triple.reshape(cameras, -1, 3, HEADS, HEAD_DIM)
    queries = shaped[:, :, 0].astype(jnp.float32)
    key_heads = shaped[:, :, 1].astype(jnp.float32)
    values = shaped[:, :, 2].astype(jnp.float32)
    scores = jnp.einsum('cqhd,ckhd->chqk', queries, key_heads) * HEAD_DIM ** (-0.5)
    raised = jnp.exp(scores)
    attention_probs = (raised / lax.optimization_barrier(jnp.sum(raised, axis=-1, keepdims=True))).astype(jnp.bfloat16)
    mixed_heads = jnp.einsum('chqk,ckhd->cqhd', attention_probs.astype(jnp.float32), values)
    return mixed_heads.reshape(triple.shape[0], -1).astype(jnp.bfloat16)

def layer_forward(stream, params, cameras):
    attn_scale, qkv_matrix, proj_matrix, mlp_scale, up_matrix, down_matrix = params
    normed = norm_rows(stream, attn_scale).astype(jnp.bfloat16)
    triple = jnp.dot(normed, qkv_matrix, preferred_element_type=jnp.float32).astype(jnp.bfloat16)
    mixed_heads = attend(triple, cameras)
    middle = stream + jnp.dot(mixed_heads, proj_matrix, preferred_element_type=jnp.float32)
    second = norm_rows(middle, mlp_scale).astype(jnp.bfloat16)
    before = jnp.dot(second, up_matrix, preferred_element_type=jnp.float32)
    hidden = jax.nn.gelu(before, approximate=False).astype(jnp.bfloat16)
    output = middle + jnp.dot(hidden, down_matrix, preferred_element_type=jnp.float32)
    return (output, (stream, normed, triple, mixed_heads, middle, second, before, hidden))

def layer_backward(upstream, stored, params, cameras):
    attn_scale, qkv_matrix, proj_matrix, mlp_scale, up_matrix, down_matrix = params
    stream, normed, triple, mixed_heads, middle, second, before, hidden = stored
    down_in = upstream.astype(jnp.bfloat16)
    grad_down = cross_rows(hidden, down_in)
    hidden_grad = cross_cols(down_in, down_matrix)
    before_grad = jax.vjp(partial(jax.nn.gelu, approximate=False), before)[1](hidden_grad)[0]
    up_in = before_grad.astype(jnp.bfloat16)
    grad_up = cross_rows(second, up_in)
    second_grad = cross_cols(up_in, up_matrix)
    middle_grad = upstream + jax.vjp(partial(norm_rows, gain_row=mlp_scale), middle)[1](second_grad)[0]
    proj_in = middle_grad.astype(jnp.bfloat16)
    grad_proj = cross_rows(mixed_heads, proj_in)
    mixed_grad = cross_cols(proj_in, proj_matrix).astype(jnp.bfloat16)
    triple_grad = jax.vjp(partial(attend, cameras=cameras), triple)[1](mixed_grad)[0]
    grad_qkv = cross_rows(normed, triple_grad)
    normed_grad = cross_cols(triple_grad, qkv_matrix)
    stream_grad = middle_grad + jax.vjp(partial(norm_rows, gain_row=attn_scale), stream)[1](normed_grad)[0]
    return (stream_grad, (grad_qkv, grad_proj, grad_up, grad_down))

def encode(patches, emb_grad, patch_weight, pos_embed, layer_params, final_gain):
    cameras = patches.shape[0]
    flat_rows = patches.reshape(cameras * PATCHES, PATCH_DIM)
    stream = jnp.dot(flat_rows, patch_weight, preferred_element_type=jnp.float32).reshape(cameras, PATCHES, D)
    stream = (stream + pos_embed.astype(jnp.float32)[None]).reshape(cameras * PATCHES, D)
    stores = []
    for params in layer_params:
        stream, stored = layer_forward(stream, params, cameras)
        stores.append(stored)
    pooled = lax.optimization_barrier(jnp.mean(stream.reshape(cameras, PATCHES, D), axis=1))
    embedded, pull_final = jax.vjp(partial(norm_rows, gain_row=final_gain), pooled)
    pooled_grad = pull_final(emb_grad)[0]
    stream_grad = jnp.broadcast_to(pooled_grad[:, None, :] / PATCHES, (cameras, PATCHES, D)).reshape(cameras * PATCHES, D)
    collected = []
    for layer_index in range(LAYERS - 1, -1, -1):
        stream_grad, layer_grads = layer_backward(stream_grad, stores[layer_index], layer_params[layer_index], cameras)
        collected.insert(0, layer_grads)
    grad_patch = cross_rows(flat_rows, stream_grad.astype(jnp.bfloat16))
    stacks = tuple((jnp.stack([entry[which] for entry in collected]) for which in range(4)))
    return (embedded, (grad_patch,) + stacks)

def reference(images, camera_counts, slot_of, patch_weight, pos_embed, attn_gain, qkv_weight, proj_weight, mlp_gain, up_weight, down_weight, final_gain, cotangent):
    total_envs = images.shape[0]
    capacity = total_envs // ENV_DEV * BAL_CAP
    block_size = 8 * BAL_CAP
    slot_live = (jnp.arange(CAMS, dtype=jnp.int32)[None, :] < camera_counts[:, None]).reshape(-1)
    packed_order = jnp.argsort(jnp.where(slot_live, 0, 1).astype(jnp.int32), stable=True)[:capacity].astype(jnp.int32)
    row_env = packed_order // CAMS
    row_live = slot_live[packed_order]
    counts_float = camera_counts.astype(jnp.float32)
    env_grad = cotangent[slot_of].astype(jnp.float32) / counts_float[:, None]
    row_grad = jnp.where(row_live[:, None], env_grad[row_env], jnp.float32(0.0))
    patches = images.reshape(total_envs * CAMS, PATCHES, PATCH_DIM)[packed_order]
    layer_params = [(attn_gain[index_layer], qkv_weight[index_layer], proj_weight[index_layer], mlp_gain[index_layer], up_weight[index_layer], down_weight[index_layer]) for index_layer in range(LAYERS)]
    initial = (jnp.zeros((PATCH_DIM, D), jnp.float32), jnp.zeros((LAYERS, D, 3 * D), jnp.float32), jnp.zeros((LAYERS, D, D), jnp.float32), jnp.zeros((LAYERS, D, FF), jnp.float32), jnp.zeros((LAYERS, FF, D), jnp.float32))

    def block_step(running, start_row):
        block_patches = lax.dynamic_slice_in_dim(patches, start_row, block_size, 0)
        block_grad = lax.dynamic_slice_in_dim(row_grad, start_row, block_size, 0)
        embedded, grads_block = encode(block_patches, block_grad, patch_weight, pos_embed, layer_params, final_gain)
        return (tuple((first + later for first, later in zip(running, grads_block))), embedded)
    starts = jnp.arange(capacity // block_size, dtype=jnp.int32) * block_size
    totals, embedded = lax.scan(block_step, initial, starts)
    embedded = embedded.reshape(capacity, D)
    summed = jnp.zeros((total_envs, D), jnp.float32).at[row_env].add(jnp.where(row_live[:, None], embedded, jnp.float32(0.0)))
    tokens = (summed / counts_float[:, None]).astype(jnp.bfloat16)
    learner_tokens = jnp.zeros_like(tokens).at[slot_of].set(tokens)
    return (learner_tokens, totals[0], totals[1], totals[2], totals[3], totals[4])
```

```python
from functools import partial

import jax
import jax.numpy as jnp
from jax import lax
from jax.experimental import pallas as pl
from jax.experimental.pallas import tpu as pltpu
from jax.sharding import PartitionSpec as P

F32 = jnp.float32
BF16 = jnp.bfloat16
D = 384
FF = 1536
HEADS = 6
PATCHES = 36
PATCH_DIM = 768
CAMS = 4
SLOTS = 8
CAM_MOST = 7
ROWS = 256
SLOT_ROWS = 48
VMEM_BYTES = 56 * 1024 * 1024
EPS = 1e-06


def mm(left, right):
    return jnp.dot(left, right, preferred_element_type=F32)


def mm_nt(left, right):
    return lax.dot_general(left, right, (((1,), (1,)), ((), ())), preferred_element_type=F32)


def mm_tn(left, right):
    return lax.dot_general(left, right, (((0,), (0,)), ((), ())), preferred_element_type=F32)


def exact_mm(left, right):
    return jnp.dot(left, right, preferred_element_type=F32, precision=lax.Precision.HIGHEST)


def iota(shape, dim):
    return lax.broadcasted_iota(jnp.int32, shape, dim)


def steps_of(value, step, count):
    total = jnp.zeros_like(value)
    for at in range(1, count):
        total = total + jnp.where(value >= at * step, 1, 0)
    return total


def norm_rows(values, gain_row):
    centered = values - jnp.mean(values, axis=-1, keepdims=True)
    spread = jnp.mean(centered * centered, axis=-1, keepdims=True)
    return centered * lax.rsqrt(spread + EPS) * gain_row


def norm_pull(values, gain_row, upstream):
    centered = values - jnp.mean(values, axis=-1, keepdims=True)
    inv = lax.rsqrt(jnp.mean(centered * centered, axis=-1, keepdims=True) + EPS)
    hat = centered * inv
    scaled = upstream * gain_row
    return inv * (
        scaled
        - jnp.mean(scaled, axis=-1, keepdims=True)
        - hat * jnp.mean(scaled * hat, axis=-1, keepdims=True)
    )


def gelu_and_slope(before):
    size = jnp.abs(before)
    bell = jnp.exp(before * before * -0.5)
    t = 1.0 / (1.0 + (0.3275911 * 0.7071067811865476) * size)
    poly = t * (
        0.5 * 0.254829592
        + t
        * (
            0.5 * -0.284496736
            + t * (0.5 * 1.421413741 + t * (0.5 * -1.453152027 + t * (0.5 * 1.061405429)))
        )
    )
    tail = poly * bell
    below = jnp.where(before > 0, 1.0 - tail, tail)
    return before * below, below + before * bell * 0.3989422804014327


def camera_bias():
    cam_row = steps_of(iota((ROWS, 1), 0), PATCHES, CAM_MOST + 1)
    cam_col = steps_of(iota((1, ROWS), 1), PATCHES, CAM_MOST + 1)
    return jnp.where(cam_row == cam_col, 0.0, -1e30)


def head_mask(width_lanes, which):
    lane = iota((1, width_lanes), 1)
    return lane < 64 if which == 0 else lane >= 64


def forward_layer(stream, gain_a, qkv, proj, gain_m, up, down, store):
    normed_s, triple_s, probs_s, mixed_s, middle_s, second_s, hidden_s, slope_s = store
    normed_s[...] = norm_rows(stream, gain_a).astype(BF16)
    for j in range(3):
        cols = pl.ds(j * D, D)
        triple_s[:, cols] = mm(normed_s[...], qkv[:, cols]).astype(BF16)
    bias = camera_bias()
    for pair in range(3):
        q = triple_s[:, pl.ds(pair * 128, 128)]
        k = triple_s[:, pl.ds(D + pair * 128, 128)]
        v = triple_s[:, pl.ds(2 * D + pair * 128, 128)]
        mixed = None
        for h in range(2):
            mask = head_mask(128, h)
            scores = mm_nt(jnp.where(mask, q * 0.125, 0.0).astype(BF16), k) + bias
            raised = jnp.exp(scores)
            probs = (raised * (1.0 / jnp.sum(raised, axis=-1, keepdims=True))).astype(BF16)
            probs_s[pair * 2 + h] = probs
            part = mm(probs, jnp.where(mask, v, 0.0).astype(BF16))
            mixed = part if mixed is None else mixed + part
        mixed_s[:, pl.ds(pair * 128, 128)] = mixed.astype(BF16)
    middle = stream + mm(mixed_s[...], proj[...])
    middle_s[...] = middle
    second_s[...] = norm_rows(middle, gain_m).astype(BF16)
    total = middle
    for j in range(FF // D):
        cols = pl.ds(j * D, D)
        hidden, slope = gelu_and_slope(mm(second_s[...], up[:, cols]))
        slope_s[:, cols] = slope.astype(BF16)
        hidden_s[:, cols] = hidden.astype(BF16)
        total = total + mm(hidden_s[:, cols], down[cols, :])
    return total


def pick(order):
    return jnp.where(order == iota((D, D), 1), 1.0, 0.0).astype(BF16)


def own_first(my_core):
    p = iota((D, 1), 0)
    swap = jnp.where(p >= D // 2, 1, 0)
    core = jnp.where(swap == my_core, 0, 1)
    return core, p - swap * (D // 2)


def order_three(my_core):
    core, rest = own_first(my_core)
    first = steps_of(rest, 48, 4)
    rest = rest - first * 48
    r = steps_of(rest, 16, 3)
    rest = rest - r * 16
    second, z = lax.shift_right_logical(rest, 2), lax.bitwise_and(rest, 3)
    x, y = jnp.where(core == 0, first, second), jnp.where(core == 0, second, first)
    return z * 96 + x * 24 + y * 6 + core * 3 + r


def chips_of(core, rest):
    second, third = lax.shift_right_logical(rest, 2), lax.bitwise_and(rest, 3)
    return jnp.where(core == 0, third * 4 + second, second * 4 + third)


def order_twelve(my_core):
    core, rest = own_first(my_core)
    r = lax.shift_right_logical(rest, 4)
    return chips_of(core, lax.bitwise_and(rest, 15)) * 24 + core * 12 + r


def order_six(my_core):
    core, rest = own_first(my_core)
    z = steps_of(rest, 96, 2)
    rest = rest - z * 96
    r = lax.shift_right_logical(rest, 4)
    return z * 192 + chips_of(core, lax.bitwise_and(rest, 15)) * 12 + core * 6 + r


def turned(order, columns):
    return mm_nt(pick(order), columns).astype(BF16)


def emit(tile, places):
    for at, (ref, first, q) in enumerate(places):
        ref[first, q] = tile[at * 16 : at * 16 + 16].astype(BF16)


def spots_three(refs, q_of):
    return [(ref, a, q_of(r)) for ref in refs for a in range(4) for r in range(3)]


def backward_layer(my_core, upstream, stream, gain_a, qkv, proj, gain_m, up, down, store, keep, send, wide_s):
    downs, wides = (keep[0], send[0]), (keep[1], send[1])
    normed_s, triple_s, probs_s, mixed_s, middle_s, second_s, hidden_s, slope_s = store
    down_in = upstream.astype(BF16)
    order_d = order_three(my_core)
    rows_up = turned(order_d, second_s[...])
    order_down = order_twelve(my_core)
    second_grad = None
    for j in range(FF // D):
        cols = pl.ds(j * D, D)
        tile = mm(turned(order_down, hidden_s[:, cols]), down_in)
        emit(tile, [(ref, j, r) for ref in downs for r in range(12)])
        up_in = (slope_s[:, cols].astype(F32) * mm_nt(down_in, down[cols, :])).astype(BF16)
        emit(mm(rows_up, up_in), spots_three(wides, lambda r: j * 3 + r))
        part = mm_nt(up_in, up[:, cols])
        second_grad = part if second_grad is None else second_grad + part
    middle_grad = upstream + norm_pull(middle_s[...], gain_m, second_grad)
    proj_in = middle_grad.astype(BF16)
    emit(mm(turned(order_d, mixed_s[...]), proj_in), spots_three(wides, lambda r: 21 + r))
    mixed_grad = mm_nt(proj_in, proj[...]).astype(BF16)
    for pair in range(3):
        lanes = pl.ds(pair * 128, 128)
        q = triple_s[:, lanes] * 0.125
        k = triple_s[:, pl.ds(D + pair * 128, 128)]
        v = triple_s[:, pl.ds(2 * D + pair * 128, 128)]
        mg = mixed_grad[:, pair * 128 : pair * 128 + 128]
        product = mg.astype(F32) * mixed_s[:, lanes].astype(F32)
        dq = dk = dv = None
        for h in range(2):
            mask = head_mask(128, h)
            probs = probs_s[pair * 2 + h]
            mg_h = jnp.where(mask, mg, 0.0).astype(BF16)
            delta = jnp.sum(jnp.where(mask, product, 0.0), axis=-1, keepdims=True)
            probs_grad = mm_nt(mg_h, v)
            scores_grad = (probs.astype(F32) * (probs_grad - delta)).astype(BF16)
            part_q = mm(scores_grad, jnp.where(mask, k, 0.0).astype(BF16))
            part_k = mm_tn(scores_grad, jnp.where(mask, q, 0.0).astype(BF16))
            part_v = mm_tn(probs, mg_h)
            dq = part_q if dq is None else dq + part_q
            dk = part_k if dk is None else dk + part_k
            dv = part_v if dv is None else dv + part_v
        wide_s[:, lanes] = (dq * 0.125).astype(BF16)
        wide_s[:, pl.ds(D + pair * 128, 128)] = dk.astype(BF16)
        wide_s[:, pl.ds(2 * D + pair * 128, 128)] = dv.astype(BF16)
    rows_qkv = turned(order_d, normed_s[...])
    normed_grad = None
    for j in range(3):
        cols = pl.ds(j * D, D)
        emit(mm(rows_qkv, wide_s[:, cols]), spots_three(wides, lambda r: 12 + j * 3 + r))
        part = mm_nt(wide_s[:, cols], qkv[:, cols])
        normed_grad = part if normed_grad is None else normed_grad + part
    return middle_grad + norm_pull(stream, gain_a, normed_grad)


def store_shapes():
    return [
        ((ROWS, D), BF16),
        ((ROWS, 3 * D), BF16),
        ((HEADS, ROWS, ROWS), BF16),
        ((ROWS, D), BF16),
        ((ROWS, D), F32),
        ((ROWS, D), BF16),
        ((ROWS, FF), BF16),
        ((ROWS, FF), BF16),
    ]


def of_layer(layer, shape):
    return pl.BlockSpec((None,) + shape, lambda *_: (layer,) + (0,) * len(shape))


def layer_specs(layer):
    return [
        whole((2, D)),
        of_layer(layer, (D, 3 * D)),
        of_layer(layer, (D, D)),
        whole((2, D)),
        of_layer(layer, (D, FF)),
        of_layer(layer, (FF, D)),
    ]


def whole(shape):
    return pl.BlockSpec(shape, lambda *_: (0,) * len(shape))


def shapes_of(items):
    return [jax.ShapeDtypeStruct(s, d) for s, d in items]


def first_kernel(counts, images, patch_weight, pos, gain_a, qkv, proj, gain_m, up, down, *rest):
    rows_o, stream_o, after_o = rest[:3]
    store = rest[3:11]
    flat_s = rest[11]
    for slot in range(SLOTS):
        flat_s[pl.ds(slot * SLOT_ROWS, SLOT_ROWS)] = jnp.zeros((SLOT_ROWS, PATCH_DIM), BF16)
        flat_s[pl.ds(slot * SLOT_ROWS, PATCHES)] = images[slot // CAMS, slot % CAMS]
    first, second = counts[0], counts[1]
    row = iota((ROWS, 1), 0)
    cam = steps_of(row, PATCHES, CAM_MOST + 1)
    patch = row - cam * PATCHES
    slot = jnp.where(cam < first, cam, CAMS + cam - first)
    used = cam < first + second
    source = jnp.where(used, slot * SLOT_ROWS + patch, -1)
    rows = mm(
        jnp.where(source == iota((ROWS, SLOTS * SLOT_ROWS), 1), 1.0, 0.0).astype(BF16), flat_s[...]
    ).astype(BF16)
    rows_o[...] = rows
    place = jnp.where(used & (patch == iota((ROWS, PATCHES), 1)), 1.0, 0.0).astype(BF16)
    stream = mm(rows, patch_weight[...]) + mm(place, pos[...])
    stream_o[...] = stream
    after_o[...] = forward_layer(stream, gain_a[0:1], qkv, proj, gain_m[0:1], up, down, store)


def run_first(counts, images, patch_weight, pos, params):
    return pl.pallas_call(
        first_kernel,
        grid=(1,),
        in_specs=[
            pl.BlockSpec(memory_space=pltpu.SMEM),
            whole((2, CAMS, PATCHES, PATCH_DIM)),
            whole((PATCH_DIM, D)),
            whole((PATCHES, D)),
        ]
        + layer_specs(0),
        out_specs=[whole(s) for s, _ in [((ROWS, PATCH_DIM), BF16), ((ROWS, D), F32), ((ROWS, D), F32)] + store_shapes()],
        out_shape=shapes_of(
            [((ROWS, PATCH_DIM), BF16), ((ROWS, D), F32), ((ROWS, D), F32)] + store_shapes()
        ),
        scratch_shapes=[pltpu.VMEM((SLOTS * SLOT_ROWS, PATCH_DIM), BF16)],
        compiler_params=pltpu.CompilerParams(vmem_limit_bytes=VMEM_BYTES),
        name="first_layer",
    )(counts, images, patch_weight, pos, *params)


def camera_members():
    cam = steps_of(iota((1, ROWS), 1), PATCHES, CAM_MOST + 1)
    return jnp.where(cam == iota((SLOTS, 1), 0), 1.0, 0.0)


def second_kernel(counts, stream, gain_a, qkv, proj, gain_m, up, down, final_gain, *rest):
    pooled_o, tokens_o = rest[:2]
    store = rest[2:10]
    after = forward_layer(stream[...], gain_a[1:2], qkv, proj, gain_m[1:2], up, down, store)
    pooled = exact_mm(camera_members(), after) * (1.0 / PATCHES)
    pooled_o[...] = pooled
    embedded = norm_rows(pooled, final_gain[...])
    first, second = counts[0], counts[1]
    cam = iota((SLOTS, 1), 0)
    in_first = cam < first
    in_second = (cam >= first) & (cam < first + second)
    sum_first = jnp.sum(jnp.where(in_first, embedded, 0.0), axis=0, keepdims=True)
    sum_second = jnp.sum(jnp.where(in_second, embedded, 0.0), axis=0, keepdims=True)
    row = iota((SLOTS, 1), 0)
    count_col = jnp.where(row == 0, first, second).astype(F32)
    both = jnp.where(row == 0, sum_first, jnp.where(row == 1, sum_second, 0.0))
    tokens_o[...] = (both / count_col).astype(BF16)


def run_second(counts, stream, params, final_gain):
    outs = [((SLOTS, D), F32), ((SLOTS, D), BF16)] + store_shapes()
    return pl.pallas_call(
        second_kernel,
        grid=(1,),
        in_specs=[pl.BlockSpec(memory_space=pltpu.SMEM), whole((ROWS, D))]
        + layer_specs(1)
        + [whole((1, D))],
        out_specs=[whole(s) for s, _ in outs],
        out_shape=shapes_of(outs),
        compiler_params=pltpu.CompilerParams(vmem_limit_bytes=VMEM_BYTES),
        name="second_layer",
    )(counts, stream, *params, final_gain)


GRAD_SHAPES = {
    0: [((4, 20, 16, D), BF16), ((4, 24, 16, D), BF16)] * 2,
    1: [((4, 12, 16, D), BF16), ((4, 24, 16, D), BF16)] * 2,
}


def place_of_device():
    env = lax.axis_index("env")
    return (
        lax.axis_index("grp"),
        lax.shift_right_logical(env, 3),
        lax.bitwise_and(lax.shift_right_logical(env, 1), 3),
        lax.bitwise_and(env, 1),
    )


def back_second_kernel(
    counts, arrived, pooled, final_gain, stream, gain_a, qkv, proj, gain_m, up, down, *rest
):
    store = rest[:8]
    keep, send, (grad_o, wide_s) = rest[8:10], rest[10:12], rest[12:]
    my_core = place_of_device()[3]
    first, second = counts[0], counts[1]
    parity = lax.bitwise_and(iota((1, 256), 1), 1)
    rows = mm(jnp.where(parity == iota((SLOTS, 1), 0), 1.0, 0.0).astype(BF16), arrived[...])
    cam = iota((SLOTS, 1), 0)
    seed = jnp.where(
        cam < first,
        rows[0:1] / first.astype(F32),
        jnp.where(cam < first + second, rows[1:2] / second.astype(F32), 0.0),
    )
    pooled_grad = norm_pull(pooled[...], final_gain[...], seed) * (1.0 / PATCHES)
    cam_row = steps_of(iota((ROWS, 1), 0), PATCHES, CAM_MOST + 1)
    member = jnp.where(cam_row == iota((1, SLOTS), 1), 1.0, 0.0)
    upstream = exact_mm(member, pooled_grad)
    grad_o[...] = backward_layer(
        my_core,
        upstream,
        stream[...],
        gain_a[1:2],
        qkv,
        proj,
        gain_m[1:2],
        up,
        down,
        store,
        keep,
        send,
        wide_s,
    )


def run_back_second(counts, arrived, pooled, final_gain, stream, params, store):
    outs = GRAD_SHAPES[1] + [((ROWS, D), F32)]
    return pl.pallas_call(
        back_second_kernel,
        grid=(1,),
        in_specs=[
            pl.BlockSpec(memory_space=pltpu.SMEM),
            whole((256, D)),
            whole((SLOTS, D)),
            whole((1, D)),
            whole((ROWS, D)),
        ]
        + layer_specs(1)
        + [whole(s) for s, _ in store_shapes()],
        out_specs=[whole(s) for s, _ in outs],
        out_shape=shapes_of(outs),
        scratch_shapes=[pltpu.VMEM((ROWS, 3 * D), BF16)],
        compiler_params=pltpu.CompilerParams(vmem_limit_bytes=VMEM_BYTES),
        name="back_second",
    )(counts, arrived, pooled, final_gain, stream, *params, *store)


def back_first_kernel(
    slot_of, upstream, tokens, rows, stream, gain_a, qkv, proj, gain_m, up, down, *rest
):
    store = rest[:8]
    keep, send, wide_s = rest[8:10], rest[10:12], rest[12]
    z, x, y, my_core = place_of_device()
    device = z * 32 + x * 8 + y * 2 + my_core
    p = iota((ROWS, 1), 0)
    swap = jnp.where(p >= 128, 1, 0)
    core = jnp.where(swap == my_core, 0, 1)
    rest_p = p - swap * 128
    row = lax.bitwise_and(lax.shift_right_logical(rest_p, 4), 1)
    chips = chips_of(core, lax.bitwise_and(rest_p, 15))
    learner = lax.shift_right_logical(rest_p, 5) * 64 + chips * 4 + core * 2 + row
    lane = iota((1, SLOTS), 1)
    wanted = jnp.where(
        lane == 0, slot_of[device * 2], jnp.where(lane == 1, slot_of[device * 2 + 1], -1)
    )
    spread = mm(jnp.where(learner == wanted, 1.0, 0.0).astype(BF16), tokens[...]).astype(BF16)
    spots = [(ref, a, r) for ref in (keep[0], send[0]) for a in range(4) for r in range(2)]
    for at, (ref, a, r) in enumerate(spots):
        ref[a, 18 + r] = spread[at * 16 : at * 16 + 16]
    stream_grad = backward_layer(
        my_core,
        upstream[...],
        stream[...],
        gain_a[0:1],
        qkv,
        proj,
        gain_m[0:1],
        up,
        down,
        store,
        keep,
        send,
        wide_s,
    ).astype(BF16)
    order = order_six(my_core)
    for b in range(2):
        tile = mm(turned(order, rows[:, pl.ds(b * D, D)]), stream_grad)
        emit(
            tile,
            [
                (ref, b * 2 + half, 12 + r)
                for ref in (keep[0], send[0])
                for half in range(2)
                for r in range(6)
            ],
        )


def run_back_first(slot_of, upstream, tokens, rows, stream, params, store):
    outs = GRAD_SHAPES[0]
    return pl.pallas_call(
        back_first_kernel,
        grid=(1,),
        in_specs=[
            pl.BlockSpec(memory_space=pltpu.SMEM),
            whole((ROWS, D)),
            whole((SLOTS, D)),
            whole((ROWS, PATCH_DIM)),
            whole((ROWS, D)),
        ]
        + layer_specs(0)
        + [whole(s) for s, _ in store_shapes()],
        out_specs=[whole(s) for s, _ in outs],
        out_shape=shapes_of(outs),
        scratch_shapes=[pltpu.VMEM((ROWS, 3 * D), BF16)],
        compiler_params=pltpu.CompilerParams(vmem_limit_bytes=VMEM_BYTES),
        name="back_first",
    )(slot_of, upstream, tokens, rows, stream, *params, *store)


def local_kernel(kernel, operands, outs, scratch, name):
    return pl.pallas_call(
        kernel,
        grid=(1,),
        in_specs=[whole(v.shape) for v in operands],
        out_specs=[whole(s) for s, _ in outs],
        out_shape=shapes_of(outs),
        scratch_shapes=scratch,
        compiler_params=pltpu.CompilerParams(vmem_limit_bytes=VMEM_BYTES),
        name=name,
    )(*operands)


def add_kernel(keep_d, keep_w, got_d, got_w, *outs):
    z, x, y, my_core = place_of_device()
    along = jnp.where(my_core == 0, x, y)
    for step in range(4):
        at_d, at_w = lax.bitwise_and(z + step, 3), lax.bitwise_and(along + step, 3)
        outs[step][...] = (keep_d[at_d].astype(F32) + got_d[at_d].astype(F32)).astype(BF16)
        outs[4 + step][...] = (keep_w[at_w].astype(F32) + got_w[at_w].astype(F32)).astype(BF16)


def add_pairs(layer, keep, got):
    outs = [(s[1:], BF16) for s, _ in GRAD_SHAPES[layer][:2] for _ in range(4)]
    return local_kernel(add_kernel, (*keep, *got), outs, [], "add_pairs")


def sum_of(refs):
    total = refs[0][...].astype(F32)
    for ref in refs[1:]:
        total = total + ref[...].astype(F32)
    return total


def first_sum_kernel(*rest):
    parts, outs, (total_s, turn_s) = rest[:16], rest[16:20], rest[20:]
    at = 0
    for group in range(4):
        refs = parts[group * 4 : group * 4 + 4]
        count = refs[0].shape[0]
        total_s[pl.ds(at, count)] = sum_of(refs)
        at += count
    for b in range(16):
        turn_s[b // 4, b % 4] = total_s[:, b].astype(BF16)
    _, x, y, my_core = place_of_device()
    along = jnp.where(my_core == 0, y, x)
    for step in range(4):
        outs[step][...] = turn_s[lax.bitwise_and(along + step, 3)]


def first_sum(parts):
    return local_kernel(
        first_sum_kernel,
        parts,
        [((4, 80, D), BF16)] * 4,
        [pltpu.VMEM((80, 16, D), F32), pltpu.VMEM((4, 4, 80, D), BF16)],
        "first_sum",
    )


def second_sum_kernel(*rest):
    parts, outs, total_s = rest[:4], rest[4:12], rest[12]
    total_s[...] = sum_of(parts).astype(BF16)
    z, x, y, my_core = place_of_device()
    along = jnp.where(my_core == 0, x, y)
    for step in range(4):
        outs[step][...] = total_s[lax.bitwise_and(along + step, 3), 0:32]
        outs[4 + step][...] = total_s[lax.bitwise_and(z + step, 3), 32:80]


def second_sum(parts):
    return local_kernel(
        second_sum_kernel,
        parts,
        [((32, D), BF16)] * 4 + [((48, D), BF16)] * 4,
        [pltpu.VMEM((4, 80, D), BF16)],
        "second_sum",
    )


def last_sum_kernel(*rest):
    parts, (tokens, patch, qkv, proj, up, down) = rest[:8], rest[8:]
    rows = sum_of(parts[:4])
    down[1], down[0] = rows[0:12], rows[12:24]
    patch[...] = rows[24:30]
    tokens[...] = rows[30:32].astype(BF16)
    wide = sum_of(parts[4:])
    for layer, at in ((1, 0), (0, 24)):
        for j in range(4):
            up[layer, :, pl.ds(j * D, D)] = wide[at + j * 3 : at + j * 3 + 3]
        for j in range(3):
            qkv[layer, :, pl.ds(j * D, D)] = wide[at + 12 + j * 3 : at + 15 + j * 3]
        proj[layer] = wide[at + 21 : at + 24]


def last_sum(parts):
    return local_kernel(
        last_sum_kernel,
        parts,
        [
            ((2, D), BF16),
            ((6, D), F32),
            ((2, 3, 3 * D), F32),
            ((2, 3, D), F32),
            ((2, 3, FF), F32),
            ((2, 12, D), F32),
        ],
        [],
        "last_sum",
    )


AXES = ("grp", "env")


def send_along(value, axes, step):
    pairs = []
    for device in range(128):
        z, x, y, core = device // 32, device // 8 % 4, device // 2 % 4, device % 2
        place = {"z": z, "x": x, "y": y}
        place[axes[core]] = (place[axes[core]] + step) % 4
        pairs.append((device, place["z"] * 32 + place["x"] * 8 + place["y"] * 2 + core))
    return lax.ppermute(value, AXES, pairs)


def swap_cores(value):
    return lax.ppermute(value, AXES, [(device, device ^ 1) for device in range(128)])


def exchange(pieces, axes):
    return [pieces[0]] + [send_along(pieces[step], axes, step) for step in (1, 3, 2)]


def per_device(
    images,
    camera_counts,
    slot_of,
    patch_weight,
    pos_embed,
    attn_gain,
    qkv_weight,
    proj_weight,
    mlp_gain,
    up_weight,
    down_weight,
    final_gain,
    cotangent,
):
    params = (attn_gain, qkv_weight, proj_weight, mlp_gain, up_weight, down_weight)
    last_gain = final_gain.reshape(1, D)
    device = lax.axis_index(AXES)
    outgoing = jnp.where(
        slot_of[:, None] == device * 2,
        cotangent[0:1],
        jnp.where(slot_of[:, None] == device * 2 + 1, cotangent[1:2], 0),
    ).astype(BF16)
    arrived = lax.all_to_all(outgoing.reshape(128, 2, D), AXES, 0, 0).reshape(256, D)
    rows, stream, middle_stream, *store_first = run_first(
        camera_counts, images, patch_weight, pos_embed, params
    )
    pooled, tokens, *store_second = run_second(camera_counts, middle_stream, params, last_gain)
    *grads, stream_grad = run_back_second(
        camera_counts, arrived, pooled, last_gain, middle_stream, params, store_second
    )
    got = [swap_cores(value) for value in grads[2:]]
    second_pieces = add_pairs(1, grads[:2], got)
    grads = run_back_first(slot_of, stream_grad, tokens, rows, stream, params, store_first)
    got = [swap_cores(value) for value in grads[2:]]
    first_pieces = add_pairs(0, grads[:2], got)
    parts = []
    for pieces, axes in (
        (second_pieces[:4], "zz"),
        (first_pieces[:4], "zz"),
        (second_pieces[4:], "xy"),
        (first_pieces[4:], "xy"),
    ):
        parts += exchange(pieces, axes)
    pieces = first_sum(parts)
    pieces = second_sum(exchange(pieces, "yx"))
    return tuple(last_sum(exchange(pieces[:4], "xy") + exchange(pieces[4:], "zz")))


def solution(mesh):
    placed = (
        P(("grp", "env"), None, None, None),
        P(("grp", "env")),
        P(),
        P(),
        P(),
        P(),
        P(),
        P(),
        P(),
        P(),
        P(),
        P(),
        P(("grp", "env"), None),
    )
    return jax.shard_map(
        per_device,
        mesh=mesh,
        in_specs=placed,
        out_specs=(
            P(("grp", "env"), None),
            P(("grp", "env"), None),
            P(None, ("grp", "env"), None),
            P(None, ("grp", "env"), None),
            P(None, ("grp", "env"), None),
            P(None, ("grp", "env"), None),
        ),
        check_vma=False,
    )
```

```python
from functools import partial

import jax
import jax.numpy as jnp
from jax import lax
from jax.experimental import pallas as pl
from jax.experimental.pallas import tpu as pltpu
from jax.sharding import PartitionSpec as P

F32 = jnp.float32
BF16 = jnp.bfloat16
D = 384
FF = 1536
HEADS = 6
PATCHES = 36
PATCH_DIM = 768
CAMS = 4
SLOTS = 8
CAM_MOST = 7
ROWS = 256
VMEM_BYTES = 20 * 1024 * 1024
SMALL_VMEM_BYTES = 14 * 1024 * 1024
EPS = 1e-06


def mm(left, right):
    return jnp.dot(left, right, preferred_element_type=F32)


def mm_nt(left, right):
    return lax.dot_general(left, right, (((1,), (1,)), ((), ())), preferred_element_type=F32)


def mm_tn(left, right):
    return lax.dot_general(left, right, (((0,), (0,)), ((), ())), preferred_element_type=F32)


def exact_mm(left, right):
    return jnp.dot(left, right, preferred_element_type=F32, precision=lax.Precision.HIGHEST)


def iota(shape, dim):
    return lax.broadcasted_iota(jnp.int32, shape, dim)


def steps_of(value, step, count):
    total = jnp.zeros_like(value)
    for at in range(1, count):
        total = total + jnp.where(value >= at * step, 1, 0)
    return total


def norm_rows(values, gain_row):
    centered = values - jnp.mean(values, axis=-1, keepdims=True)
    spread = jnp.mean(centered * centered, axis=-1, keepdims=True)
    return centered * lax.rsqrt(spread + EPS) * gain_row


def norm_pull(values, gain_row, upstream):
    centered = values - jnp.mean(values, axis=-1, keepdims=True)
    inv = lax.rsqrt(jnp.mean(centered * centered, axis=-1, keepdims=True) + EPS)
    hat = centered * inv
    scaled = upstream * gain_row
    return inv * (
        scaled
        - jnp.mean(scaled, axis=-1, keepdims=True)
        - hat * jnp.mean(scaled * hat, axis=-1, keepdims=True)
    )


def gelu_and_slope(before):
    size = jnp.abs(before)
    bell = jnp.exp(before * before * -0.5)
    t = 1.0 / (1.0 + (0.3275911 * 0.7071067811865476) * size)
    poly = t * (
        0.5 * 0.254829592
        + t
        * (
            0.5 * -0.284496736
            + t * (0.5 * 1.421413741 + t * (0.5 * -1.453152027 + t * (0.5 * 1.061405429)))
        )
    )
    tail = poly * bell
    below = jnp.where(before > 0, 1.0 - tail, tail)
    return before * below, below + before * bell * 0.3989422804014327


def camera_bias():
    cam_row = steps_of(iota((ROWS, 1), 0), PATCHES, CAM_MOST + 1)
    cam_col = steps_of(iota((1, ROWS), 1), PATCHES, CAM_MOST + 1)
    return jnp.where(cam_row == cam_col, 0.0, -1e30)


def head_mask(width_lanes, which):
    lane = iota((1, width_lanes), 1)
    return lane < 64 if which == 0 else lane >= 64


def forward_layer(stream, gain_a, qkv, proj, gain_m, up, down, store, need):
    normed_s, triple_s, probs_s, mixed_s, middle_s, second_s, hidden_s, slope_s = store
    normed_s[...] = norm_rows(stream, gain_a).astype(BF16)
    need(0)
    for j in range(3):
        cols = pl.ds(j * D, D)
        triple_s[:, cols] = mm(normed_s[...], qkv[:, cols]).astype(BF16)
    bias = camera_bias()
    for pair in range(3):
        q = triple_s[:, pl.ds(pair * 128, 128)]
        k = triple_s[:, pl.ds(D + pair * 128, 128)]
        v = triple_s[:, pl.ds(2 * D + pair * 128, 128)]
        mixed = None
        for h in range(2):
            mask = head_mask(128, h)
            scores = mm_nt(jnp.where(mask, q * 0.125, 0.0).astype(BF16), k) + bias
            raised = jnp.exp(scores)
            probs = (raised * (1.0 / jnp.sum(raised, axis=-1, keepdims=True))).astype(BF16)
            probs_s[pair * 2 + h] = probs
            part = mm(probs, jnp.where(mask, v, 0.0).astype(BF16))
            mixed = part if mixed is None else mixed + part
        mixed_s[:, pl.ds(pair * 128, 128)] = mixed.astype(BF16)
    need(1)
    middle = stream + mm(mixed_s[...], proj[...])
    middle_s[...] = middle
    second_s[...] = norm_rows(middle, gain_m).astype(BF16)
    total = middle
    need(2)
    need(3)
    for j in range(FF // D):
        cols = pl.ds(j * D, D)
        hidden, slope = gelu_and_slope(mm(second_s[...], up[:, cols]))
        slope_s[:, cols] = slope.astype(BF16)
        hidden_s[:, cols] = hidden.astype(BF16)
        total = total + mm(hidden_s[:, cols], down[cols, :])
    return total


def pick(order):
    return jnp.where(order == iota((D, D), 1), 1.0, 0.0).astype(BF16)


def own_first(my_core):
    p = iota((D, 1), 0)
    swap = jnp.where(p >= D // 2, 1, 0)
    core = jnp.where(swap == my_core, 0, 1)
    return core, p - swap * (D // 2)


def order_three(my_core):
    core, rest = own_first(my_core)
    first = steps_of(rest, 48, 4)
    rest = rest - first * 48
    r = steps_of(rest, 16, 3)
    rest = rest - r * 16
    z, third = lax.shift_right_logical(rest, 2), lax.bitwise_and(rest, 3)
    x, y = jnp.where(core == 0, first, third), jnp.where(core == 0, third, first)
    return z * 96 + x * 24 + y * 6 + core * 3 + r


def chips_of(core, rest):
    second, third = lax.shift_right_logical(rest, 2), lax.bitwise_and(rest, 3)
    return jnp.where(core == 0, second * 4 + third, third * 4 + second)


def order_twelve(my_core):
    core, rest = own_first(my_core)
    r = lax.shift_right_logical(rest, 4)
    return chips_of(core, lax.bitwise_and(rest, 15)) * 24 + core * 12 + r


def order_six(my_core):
    core, rest = own_first(my_core)
    z = steps_of(rest, 96, 2)
    rest = rest - z * 96
    r = lax.shift_right_logical(rest, 4)
    return z * 192 + chips_of(core, lax.bitwise_and(rest, 15)) * 12 + core * 6 + r


def turned(order, columns):
    return mm_nt(pick(order), columns).astype(BF16)


def emit(tile, places):
    for at, (ref, first, q) in enumerate(places):
        ref[first, q] = tile[at * 16 : at * 16 + 16].astype(BF16)


def spots_three(refs, q_of):
    return [(ref, a, q_of(r)) for ref in refs for a in range(4) for r in range(3)]


def backward_mlp(my_core, upstream, gain_m, proj, up, down, store, keep, send):
    mixed_s, middle_s, second_s, hidden_s, slope_s = store
    downs, wides = (keep[0], send[0]), (keep[1], send[1])
    down_in = upstream.astype(BF16)
    order_d = order_three(my_core)
    rows_up = turned(order_d, second_s[...])
    order_down = order_twelve(my_core)
    second_grad = None
    for j in range(FF // D):
        cols = pl.ds(j * D, D)
        tile = mm(turned(order_down, hidden_s[:, cols]), down_in)
        emit(tile, [(ref, j, r) for ref in downs for r in range(12)])
        up_in = (slope_s[:, cols].astype(F32) * mm_nt(down_in, down[cols, :])).astype(BF16)
        emit(mm(rows_up, up_in), spots_three(wides, lambda r: j * 3 + r))
        part = mm_nt(up_in, up[:, cols])
        second_grad = part if second_grad is None else second_grad + part
    middle_grad = upstream + norm_pull(middle_s[...], gain_m, second_grad)
    proj_in = middle_grad.astype(BF16)
    emit(mm(turned(order_d, mixed_s[...]), proj_in), spots_three(wides, lambda r: 12 + r))
    return middle_grad, mm_nt(proj_in, proj[...]).astype(BF16)


def backward_attention(
    my_core, middle_grad, mixed_grad, stream_s, gain_a, qkv, store, wides, first_q, wide_s
):
    normed_s, triple_s, probs_s, mixed_s = store
    for pair in range(3):
        lanes = pl.ds(pair * 128, 128)
        q = triple_s[:, lanes] * 0.125
        k = triple_s[:, pl.ds(D + pair * 128, 128)]
        v = triple_s[:, pl.ds(2 * D + pair * 128, 128)]
        mg = mixed_grad[:, pair * 128 : pair * 128 + 128]
        product = mg.astype(F32) * mixed_s[:, lanes].astype(F32)
        dq = dk = dv = None
        for h in range(2):
            mask = head_mask(128, h)
            probs = probs_s[pair * 2 + h]
            mg_h = jnp.where(mask, mg, 0.0).astype(BF16)
            delta = jnp.sum(jnp.where(mask, product, 0.0), axis=-1, keepdims=True)
            probs_grad = mm_nt(mg_h, v)
            scores_grad = (probs.astype(F32) * (probs_grad - delta)).astype(BF16)
            part_q = mm(scores_grad, jnp.where(mask, k, 0.0).astype(BF16))
            part_k = mm_tn(scores_grad, jnp.where(mask, q, 0.0).astype(BF16))
            part_v = mm_tn(probs, mg_h)
            dq = part_q if dq is None else dq + part_q
            dk = part_k if dk is None else dk + part_k
            dv = part_v if dv is None else dv + part_v
        wide_s[:, lanes] = (dq * 0.125).astype(BF16)
        wide_s[:, pl.ds(D + pair * 128, 128)] = dk.astype(BF16)
        wide_s[:, pl.ds(2 * D + pair * 128, 128)] = dv.astype(BF16)
    rows_qkv = turned(order_three(my_core), normed_s[...])
    normed_grad = None
    for j in range(3):
        cols = pl.ds(j * D, D)
        emit(mm(rows_qkv, wide_s[:, cols]), spots_three(wides, lambda r: first_q + j * 3 + r))
        part = mm_nt(wide_s[:, cols], qkv[:, cols])
        normed_grad = part if normed_grad is None else normed_grad + part
    return middle_grad + norm_pull(stream_s[...], gain_a, normed_grad)


def store_shapes():
    return [
        ((ROWS, D), BF16),
        ((ROWS, 3 * D), BF16),
        ((HEADS, ROWS, ROWS), BF16),
        ((ROWS, D), BF16),
        ((ROWS, D), F32),
        ((ROWS, D), BF16),
        ((ROWS, FF), BF16),
        ((ROWS, FF), BF16),
    ]


def whole(shape):
    return pl.BlockSpec(shape, lambda *_: (0,) * len(shape))


def shapes_of(items):
    return [jax.ShapeDtypeStruct(s, d) for s, d in items]


WEIGHTS = {
    "qkv": ((D, 3 * D), BF16),
    "proj": ((D, D), BF16),
    "up": ((D, FF), BF16),
    "down": ((FF, D), BF16),
}
STORES = dict(
    zip(
        ("normed", "triple", "probs", "mixed", "middle", "second", "hidden", "slope"),
        store_shapes(),
        strict=True,
    )
)
ANY_SPEC = pl.BlockSpec(memory_space=pl.ANY)
SCALARS = pl.BlockSpec(memory_space=pltpu.SMEM)
IN_VMEM = pl.BlockSpec(memory_space=pltpu.VMEM)
IN_HBM = pl.BlockSpec(memory_space=pltpu.HBM)


def pack_kernel(slot_of, cotangent, out, flat_s, slots_s, own_s, sems):
    z, x, y, my_core = place_of_device()
    device = z * 32 + x * 8 + y * 2 + my_core
    copies = [
        pltpu.make_async_copy(slot_of, slots_s, sems.at[0]),
        pltpu.make_async_copy(cotangent, own_s, sems.at[1]),
    ]
    for copy in copies:
        copy.start()
    for copy in copies:
        copy.wait()
    chosen = jnp.where(slots_s[...][None] == device * 2 + iota((2, 1), 0), 1.0, 0.0)
    flat_s[...] = mm_tn(chosen.astype(BF16), own_s[...])
    for to in range(128):
        out[to] = flat_s[pl.ds(to * 2, 2)].astype(BF16)


def pack_cotangent(slot_of, cotangent):
    return big_kernel(
        pack_kernel,
        [(in_hbm(slot_of), IN_HBM), (in_hbm(cotangent), IN_HBM)],
        [((128, 2, D), BF16)],
        [((256, D), F32), ((256,), jnp.int32), ((2, D), BF16)],
        1000000,
        2,
        "pack_cotangent",
    )[0]


def big_kernel(kernel, operands, outs, scratch, flops, copies, name):
    return pl.pallas_call(
        kernel,
        in_specs=[spec for _, spec in operands],
        out_specs=[IN_VMEM for _ in outs],
        out_shape=shapes_of(outs),
        scratch_shapes=[pltpu.VMEM(s, d) for s, d in scratch]
        + [pltpu.SemaphoreType.DMA((copies,))] * (copies > 0),
        compiler_params=pltpu.CompilerParams(vmem_limit_bytes=VMEM_BYTES),
        cost_estimate=pl.CostEstimate(flops=flops, bytes_accessed=8000000, transcendentals=0),
        name=name,
    )(*[v for v, _ in operands])


def in_hbm(value):
    return pltpu.with_memory_space_constraint(value, pltpu.HBM)


def forward_kernel(
    counts, arrived, images, patch_weight, pos, gain_a, qkv, proj, gain_m, up, down, final_gain, *rest
):
    pooled_o, tokens_o, seeds_o, rows_o, stream_o, after_o = rest[:6]
    stores_o, held, gains = (rest[6:14], rest[14:22]), rest[22:26], rest[26:29]
    flat_s, images_s, patch_s, pos_s, arrived_s, sems = rest[29:]
    first_copies = [
        pltpu.make_async_copy(source, target, sems.at[8 + at])
        for at, (source, target) in enumerate(
            (
                (images, images_s),
                (patch_weight, patch_s),
                (pos, pos_s),
                (gain_a, gains[0]),
                (gain_m, gains[1]),
                (final_gain, gains[2]),
                (arrived, arrived_s),
            )
        )
    ]
    copies = {}
    for layer in range(2):
        for at, (source, target) in enumerate(zip((qkv, proj, up, down), held, strict=True)):
            copies[layer, at] = pltpu.make_async_copy(
                source.at[layer], target.at[layer], sems.at[layer * 4 + at]
            )
    for copy in first_copies + list(copies.values()):
        copy.start()

    def run_layer(layer, stream):
        return forward_layer(
            stream,
            gains[0][layer : layer + 1],
            held[0].at[layer],
            held[1].at[layer],
            gains[1][layer : layer + 1],
            held[2].at[layer],
            held[3].at[layer],
            stores_o[layer],
            lambda at: copies[layer, at].wait(),
        )

    first_copies[0].wait()
    for env in range(2):
        for patch in range(PATCHES):
            at = (env * PATCHES + patch) * CAMS
            flat_s[pl.ds(at, CAMS)] = images_s[env, patch].astype(F32)
    first, second = counts[0], counts[1]
    row = iota((ROWS, 1), 0)
    cam = steps_of(row, PATCHES, CAM_MOST + 1)
    patch = row - cam * PATCHES
    slot = jnp.where(cam < first, cam, CAMS * PATCHES + cam - first)
    used = cam < first + second
    source = jnp.where(used, slot + patch * CAMS, -1)
    rows = mm(
        jnp.where(source == iota((ROWS, SLOTS * PATCHES), 1), 1.0, 0.0).astype(BF16),
        flat_s[...].astype(BF16),
    ).astype(BF16)
    rows_o[...] = rows
    place = jnp.where(used & (patch == iota((ROWS, PATCHES), 1)), 1.0, 0.0).astype(BF16)
    for copy in first_copies[1:]:
        copy.wait()
    seeds_o[...] = jnp.sum(arrived_s[...].astype(F32), axis=0)
    stream = mm(rows, patch_s[...]) + mm(place, pos_s[...])
    stream_o[...] = stream
    after_o[...] = run_layer(0, stream)
    last = run_layer(1, after_o[...])
    pooled = exact_mm(camera_members(), last) * (1.0 / PATCHES)
    pooled_o[...] = pooled
    embedded = norm_rows(pooled, gains[2][...][None])
    cam = iota((SLOTS, 1), 0)
    in_first = cam < first
    in_second = (cam >= first) & (cam < first + second)
    sum_first = jnp.sum(jnp.where(in_first, embedded, 0.0), axis=0, keepdims=True)
    sum_second = jnp.sum(jnp.where(in_second, embedded, 0.0), axis=0, keepdims=True)
    row = iota((SLOTS, 1), 0)
    count_col = jnp.where(row == 0, first, second).astype(F32)
    both = jnp.where(row == 0, sum_first, jnp.where(row == 1, sum_second, 0.0))
    tokens_o[...] = (both / count_col).astype(BF16)


def camera_members():
    cam = steps_of(iota((1, ROWS), 1), PATCHES, CAM_MOST + 1)
    return jnp.where(cam == iota((SLOTS, 1), 0), 1.0, 0.0)


def run_forward(counts, arrived, images, patch_weight, pos, params, final_gain):
    gain_a, qkv, proj, gain_m, up, down = params
    rows = [((ROWS, PATCH_DIM), BF16), ((ROWS, D), F32), ((ROWS, D), F32)]
    sources = (arrived, images, patch_weight, pos, gain_a, qkv, proj, gain_m, up, down, final_gain)
    got = big_kernel(
        forward_kernel,
        [(counts, SCALARS)] + [(in_hbm(v), IN_HBM) for v in sources],
        [((SLOTS, D), F32), ((SLOTS, D), BF16), ((2, D), F32)]
        + rows
        + store_shapes() * 2
        + [((2, *s), d) for s, d in WEIGHTS.values()]
        + [((2, D), F32), ((2, D), F32), ((D,), F32)],
        [
            ((SLOTS * PATCHES, PATCH_DIM), F32),
            (images.shape, BF16),
            ((PATCH_DIM, D), BF16),
            ((PATCHES, D), BF16),
            ((128, 2, D), BF16),
        ],
        12000000000,
        15,
        "forward",
    )
    pooled, tokens, seeds, rows, stream, after = got[:6]
    gain_a, gain_m, final_gain = got[26:29]
    params = (gain_a, *got[22:24], gain_m, *got[24:26])
    return pooled, tokens, seeds, rows, stream, after, got[6:14], got[14:22], params, final_gain


GRAD_COUNTS = {"second": (12, 24), "first_mlp": (12, 15), "first_attention": (8, 9)}


def grad_shapes(group):
    return [((4, n, 16, D), BF16) for n in GRAD_COUNTS[group]] * 2


def place_of_device():
    env = lax.axis_index("env")
    return (
        lax.axis_index("grp"),
        lax.shift_right_logical(env, 3),
        lax.bitwise_and(lax.shift_right_logical(env, 1), 3),
        lax.bitwise_and(env, 1),
    )


SECOND_IN = ("second", "hidden", "down", "slope", "up", "middle", "mixed", "proj")
ATTENTION_IN = ("triple", "probs", "normed", "qkv")


def of_layer(names, refs, layer):
    refs = dict(zip(names, refs))
    return {key: ref.at[layer] if key in WEIGHTS else ref for key, ref in refs.items()}


def back_second_kernel(counts, seeds, pooled, final_gain, gain_a, gain_m, *rest):
    names = SECOND_IN + ATTENTION_IN + ("stream",)
    held, rest = of_layer(names, rest, 1), rest[len(names) :]
    keep, send, grad_o, wide_s = rest[:2], rest[2:4], rest[4], rest[5]
    my_core = place_of_device()[3]
    first, second = counts[0], counts[1]
    cam = iota((SLOTS, 1), 0)
    seed = jnp.where(
        cam < first,
        seeds[0:1] / first.astype(F32),
        jnp.where(cam < first + second, seeds[1:2] / second.astype(F32), 0.0),
    )
    pooled_grad = norm_pull(pooled[...], final_gain[...][None], seed) * (1.0 / PATCHES)
    cam_row = steps_of(iota((ROWS, 1), 0), PATCHES, CAM_MOST + 1)
    member = jnp.where(cam_row == iota((1, SLOTS), 1), 1.0, 0.0)
    upstream = exact_mm(member, pooled_grad)
    middle_grad, mixed_grad = backward_mlp(
        my_core,
        upstream,
        gain_m[1:2],
        held["proj"],
        held["up"],
        held["down"],
        [held[k] for k in ("mixed", "middle", "second", "hidden", "slope")],
        keep,
        send,
    )
    grad_o[...] = backward_attention(
        my_core,
        middle_grad,
        mixed_grad,
        held["stream"],
        gain_a[1:2],
        held["qkv"],
        [held[k] for k in ("normed", "triple", "probs", "mixed")],
        (keep[1], send[1]),
        15,
        wide_s,
    )


def run_back_second(counts, seeds, pooled, final_gain, stream, params, store):
    gain_a, qkv, proj, gain_m, up, down = params
    values = {"qkv": qkv, "proj": proj, "up": up, "down": down, "stream": stream}
    values.update(zip(STORES, store, strict=True))
    names = SECOND_IN + ATTENTION_IN + ("stream",)
    return big_kernel(
        back_second_kernel,
        [(counts, SCALARS)]
        + [(v, IN_VMEM) for v in (seeds, pooled, final_gain, gain_a, gain_m)]
        + [(values[k], IN_VMEM) for k in names],
        grad_shapes("second") + [((ROWS, D), F32)],
        [((ROWS, 3 * D), BF16)],
        8000000000,
        0,
        "back_second",
    )


def back_mlp_kernel(gain_m, *rest):
    names = ("stream",) + SECOND_IN
    held, rest = of_layer(names, rest, 0), rest[len(names) :]
    grads, middle_o, mixed_o = rest[:4], rest[4], rest[5]
    middle_o[...], mixed_o[...] = backward_mlp(
        place_of_device()[3],
        held["stream"][...],
        gain_m[0:1],
        held["proj"],
        held["up"],
        held["down"],
        [held[k] for k in ("mixed", "middle", "second", "hidden", "slope")],
        grads[:2],
        grads[2:],
    )


def run_back_mlp(upstream, params, store):
    _, _, proj, gain_m, up, down = params
    values = {"proj": proj, "up": up, "down": down, "stream": upstream}
    values.update(zip(STORES, store, strict=True))
    names = ("stream",) + SECOND_IN
    return big_kernel(
        back_mlp_kernel,
        [(gain_m, IN_VMEM)] + [(values[k], IN_VMEM) for k in names],
        grad_shapes("first_mlp") + [((ROWS, D), F32), ((ROWS, D), BF16)],
        [],
        5000000000,
        0,
        "back_first_mlp",
    )


def back_attention_kernel(slot_of, tokens, middle_grad, mixed_grad, gain_a, *rest):
    names = ("mixed",) + ATTENTION_IN + ("stream", "rows")
    held, rest = of_layer(names, rest, 0), rest[len(names) :]
    keep, send, wide_s = rest[:2], rest[2:4], rest[4]
    z, x, y, my_core = place_of_device()
    device = z * 32 + x * 8 + y * 2 + my_core
    p = iota((ROWS, 1), 0)
    swap = jnp.where(p >= 128, 1, 0)
    core = jnp.where(swap == my_core, 0, 1)
    rest_p = p - swap * 128
    row = lax.bitwise_and(lax.shift_right_logical(rest_p, 4), 1)
    chips = chips_of(core, lax.bitwise_and(rest_p, 15))
    learner = lax.shift_right_logical(rest_p, 5) * 64 + chips * 4 + core * 2 + row
    lane = iota((1, SLOTS), 1)
    wanted = jnp.where(
        lane == 0, slot_of[device * 2], jnp.where(lane == 1, slot_of[device * 2 + 1], -1)
    )
    spread = mm(jnp.where(learner == wanted, 1.0, 0.0).astype(BF16), tokens[...]).astype(BF16)
    spots = [(ref, a, r) for ref in (keep[0], send[0]) for a in range(4) for r in range(2)]
    for at, (ref, a, r) in enumerate(spots):
        ref[a, 6 + r] = spread[at * 16 : at * 16 + 16]
    stream_grad = backward_attention(
        my_core,
        middle_grad[...],
        mixed_grad[...],
        held["stream"],
        gain_a[0:1],
        held["qkv"],
        [held[k] for k in ("normed", "triple", "probs", "mixed")],
        (keep[1], send[1]),
        0,
        wide_s,
    ).astype(BF16)
    order = order_six(my_core)
    for b in range(2):
        tile = mm(turned(order, held["rows"][:, pl.ds(b * D, D)]), stream_grad)
        emit(
            tile,
            [
                (ref, b * 2 + half, r)
                for ref in (keep[0], send[0])
                for half in range(2)
                for r in range(6)
            ],
        )


def run_back_attention(slot_of, tokens, middle_grad, mixed_grad, rows, stream, params, store):
    values = {"qkv": params[1], "stream": stream, "rows": rows}
    values.update(zip(STORES, store, strict=True))
    names = ("mixed",) + ATTENTION_IN + ("stream", "rows")
    return big_kernel(
        back_attention_kernel,
        [(slot_of, SCALARS)]
        + [(v, IN_VMEM) for v in (tokens, middle_grad, mixed_grad, params[0])]
        + [(values[k], IN_VMEM) for k in names],
        grad_shapes("first_attention"),
        [((ROWS, 3 * D), BF16)],
        4000000000,
        0,
        "back_first_attention",
    )


def local_kernel(kernel, operands, outs, scratch, name):
    return pl.pallas_call(
        kernel,
        in_specs=[IN_VMEM for _ in operands],
        out_specs=[IN_VMEM for _ in outs],
        out_shape=shapes_of(outs),
        scratch_shapes=scratch,
        compiler_params=pltpu.CompilerParams(vmem_limit_bytes=SMALL_VMEM_BYTES),
        name=name,
    )(*operands)


def add_kernel(*rest):
    parts, outs = rest[:-8], rest[-8:]
    z, x, y, my_core = place_of_device()
    along = jnp.where(my_core == 0, x, y)
    for group in range(0, len(parts), 4):
        keep_d, keep_w, got_d, got_w = parts[group : group + 4]
        rows_d = sum(part.shape[1] for part in parts[:group:4])
        rows_w = sum(part.shape[1] for part in parts[1:group:4])
        count_d, count_w = keep_d.shape[1], keep_w.shape[1]
        for step in range(4):
            at_d, at_w = lax.bitwise_and(z + step, 3), lax.bitwise_and(along + step, 3)
            outs[step][pl.ds(rows_d, count_d)] = keep_d[at_d] + got_d[at_d]
            outs[4 + step][pl.ds(rows_w, count_w)] = keep_w[at_w] + got_w[at_w]


def add_pairs(*parts):
    counts = [sum(part.shape[1] for part in parts[at::4]) for at in range(2)]
    return local_kernel(
        add_kernel, parts, [((n, 16, D), BF16) for n in counts for _ in range(4)], [], "add_pairs"
    )


def sum_of(refs):
    total = refs[0][...].astype(F32)
    for ref in refs[1:]:
        total = total + ref[...].astype(F32)
    return total


def first_sum_kernel(*rest):
    parts, outs, (total_s, turn_s) = rest[:8], rest[8:16], rest[16:]
    for group, at, count in ((0, 0, 32), (1, 32, 48)):
        total = sum_of(parts[group * 4 : group * 4 + 4]).reshape(count * 16, D)
        for lanes in range(3):
            total_s[lanes, pl.ds(at * 16, count * 16)] = total[:, lanes * 128 : lanes * 128 + 128]
    for b in range(16):
        for lanes in range(3):
            turn_s[b // 4, b % 4, :, pl.ds(lanes * 128, 128)] = total_s[
                lanes, pl.ds(b, 80, 16)
            ].astype(BF16)
    z, x, y, my_core = place_of_device()
    along = jnp.where(my_core == 0, x, y)
    for step in range(4):
        outs[step][...] = turn_s[lax.bitwise_and(along + step, 3), :, 0:32]
        outs[4 + step][...] = turn_s[lax.bitwise_and(z + step, 3), :, 32:80]


def first_sum(parts):
    return local_kernel(
        first_sum_kernel,
        parts,
        [((4, 32, D), BF16)] * 4 + [((4, 48, D), BF16)] * 4,
        [pltpu.VMEM((3, 1280, 128), F32), pltpu.VMEM((4, 4, 80, D), BF16)],
        "first_sum",
    )


def second_sum_kernel(*rest):
    parts, outs, total_s = rest[:8], rest[8:12], rest[12]
    total_s[:, 0:32] = sum_of(parts[:4]).astype(BF16)
    total_s[:, 32:80] = sum_of(parts[4:]).astype(BF16)
    _, x, y, my_core = place_of_device()
    along = jnp.where(my_core == 0, y, x)
    for step in range(4):
        outs[step][...] = total_s[lax.bitwise_and(along + step, 3)]


def second_sum(parts):
    return local_kernel(
        second_sum_kernel,
        parts,
        [((80, D), BF16)] * 4,
        [pltpu.VMEM((4, 80, D), BF16)],
        "second_sum",
    )


def last_sum_kernel(*rest):
    parts, (tokens, patch, qkv, proj, up, down) = rest[:4], rest[4:]
    rows = sum_of(parts)
    down[:, 1], down[:, 0] = rows[0:12], rows[12:24]
    patch[...] = rows[24:30]
    tokens[...] = rows[30:32].astype(BF16)
    wide = rows[32:80]
    for layer, at in ((1, 0), (0, 24)):
        for j in range(4):
            up[:, layer, pl.ds(j * D, D)] = wide[at + j * 3 : at + j * 3 + 3]
        proj[:, layer] = wide[at + 12 : at + 15]
        for j in range(3):
            qkv[:, layer, pl.ds(j * D, D)] = wide[at + 15 + j * 3 : at + 18 + j * 3]


def last_sum(parts):
    return local_kernel(
        last_sum_kernel,
        parts,
        [
            ((2, D), BF16),
            ((6, D), F32),
            ((3, 2, 3 * D), F32),
            ((3, 2, D), F32),
            ((3, 2, FF), F32),
            ((12, 2, D), F32),
        ],
        [],
        "last_sum",
    )


AXES = ("grp", "env")


def send_along(value, axes, step):
    pairs = []
    for device in range(128):
        z, x, y, core = device // 32, device // 8 % 4, device // 2 % 4, device % 2
        place = {"z": z, "x": x, "y": y}
        place[axes[core]] = (place[axes[core]] + step) % 4
        pairs.append((device, place["z"] * 32 + place["x"] * 8 + place["y"] * 2 + core))
    return lax.ppermute(value, AXES, pairs)


def swap_cores(value):
    return lax.ppermute(value, AXES, [(device, device ^ 1) for device in range(128)])


def exchange(pieces, axes):
    return [pieces[0]] + [send_along(pieces[step], axes, step) for step in (1, 3, 2)]


def per_device(
    images,
    camera_counts,
    slot_of,
    patch_weight,
    pos_embed,
    attn_gain,
    qkv_weight,
    proj_weight,
    mlp_gain,
    up_weight,
    down_weight,
    final_gain,
    cotangent,
):
    params = (attn_gain, qkv_weight, proj_weight, mlp_gain, up_weight, down_weight)
    arrived = lax.all_to_all(pack_cotangent(slot_of, cotangent), AXES, 0, 0)
    (
        pooled,
        tokens,
        seeds,
        rows,
        stream,
        middle_stream,
        store_first,
        store_second,
        params,
        final_gain,
    ) = run_forward(
        camera_counts,
        arrived,
        jnp.swapaxes(images, 1, 2),
        patch_weight,
        pos_embed,
        params,
        final_gain,
    )
    *grads, stream_grad = run_back_second(
        camera_counts, seeds, pooled, final_gain, middle_stream, params, store_second
    )
    got = [swap_cores(value) for value in grads[2:]]
    *mlp_grads, middle_grad, mixed_grad = run_back_mlp(stream_grad, params, store_first)
    mlp_got = [swap_cores(value) for value in mlp_grads[2:]]
    second_parts = (*grads[:2], *got)
    grads = run_back_attention(
        slot_of,
        tokens,
        middle_grad,
        mixed_grad,
        rows,
        stream,
        params,
        store_first,
    )
    got = [swap_cores(value) for value in grads[2:]]
    pieces = add_pairs(*second_parts, *mlp_grads[:2], *mlp_got, *grads[:2], *got)
    pieces = first_sum(exchange(pieces[:4], "zz") + exchange(pieces[4:], "xy"))
    pieces = second_sum(exchange(pieces[:4], "xy") + exchange(pieces[4:], "zz"))
    tokens, patch, *stacks = last_sum(exchange(pieces, "yx"))
    return (tokens, patch, *(jnp.swapaxes(stack, 0, 1) for stack in stacks))


def solution(mesh):
    placed = (
        P(("grp", "env"), None, None, None),
        P(("grp", "env")),
        P(),
        P(),
        P(),
        P(),
        P(),
        P(),
        P(),
        P(),
        P(),
        P(),
        P(("grp", "env"), None),
    )
    return jax.shard_map(
        per_device,
        mesh=mesh,
        in_specs=placed,
        out_specs=(
            P(("grp", "env"), None),
            P(("grp", "env"), None),
            P(None, ("grp", "env"), None),
            P(None, ("grp", "env"), None),
            P(None, ("grp", "env"), None),
            P(None, ("grp", "env"), None),
        ),
        check_vma=False,
    )
```

```python
from functools import partial

import jax
import jax.numpy as jnp
from jax import lax
from jax.experimental import pallas as pl
from jax.experimental.pallas import tpu as pltpu
from jax.sharding import PartitionSpec as P

F32 = jnp.float32
BF16 = jnp.bfloat16
D = 384
FF = 1536
HEADS = 6
PATCHES = 36
PATCH_DIM = 768
CAMS = 4
SLOTS = 8
CAM_MOST = 7
ROWS = 256
VMEM_BYTES = 20 * 1024 * 1024
SMALL_VMEM_BYTES = 14 * 1024 * 1024
EPS = 1e-06


def mm(left, right):
    return jnp.dot(left, right, preferred_element_type=F32)


def mm_nt(left, right):
    return lax.dot_general(left, right, (((1,), (1,)), ((), ())), preferred_element_type=F32)


def mm_tn(left, right):
    return lax.dot_general(left, right, (((0,), (0,)), ((), ())), preferred_element_type=F32)


def exact_mm(left, right):
    return jnp.dot(left, right, preferred_element_type=F32, precision=lax.Precision.HIGHEST)


def iota(shape, dim):
    return lax.broadcasted_iota(jnp.int32, shape, dim)


def steps_of(value, step, count):
    total = jnp.zeros_like(value)
    for at in range(1, count):
        total = total + jnp.where(value >= at * step, 1, 0)
    return total


def norm_rows(values, gain_row):
    centered = values - jnp.mean(values, axis=-1, keepdims=True)
    spread = jnp.mean(centered * centered, axis=-1, keepdims=True)
    return centered * lax.rsqrt(spread + EPS) * gain_row


def norm_pull(values, gain_row, upstream):
    centered = values - jnp.mean(values, axis=-1, keepdims=True)
    inv = lax.rsqrt(jnp.mean(centered * centered, axis=-1, keepdims=True) + EPS)
    hat = centered * inv
    scaled = upstream * gain_row
    return inv * (
        scaled
        - jnp.mean(scaled, axis=-1, keepdims=True)
        - hat * jnp.mean(scaled * hat, axis=-1, keepdims=True)
    )


def gelu_and_slope(before):
    size = jnp.abs(before)
    bell = jnp.exp(before * before * -0.5)
    t = 1.0 / (1.0 + (0.3275911 * 0.7071067811865476) * size)
    poly = t * (
        0.5 * 0.254829592
        + t
        * (
            0.5 * -0.284496736
            + t * (0.5 * 1.421413741 + t * (0.5 * -1.453152027 + t * (0.5 * 1.061405429)))
        )
    )
    tail = poly * bell
    below = jnp.where(before > 0, 1.0 - tail, tail)
    return before * below, below + before * bell * 0.3989422804014327


def camera_bias():
    cam_row = steps_of(iota((ROWS, 1), 0), PATCHES, CAM_MOST + 1)
    cam_col = steps_of(iota((1, ROWS), 1), PATCHES, CAM_MOST + 1)
    return jnp.where(cam_row == cam_col, 0.0, -1e30)


def head_mask(width_lanes, which):
    lane = iota((1, width_lanes), 1)
    return lane < 64 if which == 0 else lane >= 64


def attention_half(stream, gain_a, qkv, proj, store, need):
    normed_s, triple_s, probs_s, mixed_s, middle_s = store
    normed_s[...] = norm_rows(stream, gain_a).astype(BF16)
    need(0)
    for j in range(3):
        cols = pl.ds(j * D, D)
        triple_s[:, cols] = mm(normed_s[...], qkv[:, cols]).astype(BF16)
    bias = camera_bias()
    for pair in range(3):
        q = triple_s[:, pl.ds(pair * 128, 128)]
        k = triple_s[:, pl.ds(D + pair * 128, 128)]
        v = triple_s[:, pl.ds(2 * D + pair * 128, 128)]
        mixed = None
        for h in range(2):
            mask = head_mask(128, h)
            scores = mm_nt(jnp.where(mask, q * 0.125, 0.0).astype(BF16), k) + bias
            raised = jnp.exp(scores)
            probs = (raised * (1.0 / jnp.sum(raised, axis=-1, keepdims=True))).astype(BF16)
            probs_s[pair * 2 + h] = probs
            part = mm(probs, jnp.where(mask, v, 0.0).astype(BF16))
            mixed = part if mixed is None else mixed + part
        mixed_s[:, pl.ds(pair * 128, 128)] = mixed.astype(BF16)
    need(1)
    middle_s[...] = stream + mm(mixed_s[...], proj[...])


def mlp_half(middle, gain_m, up, down, store):
    second_s, hidden_s, slope_s = store
    second_s[...] = norm_rows(middle, gain_m).astype(BF16)
    total = middle
    for j in range(FF // D):
        cols = pl.ds(j * D, D)
        hidden, slope = gelu_and_slope(mm(second_s[...], up[:, cols]))
        slope_s[:, cols] = slope.astype(BF16)
        hidden_s[:, cols] = hidden.astype(BF16)
        total = total + mm(hidden_s[:, cols], down[cols, :])
    return total


def pick(order, width=D):
    return jnp.where(order == iota((D, width), 1), 1.0, 0.0).astype(BF16)


def own_first(my_core):
    p = iota((D, 1), 0)
    swap = jnp.where(p >= D // 2, 1, 0)
    core = jnp.where(swap == my_core, 0, 1)
    return core, p - swap * (D // 2)


def order_three(my_core):
    core, rest = own_first(my_core)
    first = steps_of(rest, 48, 4)
    rest = rest - first * 48
    r = steps_of(rest, 16, 3)
    rest = rest - r * 16
    z, third = lax.shift_right_logical(rest, 2), lax.bitwise_and(rest, 3)
    x, y = jnp.where(core == 0, first, third), jnp.where(core == 0, third, first)
    return z * 96 + x * 24 + y * 6 + core * 3 + r


def chips_of(core, rest):
    second, third = lax.shift_right_logical(rest, 2), lax.bitwise_and(rest, 3)
    return jnp.where(core == 0, second * 4 + third, third * 4 + second)


def order_twelve(my_core):
    core, rest = own_first(my_core)
    r = lax.shift_right_logical(rest, 4)
    return chips_of(core, lax.bitwise_and(rest, 15)) * 24 + core * 12 + r


def order_six(core):
    p = iota((D, 1), 0)
    first = steps_of(p, 96, 4)
    rest = p - first * 96
    r = lax.shift_right_logical(rest, 4)
    rest = lax.bitwise_and(rest, 15)
    z, third = lax.shift_right_logical(rest, 2), lax.bitwise_and(rest, 3)
    x, y = jnp.where(core == 0, first, third), jnp.where(core == 0, third, first)
    return z * 192 + x * 48 + y * 12 + core * 6 + r


def turned(picks, columns):
    return mm_nt(picks, columns).astype(BF16)


def emit(tile, places):
    for at, (ref, first, q) in enumerate(places):
        ref[first, q] = tile[at * 16 : at * 16 + 16].astype(BF16)


def spots_three(refs, q_of):
    return [(ref, a, q_of(r)) for ref in refs for a in range(4) for r in range(3)]


def backward_mlp(my_core, upstream, gain_m, proj, up, down, store, keep, send):
    mixed_s, middle_s, second_s, hidden_s, slope_s = store
    both = (keep, send)
    down_in = upstream.astype(BF16)
    picks = pick(order_three(my_core))
    rows_up = turned(picks, second_s[...])
    picks_down = pick(order_twelve(my_core))
    second_grad = None
    for j in range(FF // D):
        cols = pl.ds(j * D, D)
        tile = mm(turned(picks_down, hidden_s[:, cols]), down_in)
        emit(tile, [(ref, j, r) for ref in both for r in range(12)])
        up_in = (slope_s[:, cols].astype(F32) * mm_nt(down_in, down[cols, :])).astype(BF16)
        emit(mm(rows_up, up_in), spots_three(both, lambda r: 12 + j * 3 + r))
        part = mm_nt(up_in, up[:, cols])
        second_grad = part if second_grad is None else second_grad + part
    middle_grad = upstream + norm_pull(middle_s[...], gain_m, second_grad)
    proj_in = middle_grad.astype(BF16)
    emit(mm(turned(picks, mixed_s[...]), proj_in), spots_three(both, lambda r: 24 + r))
    return middle_grad, mm_nt(proj_in, proj[...]).astype(BF16)


def backward_attention(
    my_core, middle_grad, mixed_grad, stream_s, gain_a, qkv, store, wides, first_q, wide_s
):
    normed_s, triple_s, probs_s, mixed_s = store
    for pair in range(3):
        lanes = pl.ds(pair * 128, 128)
        q = triple_s[:, lanes] * 0.125
        k = triple_s[:, pl.ds(D + pair * 128, 128)]
        v = triple_s[:, pl.ds(2 * D + pair * 128, 128)]
        mg = mixed_grad[:, pair * 128 : pair * 128 + 128]
        product = mg.astype(F32) * mixed_s[:, lanes].astype(F32)
        dq = dk = dv = None
        for h in range(2):
            mask = head_mask(128, h)
            probs = probs_s[pair * 2 + h]
            mg_h = jnp.where(mask, mg, 0.0).astype(BF16)
            delta = jnp.sum(jnp.where(mask, product, 0.0), axis=-1, keepdims=True)
            probs_grad = mm_nt(mg_h, v)
            scores_grad = (probs.astype(F32) * (probs_grad - delta)).astype(BF16)
            part_q = mm(scores_grad, jnp.where(mask, k, 0.0).astype(BF16))
            part_k = mm_tn(scores_grad, jnp.where(mask, q, 0.0).astype(BF16))
            part_v = mm_tn(probs, mg_h)
            dq = part_q if dq is None else dq + part_q
            dk = part_k if dk is None else dk + part_k
            dv = part_v if dv is None else dv + part_v
        wide_s[:, lanes] = (dq * 0.125).astype(BF16)
        wide_s[:, pl.ds(D + pair * 128, 128)] = dk.astype(BF16)
        wide_s[:, pl.ds(2 * D + pair * 128, 128)] = dv.astype(BF16)
    rows_qkv = turned(pick(order_three(my_core)), normed_s[...])
    normed_grad = None
    for j in range(3):
        cols = pl.ds(j * D, D)
        emit(mm(rows_qkv, wide_s[:, cols]), spots_three(wides, lambda r: first_q + j * 3 + r))
        part = mm_nt(wide_s[:, cols], qkv[:, cols])
        normed_grad = part if normed_grad is None else normed_grad + part
    return middle_grad + norm_pull(stream_s[...], gain_a, normed_grad)


def store_shapes():
    return [
        ((ROWS, D), BF16),
        ((ROWS, 3 * D), BF16),
        ((HEADS, ROWS, ROWS), BF16),
        ((ROWS, D), BF16),
        ((ROWS, D), F32),
        ((ROWS, D), BF16),
        ((ROWS, FF), BF16),
        ((ROWS, FF), BF16),
    ]


def whole(shape):
    return pl.BlockSpec(shape, lambda *_: (0,) * len(shape))


def shapes_of(items):
    return [jax.ShapeDtypeStruct(s, d) for s, d in items]


WEIGHTS = {
    "qkv": ((D, 3 * D), BF16),
    "proj": ((D, D), BF16),
    "up": ((D, FF), BF16),
    "down": ((FF, D), BF16),
}
STORES = dict(
    zip(
        ("normed", "triple", "probs", "mixed", "middle", "second", "hidden", "slope"),
        store_shapes(),
        strict=True,
    )
)
ANY_SPEC = pl.BlockSpec(memory_space=pl.ANY)
SCALARS = pl.BlockSpec(memory_space=pltpu.SMEM)
IN_VMEM = pl.BlockSpec(memory_space=pltpu.VMEM)
IN_HBM = pl.BlockSpec(memory_space=pltpu.HBM)


def gather_kernel(axis, *rest):
    pieces, out = rest[:4], rest[5]
    at = dict(zip("zxy", place_of_device()))[axis]
    for step, piece in zip((0, *STEPS), pieces, strict=True):
        out[lax.bitwise_and(at - step, 3)] = piece[...]


def gather_ring(axis, pieces, after):
    return local_kernel(
        partial(gather_kernel, axis),
        (*pieces, after),
        [((4, *pieces[0].shape), BF16)],
        [],
        "gather_ring",
    )[0]


def take_kernel(slot_of, *rest):
    pieces, (own_o, sibling_o, held_s) = rest[:4], rest[4:]
    z, x, y, my_core = place_of_device()
    for step, piece in zip((0, *STEPS), pieces, strict=True):
        held_s[lax.bitwise_and(y - step, 3)] = piece[...].astype(F32)
    device = z * 32 + x * 8 + y * 2 + my_core
    row = iota((2, 1), 0)
    for target, out in ((device, own_o), (lax.bitwise_xor(device, 1), sibling_o)):
        taken = []
        for env in range(2):
            slot = slot_of[target * 2 + env]
            pair = held_s[
                lax.bitwise_and(lax.shift_right_logical(slot, 2), 3),
                lax.bitwise_and(lax.shift_right_logical(slot, 4), 3),
                lax.shift_right_logical(slot, 6),
            ]
            mine = lax.bitwise_and(lax.shift_right_logical(slot, 1), 1) == my_core
            chosen = mine & (row == lax.bitwise_and(slot, 1))
            taken.append(jnp.sum(jnp.where(chosen, pair, 0.0), axis=0, keepdims=True))
        out[...] = jnp.where(row == 0, taken[0], taken[1]).astype(BF16)


def take_rows(slot_of, pieces):
    return pl.pallas_call(
        take_kernel,
        in_specs=[SCALARS] + [IN_VMEM] * 4,
        out_specs=[IN_VMEM] * 2,
        out_shape=shapes_of([((2, D), BF16)] * 2),
        scratch_shapes=[pltpu.VMEM((4, 4, 4, 2, D), F32)],
        compiler_params=pltpu.CompilerParams(vmem_limit_bytes=SMALL_VMEM_BYTES),
        name="take_rows",
    )(slot_of, *pieces)


def big_kernel(kernel, operands, outs, scratch, flops, copies, name):
    return pl.pallas_call(
        kernel,
        in_specs=[spec for _, spec in operands],
        out_specs=[IN_VMEM for _ in outs],
        out_shape=shapes_of(outs),
        scratch_shapes=[(pltpu.VMEM if d != jnp.int32 else pltpu.SMEM)(s, d) for s, d in scratch]
        + [pltpu.SemaphoreType.DMA((copies,))] * (copies > 0),
        compiler_params=pltpu.CompilerParams(vmem_limit_bytes=VMEM_BYTES),
        cost_estimate=pl.CostEstimate(flops=flops, bytes_accessed=8000000, transcendentals=0),
        name=name,
    )(*[v for v, _ in operands])


def in_hbm(value):
    return pltpu.with_memory_space_constraint(value, pltpu.HBM)


def embed_kernel(
    counts, images, patch_weight, pos, gain_a, qkv, proj, gain_m, up, down, final_gain, *rest
):
    rows_o, stream_o, store, held, gains = rest[0], rest[1], rest[2:7], rest[7:11], rest[11:14]
    counts_o, flat_s, images_s, patch_s, pos_s, sems = rest[14:]
    first_copies = [
        pltpu.make_async_copy(source, target, sems.at[8 + at])
        for at, (source, target) in enumerate(
            (
                (images, images_s),
                (counts, counts_o),
                (patch_weight, patch_s),
                (pos, pos_s),
                (gain_a, gains[0]),
                (gain_m, gains[1]),
                (final_gain, gains[2]),
            )
        )
    ]
    copies = {}
    for layer in range(2):
        for at, (source, target) in enumerate(zip((qkv, proj, up, down), held, strict=True)):
            copies[layer, at] = pltpu.make_async_copy(
                source.at[layer], target.at[layer], sems.at[layer * 4 + at]
            )
    for copy in first_copies + list(copies.values()):
        copy.start()
    first_copies[0].wait()
    for env in range(2):
        for patch in range(PATCHES):
            at = (env * PATCHES + patch) * CAMS
            flat_s[pl.ds(at, CAMS)] = images_s[env, patch].astype(F32)
    first_copies[1].wait()
    first, second = counts_o[0], counts_o[1]
    row = iota((ROWS, 1), 0)
    cam = steps_of(row, PATCHES, CAM_MOST + 1)
    patch = row - cam * PATCHES
    slot = jnp.where(cam < first, cam, CAMS * PATCHES + cam - first)
    used = cam < first + second
    source = jnp.where(used, slot + patch * CAMS, -1)
    rows = mm(
        jnp.where(source == iota((ROWS, SLOTS * PATCHES), 1), 1.0, 0.0).astype(BF16),
        flat_s[...].astype(BF16),
    ).astype(BF16)
    rows_o[...] = rows
    place = jnp.where(used & (patch == iota((ROWS, PATCHES), 1)), 1.0, 0.0).astype(BF16)
    for copy in first_copies[2:]:
        copy.wait()
    stream = mm(rows, patch_s[...]) + mm(place, pos_s[...])
    stream_o[...] = stream
    attention_half(
        stream,
        gains[0][0:1],
        held[0].at[0],
        held[1].at[0],
        store,
        lambda at: copies[0, at].wait(),
    )
    for key in ((0, 2), (0, 3), (1, 0), (1, 1), (1, 2), (1, 3)):
        copies[key].wait()


STORE_A = ("normed", "triple", "probs", "mixed", "middle")
STORE_M = ("second", "hidden", "slope")


def run_embed(counts, images, patch_weight, pos, params, final_gain):
    gain_a, qkv, proj, gain_m, up, down = params
    sources = (counts, images, patch_weight, pos, gain_a, qkv, proj, gain_m, up, down, final_gain)
    got = big_kernel(
        embed_kernel,
        [(in_hbm(v), IN_HBM) for v in sources],
        [((ROWS, PATCH_DIM), BF16), ((ROWS, D), F32)]
        + [STORES[k] for k in STORE_A]
        + [((2, *s), d) for s, d in WEIGHTS.values()]
        + [((2, D), F32), ((2, D), F32), ((D,), F32)],
        [
            ((2,), jnp.int32),
            ((SLOTS * PATCHES, PATCH_DIM), F32),
            (images.shape, BF16),
            ((PATCH_DIM, D), BF16),
            ((PATCHES, D), BF16),
        ],
        7000000000,
        15,
        "embed_attend",
    )
    gain_a, gain_m, final_gain = got[11:14]
    params = (gain_a, *got[7:9], gain_m, *got[9:11])
    return got[0], got[1], dict(zip(STORE_A, got[2:7])), params, final_gain


def middle_kernel(middle, gain_a, gain_m, up, down, qkv, proj, _, *rest):
    stream_o, store_m, store_a = rest[0], rest[1:4], rest[4:9]
    stream_o[...] = mlp_half(middle[...], gain_m[0:1], up.at[0], down.at[0], store_m)
    attention_half(
        stream_o[...], gain_a[1:2], qkv.at[1], proj.at[1], store_a, lambda at: None
    )


def run_middle(middle, params, after):
    gain_a, qkv, proj, gain_m, up, down = params
    got = big_kernel(
        middle_kernel,
        [(v, IN_VMEM) for v in (middle, gain_a, gain_m, up, down, qkv, proj)] + [(after, ANY_SPEC)],
        [((ROWS, D), F32)] + [STORES[k] for k in STORE_M + STORE_A],
        [],
        6000000000,
        0,
        "mlp_attend",
    )
    return got[0], dict(zip(STORE_M, got[1:4])), dict(zip(STORE_A, got[4:9]))


def pool_kernel(counts, middle, gain_m, up, down, final_gain, _, *rest):
    pooled_o, tokens_o, store_m = rest[0], rest[1], rest[2:5]
    last = mlp_half(middle[...], gain_m[1:2], up.at[1], down.at[1], store_m)
    pooled = exact_mm(camera_members(), last) * (1.0 / PATCHES)
    pooled_o[...] = pooled
    embedded = norm_rows(pooled, final_gain[...][None])
    first, second = counts[0], counts[1]
    cam = iota((SLOTS, 1), 0)
    in_first = cam < first
    in_second = (cam >= first) & (cam < first + second)
    sum_first = jnp.sum(jnp.where(in_first, embedded, 0.0), axis=0, keepdims=True)
    sum_second = jnp.sum(jnp.where(in_second, embedded, 0.0), axis=0, keepdims=True)
    row = iota((SLOTS, 1), 0)
    count_col = jnp.where(row == 0, first, second).astype(F32)
    both = jnp.where(row == 0, sum_first, jnp.where(row == 1, sum_second, 0.0))
    tokens_o[...] = (both / count_col).astype(BF16)


def run_pool(counts, middle, params, final_gain, after):
    _, _, _, gain_m, up, down = params
    got = big_kernel(
        pool_kernel,
        [(counts, SCALARS)]
        + [(v, IN_VMEM) for v in (middle, gain_m, up, down, final_gain)]
        + [(after, ANY_SPEC)],
        [((SLOTS, D), F32), ((SLOTS, D), BF16)] + [STORES[k] for k in STORE_M],
        [],
        4000000000,
        0,
        "mlp_pool",
    )
    return got[0], got[1], dict(zip(STORE_M, got[2:5]))


def camera_members():
    cam = steps_of(iota((1, ROWS), 1), PATCHES, CAM_MOST + 1)
    return jnp.where(cam == iota((SLOTS, 1), 0), 1.0, 0.0)


GRAD_COUNTS = {"second": (12, 24), "first_mlp": (12, 15), "first_attention": (0, 17)}


ROWS_D, ROWS_W = (sum(n) for n in zip(*GRAD_COUNTS.values()))


def grad_shapes(group):
    return [((4, sum(GRAD_COUNTS[group]), 16, D), BF16)] * 2


def place_of_device():
    env = lax.axis_index("env")
    return (
        lax.axis_index("grp"),
        lax.shift_right_logical(env, 3),
        lax.bitwise_and(lax.shift_right_logical(env, 1), 3),
        lax.bitwise_and(env, 1),
    )


SECOND_IN = ("second", "hidden", "down", "slope", "up", "middle", "mixed", "proj")
ATTENTION_IN = ("triple", "probs", "normed", "qkv")


def of_layer(names, refs, layer):
    refs = dict(zip(names, refs))
    return {key: ref.at[layer] if key in WEIGHTS else ref for key, ref in refs.items()}


def back_second_kernel(counts, own, other, pooled, final_gain, gain_a, gain_m, *rest):
    names = SECOND_IN + ATTENTION_IN + ("stream",)
    held, rest = of_layer(names, rest, 1), rest[len(names) :]
    keep, send, grad_o, wide_s = rest
    my_core = place_of_device()[3]
    first, second = counts[0], counts[1]
    seeds = own[...].astype(F32) + other[...].astype(F32)
    cam = iota((SLOTS, 1), 0)
    seed = jnp.where(
        cam < first,
        seeds[0:1] / first.astype(F32),
        jnp.where(cam < first + second, seeds[1:2] / second.astype(F32), 0.0),
    )
    pooled_grad = norm_pull(pooled[...], final_gain[...][None], seed) * (1.0 / PATCHES)
    cam_row = steps_of(iota((ROWS, 1), 0), PATCHES, CAM_MOST + 1)
    member = jnp.where(cam_row == iota((1, SLOTS), 1), 1.0, 0.0)
    upstream = exact_mm(member, pooled_grad)
    middle_grad, mixed_grad = backward_mlp(
        my_core,
        upstream,
        gain_m[1:2],
        held["proj"],
        held["up"],
        held["down"],
        [held[k] for k in ("mixed", "middle", "second", "hidden", "slope")],
        keep,
        send,
    )
    grad_o[...] = backward_attention(
        my_core,
        middle_grad,
        mixed_grad,
        held["stream"],
        gain_a[1:2],
        held["qkv"],
        [held[k] for k in ("normed", "triple", "probs", "mixed")],
        (keep, send),
        27,
        wide_s,
    )


def run_back_second(counts, own, other, pooled, final_gain, stream, params, store):
    gain_a, qkv, proj, gain_m, up, down = params
    values = {"qkv": qkv, "proj": proj, "up": up, "down": down, "stream": stream}
    values.update(store)
    names = SECOND_IN + ATTENTION_IN + ("stream",)
    return big_kernel(
        back_second_kernel,
        [(counts, SCALARS)]
        + [(v, IN_VMEM) for v in (own, other, pooled, final_gain, gain_a, gain_m)]
        + [(values[k], IN_VMEM) for k in names],
        grad_shapes("second") + [((ROWS, D), F32)],
        [((ROWS, 3 * D), BF16)],
        8000000000,
        0,
        "back_second",
    )


def back_mlp_kernel(gain_m, *rest):
    names = ("stream",) + SECOND_IN
    held, rest = of_layer(names, rest, 0), rest[len(names) :]
    keep, send, middle_o, mixed_o = rest
    middle_o[...], mixed_o[...] = backward_mlp(
        place_of_device()[3],
        held["stream"][...],
        gain_m[0:1],
        held["proj"],
        held["up"],
        held["down"],
        [held[k] for k in ("mixed", "middle", "second", "hidden", "slope")],
        keep,
        send,
    )


def run_back_mlp(upstream, params, store):
    _, _, proj, gain_m, up, down = params
    values = {"proj": proj, "up": up, "down": down, "stream": upstream}
    values.update(store)
    names = ("stream",) + SECOND_IN
    return big_kernel(
        back_mlp_kernel,
        [(gain_m, IN_VMEM)] + [(values[k], IN_VMEM) for k in names],
        grad_shapes("first_mlp") + [((ROWS, D), F32), ((ROWS, D), BF16)],
        [],
        5000000000,
        0,
        "back_first_mlp",
    )


def back_attention_kernel(slot_of, tokens, middle_grad, mixed_grad, gain_a, *rest):
    names = ("mixed",) + ATTENTION_IN + ("stream", "rows")
    held, rest = of_layer(names, rest, 0), rest[len(names) :]
    keep, send, wide_s = rest
    z, x, y, my_core = place_of_device()
    device = z * 32 + x * 8 + y * 2 + my_core
    p = iota((ROWS, 1), 0)
    swap = jnp.where(p >= 128, 1, 0)
    core = jnp.where(swap == my_core, 0, 1)
    rest_p = p - swap * 128
    first = lax.shift_right_logical(rest_p, 5)
    row = lax.bitwise_and(lax.shift_right_logical(rest_p, 4), 1)
    third = lax.bitwise_and(rest_p, 3)
    to_x, to_y = jnp.where(core == 0, first, third), jnp.where(core == 0, third, first)
    to_z = lax.bitwise_and(lax.shift_right_logical(rest_p, 2), 3)
    learner = to_z * 64 + to_x * 16 + to_y * 4 + core * 2 + row
    lane = iota((1, SLOTS), 1)
    wanted = jnp.where(
        lane == 0, slot_of[device * 2], jnp.where(lane == 1, slot_of[device * 2 + 1], -1)
    )
    spread = mm(jnp.where(learner == wanted, 1.0, 0.0).astype(BF16), tokens[...]).astype(BF16)
    spots = [(ref, a, r) for ref in (keep, send) for a in range(4) for r in range(2)]
    for at, (ref, a, r) in enumerate(spots):
        ref[a, 15 + r] = spread[at * 16 : at * 16 + 16]
    stream_grad = backward_attention(
        my_core,
        middle_grad[...],
        mixed_grad[...],
        held["stream"],
        gain_a[0:1],
        held["qkv"],
        [held[k] for k in ("normed", "triple", "probs", "mixed")],
        (keep, send),
        0,
        wide_s,
    ).astype(BF16)
    for ref, core in ((keep, my_core), (send, 1 - my_core)):
        tile = mm(turned(pick(order_six(core), PATCH_DIM), held["rows"][...]), stream_grad)
        emit(tile, [(ref, a, 9 + r) for a in range(4) for r in range(6)])


def run_back_attention(slot_of, tokens, middle_grad, mixed_grad, rows, stream, params, store):
    values = {"qkv": params[1], "stream": stream, "rows": rows}
    values.update(store)
    names = ("mixed",) + ATTENTION_IN + ("stream", "rows")
    return big_kernel(
        back_attention_kernel,
        [(slot_of, SCALARS)]
        + [(v, IN_VMEM) for v in (tokens, middle_grad, mixed_grad, params[0])]
        + [(values[k], IN_VMEM) for k in names],
        grad_shapes("first_attention"),
        [((ROWS, 3 * D), BF16)],
        4000000000,
        0,
        "back_first_attention",
    )


def local_kernel(kernel, operands, outs, scratch, name):
    return pl.pallas_call(
        kernel,
        in_specs=[IN_VMEM for _ in operands],
        out_specs=[IN_VMEM for _ in outs],
        out_shape=shapes_of(outs),
        scratch_shapes=scratch,
        compiler_params=pltpu.CompilerParams(vmem_limit_bytes=SMALL_VMEM_BYTES),
        name=name,
    )(*operands)


def add_kernel(*rest):
    parts, outs = rest[:-8], rest[-8:]
    z, x, y, my_core = place_of_device()
    along = jnp.where(my_core == 0, x, y)
    at_d = at_w = 0
    for group, (count_d, count_w) in enumerate(GRAD_COUNTS.values()):
        keep, got = parts[group * 2 : group * 2 + 2]
        for step in range(4):
            place_d, place_w = lax.bitwise_and(z + step, 3), lax.bitwise_and(along + step, 3)
            if count_d:
                span = pl.ds(0, count_d)
                outs[step][pl.ds(at_d, count_d)] = keep[place_d, span] + got[place_d, span]
            span = pl.ds(count_d, count_w)
            outs[4 + step][pl.ds(at_w, count_w)] = keep[place_w, span] + got[place_w, span]
        at_d, at_w = at_d + count_d, at_w + count_w


def add_pairs(*parts):
    return local_kernel(
        add_kernel,
        parts,
        [((ROWS_D, 16, D), BF16)] * 4 + [((ROWS_W, 16, D), BF16)] * 4,
        [],
        "add_pairs",
    )


def sum_of(refs):
    total = refs[0][...].astype(F32)
    for ref in refs[1:]:
        total = total + ref[...].astype(F32)
    return total


def first_sum_kernel(*rest):
    parts, outs, (total_s, turn_d, turn_w) = rest[:8], rest[8:16], rest[16:]
    for group, at, count in ((0, 0, ROWS_D), (1, ROWS_D, ROWS_W)):
        total = sum_of(parts[group * 4 : group * 4 + 4]).reshape(count * 16, D)
        for lanes in range(3):
            total_s[lanes, pl.ds(at * 16, count * 16)] = total[:, lanes * 128 : lanes * 128 + 128]
    for b in range(16):
        for lanes in range(3):
            cols = pl.ds(lanes * 128, 128)
            turn_d[b // 4, pl.ds(b % 4 * ROWS_D, ROWS_D), cols] = total_s[
                lanes, pl.ds(b, ROWS_D, 16)
            ]
            turn_w[b // 4, pl.ds(b % 4 * ROWS_W, ROWS_W), cols] = total_s[
                lanes, pl.ds(ROWS_D * 16 + b, ROWS_W, 16)
            ]
    z, x, y, my_core = place_of_device()
    along = jnp.where(my_core == 0, x, y)
    for step in range(4):
        outs[step][...] = turn_d[lax.bitwise_and(along + step, 3)].astype(BF16)
        outs[4 + step][...] = turn_w[lax.bitwise_and(z + step, 3)].astype(BF16)


def first_sum(parts):
    return local_kernel(
        first_sum_kernel,
        parts,
        [((4 * ROWS_D, D), BF16)] * 4 + [((4 * ROWS_W, D), BF16)] * 4,
        [
            pltpu.VMEM((3, 1280, 128), F32),
            pltpu.VMEM((4, 4 * ROWS_D, D), F32),
            pltpu.VMEM((4, 4 * ROWS_W, D), F32),
        ],
        "first_sum",
    )


def second_sum_kernel(*rest):
    parts, outs, total_s = rest[:8], rest[8:12], rest[12]
    total_d, total_w = sum_of(parts[:4]), sum_of(parts[4:])
    for third in range(4):
        total_s[third, pl.ds(0, ROWS_D)] = total_d[third * ROWS_D : (third + 1) * ROWS_D]
        total_s[third, pl.ds(ROWS_D, ROWS_W)] = total_w[third * ROWS_W : (third + 1) * ROWS_W]
    _, x, y, my_core = place_of_device()
    along = jnp.where(my_core == 0, y, x)
    for step in range(4):
        outs[step][...] = total_s[lax.bitwise_and(along + step, 3)].astype(BF16)


def second_sum(parts):
    return local_kernel(
        second_sum_kernel,
        parts,
        [((ROWS_D + ROWS_W, D), BF16)] * 4,
        [pltpu.VMEM((4, ROWS_D + ROWS_W, D), F32)],
        "second_sum",
    )


def last_sum_kernel(*rest):
    parts, (tokens, patch, qkv, proj, up, down) = rest[:4], rest[4:]
    rows = sum_of(parts)
    down[:, 1], down[:, 0] = rows[0:12], rows[12:24]
    wide = rows[ROWS_D:]
    for layer, at_up, at_qkv in ((1, 0, 15), (0, 24, 39)):
        for j in range(4):
            up[:, layer, pl.ds(j * D, D)] = wide[at_up + j * 3 : at_up + j * 3 + 3]
        proj[:, layer] = wide[at_up + 12 : at_up + 15]
        for j in range(3):
            qkv[:, layer, pl.ds(j * D, D)] = wide[at_qkv + j * 3 : at_qkv + j * 3 + 3]
    patch[...] = wide[48:54]
    tokens[...] = wide[54:56].astype(BF16)


def last_sum(parts):
    return local_kernel(
        last_sum_kernel,
        parts,
        [
            ((2, D), BF16),
            ((6, D), F32),
            ((3, 2, 3 * D), F32),
            ((3, 2, D), F32),
            ((3, 2, FF), F32),
            ((12, 2, D), F32),
        ],
        [],
        "last_sum",
    )


AXES = ("grp", "env")
STEPS = (2, 1, 3)


def send_along(value, axes, step):
    pairs = []
    for device in range(128):
        z, x, y, core = device // 32, device // 8 % 4, device // 2 % 4, device % 2
        place = {"z": z, "x": x, "y": y}
        place[axes[core]] = (place[axes[core]] + step) % 4
        pairs.append((device, place["z"] * 32 + place["x"] * 8 + place["y"] * 2 + core))
    return lax.ppermute(value, AXES, pairs)


def swap_cores(value):
    return lax.ppermute(value, AXES, [(device, device ^ 1) for device in range(128)])


def exchange(pieces, axes):
    return [pieces[0]] + [send_along(pieces[step], axes, step) for step in STEPS]


def per_device(
    images,
    camera_counts,
    slot_of,
    patch_weight,
    pos_embed,
    attn_gain,
    qkv_weight,
    proj_weight,
    mlp_gain,
    up_weight,
    down_weight,
    final_gain,
    cotangent,
):
    params = (attn_gain, qkv_weight, proj_weight, mlp_gain, up_weight, down_weight)
    ring = exchange([cotangent] * 4, "zz")
    rows, stream, store_first, params, final_gain = run_embed(
        camera_counts,
        jnp.swapaxes(images, 1, 2),
        patch_weight,
        pos_embed,
        params,
        final_gain,
    )
    line = gather_ring("z", ring, final_gain)
    ring = exchange([line] * 4, "xx")
    middle_stream, store, store_second = run_middle(store_first["middle"], params, line)
    store_first.update(store)
    plane = gather_ring("x", ring, store["second"])
    ring = exchange([plane] * 4, "yy")
    pooled, tokens, store = run_pool(
        camera_counts, store_second["middle"], params, final_gain, plane
    )
    store_second.update(store)
    own, for_sibling = take_rows(slot_of, ring)
    keep_second, send, stream_grad = run_back_second(
        camera_counts,
        own,
        swap_cores(for_sibling),
        pooled,
        final_gain,
        middle_stream,
        params,
        store_second,
    )
    got_second = swap_cores(send)
    keep_mlp, send, middle_grad, mixed_grad = run_back_mlp(stream_grad, params, store_first)
    got_mlp = swap_cores(send)
    keep, send = run_back_attention(
        slot_of,
        tokens,
        middle_grad,
        mixed_grad,
        rows,
        stream,
        params,
        store_first,
    )
    got = swap_cores(send)
    pieces = add_pairs(keep_second, got_second, keep_mlp, got_mlp, keep, got)
    wide = exchange(pieces[4:], "xy")
    pieces = first_sum(exchange(pieces[:4], "zz") + wide)
    wide = exchange(pieces[4:], "zz")
    pieces = second_sum(exchange(pieces[:4], "xy") + wide)
    tokens, patch, *stacks = last_sum(exchange(pieces, "yx"))
    return (tokens, patch, *(jnp.swapaxes(stack, 0, 1) for stack in stacks))


def solution(mesh):
    placed = (
        P(("grp", "env"), None, None, None),
        P(("grp", "env")),
        P(),
        P(),
        P(),
        P(),
        P(),
        P(),
        P(),
        P(),
        P(),
        P(),
        P(("grp", "env"), None),
    )
    return jax.shard_map(
        per_device,
        mesh=mesh,
        in_specs=placed,
        out_specs=(
            P(("grp", "env"), None),
            P(("grp", "env"), None),
            P(None, ("grp", "env"), None),
            P(None, ("grp", "env"), None),
            P(None, ("grp", "env"), None),
            P(None, ("grp", "env"), None),
        ),
        check_vma=False,
    )
```

```python
from functools import partial

import jax
import jax.numpy as jnp
from jax import lax
from jax.experimental import pallas as pl
from jax.experimental.pallas import tpu as pltpu
from jax.sharding import PartitionSpec as P

F32 = jnp.float32
BF16 = jnp.bfloat16
D = 384
FF = 1536
WIDE = 768
HEADS = 6
PATCHES = 36
PATCH_DIM = 768
CAMS = 4
SLOTS = 8
CAM_MOST = 7
ROWS = 256
VMEM_BYTES = 20 * 1024 * 1024
SMALL_VMEM_BYTES = 14 * 1024 * 1024
EPS = 1e-06


def mm(left, right):
    return jnp.dot(left, right, preferred_element_type=F32)


def mm_nt(left, right):
    return lax.dot_general(left, right, (((1,), (1,)), ((), ())), preferred_element_type=F32)


def mm_tn(left, right):
    return lax.dot_general(left, right, (((0,), (0,)), ((), ())), preferred_element_type=F32)


def exact_mm(left, right):
    return jnp.dot(left, right, preferred_element_type=F32, precision=lax.Precision.HIGHEST)


def iota(shape, dim):
    return lax.broadcasted_iota(jnp.int32, shape, dim)


def steps_of(value, step, count):
    total = jnp.zeros_like(value)
    for at in range(1, count):
        total = total + jnp.where(value >= at * step, 1, 0)
    return total


def norm_rows(values, gain_row):
    centered = values - jnp.mean(values, axis=-1, keepdims=True)
    spread = jnp.mean(centered * centered, axis=-1, keepdims=True)
    return centered * lax.rsqrt(spread + EPS) * gain_row


def norm_pull(values, gain_row, upstream):
    centered = values - jnp.mean(values, axis=-1, keepdims=True)
    inv = lax.rsqrt(jnp.mean(centered * centered, axis=-1, keepdims=True) + EPS)
    hat = centered * inv
    scaled = upstream * gain_row
    return inv * (
        scaled
        - jnp.mean(scaled, axis=-1, keepdims=True)
        - hat * jnp.mean(scaled * hat, axis=-1, keepdims=True)
    )


def gelu_and_slope(before):
    size = jnp.abs(before)
    bell = jnp.exp(before * before * -0.5)
    t = 1.0 / (1.0 + (0.3275911 * 0.7071067811865476) * size)
    poly = t * (
        0.5 * 0.254829592
        + t
        * (
            0.5 * -0.284496736
            + t * (0.5 * 1.421413741 + t * (0.5 * -1.453152027 + t * (0.5 * 1.061405429)))
        )
    )
    tail = poly * bell
    below = jnp.where(before > 0, 1.0 - tail, tail)
    return before * below, below + before * bell * 0.3989422804014327


def camera_bias():
    cam_row = steps_of(iota((ROWS, 1), 0), PATCHES, CAM_MOST + 1)
    cam_col = steps_of(iota((1, ROWS), 1), PATCHES, CAM_MOST + 1)
    return jnp.where(cam_row == cam_col, 0.0, -1e30)


def head_mask(width_lanes, which):
    lane = iota((1, width_lanes), 1)
    return lane < 64 if which == 0 else lane >= 64


def attention_half(stream, gain_a, qkv, proj, store, need):
    normed_s, triple_s, probs_s, mixed_s, middle_s = store
    normed_s[...] = norm_rows(stream, gain_a).astype(BF16)
    need(0)
    triple_s[...] = mm(normed_s[...], qkv[...]).astype(BF16)
    bias = camera_bias()
    for pair in range(3):
        q = triple_s[:, pl.ds(pair * 128, 128)]
        k = triple_s[:, pl.ds(D + pair * 128, 128)]
        v = triple_s[:, pl.ds(2 * D + pair * 128, 128)]
        mixed = None
        for h in range(2):
            mask = head_mask(128, h)
            scores = mm_nt(jnp.where(mask, q * 0.125, 0.0).astype(BF16), k) + bias
            raised = jnp.exp(scores)
            probs = (raised * (1.0 / jnp.sum(raised, axis=-1, keepdims=True))).astype(BF16)
            probs_s[pair * 2 + h] = probs
            part = mm(probs, jnp.where(mask, v, 0.0).astype(BF16))
            mixed = part if mixed is None else mixed + part
        mixed_s[:, pl.ds(pair * 128, 128)] = mixed.astype(BF16)
    need(1)
    middle_s[...] = stream + mm(mixed_s[...], proj[...])


def mlp_half(middle, gain_m, up, down, store):
    second_s, hidden_s, slope_s = store
    second_s[...] = norm_rows(middle, gain_m).astype(BF16)
    total = middle
    for j in range(FF // WIDE):
        cols = pl.ds(j * WIDE, WIDE)
        hidden, slope = gelu_and_slope(mm(second_s[...], up[:, cols]))
        slope_s[:, cols] = slope.astype(BF16)
        hidden_s[:, cols] = hidden.astype(BF16)
        total = total + mm(hidden_s[:, cols], down[cols, :])
    return total


def pick(order, width=D):
    return jnp.where(order == iota((D, width), 1), 1.0, 0.0).astype(BF16)


def own_first(my_core):
    p = iota((D, 1), 0)
    swap = jnp.where(p >= D // 2, 1, 0)
    core = jnp.where(swap == my_core, 0, 1)
    return core, p - swap * (D // 2)


def order_three(my_core):
    core, rest = own_first(my_core)
    first = steps_of(rest, 48, 4)
    rest = rest - first * 48
    r = steps_of(rest, 16, 3)
    rest = rest - r * 16
    z, third = lax.shift_right_logical(rest, 2), lax.bitwise_and(rest, 3)
    x, y = jnp.where(core == 0, first, third), jnp.where(core == 0, third, first)
    return z * 96 + x * 24 + y * 6 + core * 3 + r


def chips_of(core, rest):
    second, third = lax.shift_right_logical(rest, 2), lax.bitwise_and(rest, 3)
    return jnp.where(core == 0, second * 4 + third, third * 4 + second)


def order_twelve(my_core):
    core, rest = own_first(my_core)
    r = lax.shift_right_logical(rest, 4)
    return chips_of(core, lax.bitwise_and(rest, 15)) * 24 + core * 12 + r


def order_six(core):
    p = iota((D, 1), 0)
    first = steps_of(p, 96, 4)
    rest = p - first * 96
    r = lax.shift_right_logical(rest, 4)
    rest = lax.bitwise_and(rest, 15)
    z, third = lax.shift_right_logical(rest, 2), lax.bitwise_and(rest, 3)
    x, y = jnp.where(core == 0, first, third), jnp.where(core == 0, third, first)
    return z * 192 + x * 48 + y * 12 + core * 6 + r


def turned(picks, columns):
    return mm_nt(picks, columns).astype(BF16)


def emit(tile, places):
    for at, (ref, first, q) in enumerate(places):
        ref[first, q] = tile[at * 16 : at * 16 + 16].astype(BF16)


def spots_three(refs, q_of):
    return [(ref, a, q_of(r)) for ref in refs for a in range(4) for r in range(3)]


def backward_mlp(my_core, upstream, gain_m, proj, up, down, store, keep, send):
    mixed_s, middle_s, second_s, hidden_s, slope_s = store
    both = (keep, send)
    down_in = upstream.astype(BF16)
    picks = pick(order_three(my_core))
    rows_up = turned(picks, second_s[...])
    picks_down = pick(order_twelve(my_core))
    second_grad = None
    stacked = jnp.concatenate([hidden_s[:, pl.ds(j * D, D)] for j in range(FF // D)], axis=0)
    rows = turned(picks_down, stacked)
    for j in range(FF // D):
        tile = mm(rows[:, j * ROWS : j * ROWS + ROWS], down_in)
        emit(tile, [(ref, j, r) for ref in both for r in range(12)])
    for j in range(FF // WIDE):
        cols = pl.ds(j * WIDE, WIDE)
        up_in = (slope_s[:, cols].astype(F32) * mm_nt(down_in, down[cols, :])).astype(BF16)
        tile = mm(rows_up, up_in)
        for i in range(WIDE // D):
            at = 12 + (j * (WIDE // D) + i) * 3
            emit(tile[:, i * D : i * D + D], spots_three(both, lambda r, at=at: at + r))
        part = mm_nt(up_in, up[:, cols])
        second_grad = part if second_grad is None else second_grad + part
    middle_grad = upstream + norm_pull(middle_s[...], gain_m, second_grad)
    proj_in = middle_grad.astype(BF16)
    emit(mm(turned(picks, mixed_s[...]), proj_in), spots_three(both, lambda r: 24 + r))
    return middle_grad, mm_nt(proj_in, proj[...]).astype(BF16)


def backward_attention(
    my_core, middle_grad, mixed_grad, stream_s, gain_a, qkv, store, wides, first_q, wide_s
):
    normed_s, triple_s, probs_s, mixed_s = store
    for pair in range(3):
        lanes = pl.ds(pair * 128, 128)
        q = triple_s[:, lanes] * 0.125
        k = triple_s[:, pl.ds(D + pair * 128, 128)]
        v = triple_s[:, pl.ds(2 * D + pair * 128, 128)]
        mg = mixed_grad[:, pair * 128 : pair * 128 + 128]
        product = mg.astype(F32) * mixed_s[:, lanes].astype(F32)
        dq = dk = dv = None
        for h in range(2):
            mask = head_mask(128, h)
            probs = probs_s[pair * 2 + h]
            mg_h = jnp.where(mask, mg, 0.0).astype(BF16)
            delta = jnp.sum(jnp.where(mask, product, 0.0), axis=-1, keepdims=True)
            probs_grad = mm_nt(mg_h, v)
            scores_grad = (probs.astype(F32) * (probs_grad - delta)).astype(BF16)
            part_q = mm(scores_grad, jnp.where(mask, k, 0.0).astype(BF16))
            part_k = mm_tn(scores_grad, jnp.where(mask, q, 0.0).astype(BF16))
            part_v = mm_tn(probs, mg_h)
            dq = part_q if dq is None else dq + part_q
            dk = part_k if dk is None else dk + part_k
            dv = part_v if dv is None else dv + part_v
        wide_s[:, lanes] = (dq * 0.125).astype(BF16)
        wide_s[:, pl.ds(D + pair * 128, 128)] = dk.astype(BF16)
        wide_s[:, pl.ds(2 * D + pair * 128, 128)] = dv.astype(BF16)
    rows_qkv = turned(pick(order_three(my_core)), normed_s[...])
    tile = mm(rows_qkv, wide_s[...])
    for j in range(3):
        emit(tile[:, j * D : j * D + D], spots_three(wides, lambda r, j=j: first_q + j * 3 + r))
    normed_grad = mm_nt(wide_s[...], qkv[...])
    return middle_grad + norm_pull(stream_s[...], gain_a, normed_grad)


def store_shapes():
    return [
        ((ROWS, D), BF16),
        ((ROWS, 3 * D), BF16),
        ((HEADS, ROWS, ROWS), BF16),
        ((ROWS, D), BF16),
        ((ROWS, D), F32),
        ((ROWS, D), BF16),
        ((ROWS, FF), BF16),
        ((ROWS, FF), BF16),
    ]


def whole(shape):
    return pl.BlockSpec(shape, lambda *_: (0,) * len(shape))


def shapes_of(items):
    return [jax.ShapeDtypeStruct(s, d) for s, d in items]


WEIGHTS = {
    "qkv": ((D, 3 * D), BF16),
    "proj": ((D, D), BF16),
    "up": ((D, FF), BF16),
    "down": ((FF, D), BF16),
}
STORES = dict(
    zip(
        ("normed", "triple", "probs", "mixed", "middle", "second", "hidden", "slope"),
        store_shapes(),
        strict=True,
    )
)
ANY_SPEC = pl.BlockSpec(memory_space=pl.ANY)
SCALARS = pl.BlockSpec(memory_space=pltpu.SMEM)
IN_VMEM = pl.BlockSpec(memory_space=pltpu.VMEM)
IN_HBM = pl.BlockSpec(memory_space=pltpu.HBM)


def gather_kernel(axis, *rest):
    pieces, out = rest[:4], rest[5]
    at = dict(zip("zxy", place_of_device()))[axis]
    for step, piece in zip((0, *STEPS), pieces, strict=True):
        out[lax.bitwise_and(at - step, 3)] = piece[...]


def gather_ring(axis, pieces, after):
    return local_kernel(
        partial(gather_kernel, axis),
        (*pieces, after),
        [((4, *pieces[0].shape), BF16)],
        [],
        "gather_ring",
    )[0]


def join_kernel(own, other, out):
    my_core = place_of_device()[3]
    out[my_core] = own[...]
    out[1 - my_core] = other[...]


def join_cores(own, other):
    return local_kernel(join_kernel, (own, other), [((2, 2, D), BF16)], [], "join_cores")[0]


def take_kernel(slot_of, _, *rest):
    pieces, (out, held_s) = rest[:4], rest[4:]
    z, x, y, my_core = place_of_device()
    for step, piece in zip((0, *STEPS), pieces, strict=True):
        held_s[lax.bitwise_and(y - step, 3)] = piece[...].astype(F32)
    device = z * 32 + x * 8 + y * 2 + my_core
    row = iota((2, 1), 0)
    taken = []
    for env in range(2):
        slot = slot_of[device * 2 + env]
        pair = held_s[
            lax.bitwise_and(lax.shift_right_logical(slot, 2), 3),
            lax.bitwise_and(lax.shift_right_logical(slot, 4), 3),
            lax.shift_right_logical(slot, 6),
            lax.bitwise_and(lax.shift_right_logical(slot, 1), 1),
        ]
        chosen = row == lax.bitwise_and(slot, 1)
        taken.append(jnp.sum(jnp.where(chosen, pair, 0.0), axis=0, keepdims=True))
    out[...] = jnp.where(row == 0, taken[0], taken[1])


def take_rows(slot_of, pieces, after):
    return pl.pallas_call(
        take_kernel,
        in_specs=[SCALARS, ANY_SPEC] + [IN_VMEM] * 4,
        out_specs=[IN_VMEM],
        out_shape=shapes_of([((2, D), F32)]),
        scratch_shapes=[pltpu.VMEM((4, 4, 4, 2, 2, D), F32)],
        compiler_params=pltpu.CompilerParams(vmem_limit_bytes=SMALL_VMEM_BYTES),
        name="take_rows",
    )(slot_of, after, *pieces)[0]


def big_kernel(kernel, operands, outs, scratch, flops, copies, name):
    return pl.pallas_call(
        kernel,
        in_specs=[spec for _, spec in operands],
        out_specs=[IN_VMEM for _ in outs],
        out_shape=shapes_of(outs),
        scratch_shapes=[(pltpu.VMEM if d != jnp.int32 else pltpu.SMEM)(s, d) for s, d in scratch]
        + [pltpu.SemaphoreType.DMA((copies,))] * (copies > 0),
        compiler_params=pltpu.CompilerParams(vmem_limit_bytes=VMEM_BYTES),
        cost_estimate=pl.CostEstimate(flops=flops, bytes_accessed=8000000, transcendentals=0),
        name=name,
    )(*[v for v, _ in operands])


def in_hbm(value):
    return pltpu.with_memory_space_constraint(value, pltpu.HBM)


def embed_kernel(
    counts, images, patch_weight, pos, gain_a, qkv, proj, gain_m, up, down, final_gain, *rest
):
    rows_o, stream_o, store, held, gains = rest[0], rest[1], rest[2:7], rest[7:11], rest[11:14]
    counts_o, flat_s, images_s, patch_s, pos_s, sems = rest[14:]
    first_copies = [
        pltpu.make_async_copy(source, target, sems.at[8 + at])
        for at, (source, target) in enumerate(
            (
                (images, images_s),
                (counts, counts_o),
                (patch_weight, patch_s),
                (pos, pos_s),
                (gain_a, gains[0]),
                (gain_m, gains[1]),
                (final_gain, gains[2]),
            )
        )
    ]
    copies = {}
    for layer in range(2):
        for at, (source, target) in enumerate(zip((qkv, proj, up, down), held, strict=True)):
            copies[layer, at] = pltpu.make_async_copy(
                source.at[layer], target.at[layer], sems.at[layer * 4 + at]
            )
    for copy in first_copies + list(copies.values()):
        copy.start()
    first_copies[0].wait()
    for env in range(2):
        for patch in range(PATCHES):
            at = (env * PATCHES + patch) * CAMS
            flat_s[pl.ds(at, CAMS)] = images_s[env, patch].astype(F32)
    first_copies[1].wait()
    first, second = counts_o[0], counts_o[1]
    row = iota((ROWS, 1), 0)
    cam = steps_of(row, PATCHES, CAM_MOST + 1)
    patch = row - cam * PATCHES
    slot = jnp.where(cam < first, cam, CAMS * PATCHES + cam - first)
    used = cam < first + second
    source = jnp.where(used, slot + patch * CAMS, -1)
    rows = mm(
        jnp.where(source == iota((ROWS, SLOTS * PATCHES), 1), 1.0, 0.0).astype(BF16),
        flat_s[...].astype(BF16),
    ).astype(BF16)
    rows_o[...] = rows
    place = jnp.where(used & (patch == iota((ROWS, PATCHES), 1)), 1.0, 0.0).astype(BF16)
    for copy in first_copies[2:]:
        copy.wait()
    stream = mm(rows, patch_s[...]) + mm(place, pos_s[...])
    stream_o[...] = stream
    attention_half(
        stream,
        gains[0][0:1],
        held[0].at[0],
        held[1].at[0],
        store,
        lambda at: copies[0, at].wait(),
    )
    for key in ((0, 2), (0, 3), (1, 0), (1, 1), (1, 2), (1, 3)):
        copies[key].wait()


STORE_A = ("normed", "triple", "probs", "mixed", "middle")
STORE_M = ("second", "hidden", "slope")


def run_embed(counts, images, patch_weight, pos, params, final_gain):
    gain_a, qkv, proj, gain_m, up, down = params
    sources = (counts, images, patch_weight, pos, gain_a, qkv, proj, gain_m, up, down, final_gain)
    got = big_kernel(
        embed_kernel,
        [(in_hbm(v), IN_HBM) for v in sources],
        [((ROWS, PATCH_DIM), BF16), ((ROWS, D), F32)]
        + [STORES[k] for k in STORE_A]
        + [((2, *s), d) for s, d in WEIGHTS.values()]
        + [((2, D), F32), ((2, D), F32), ((D,), F32)],
        [
            ((2,), jnp.int32),
            ((SLOTS * PATCHES, PATCH_DIM), F32),
            (images.shape, BF16),
            ((PATCH_DIM, D), BF16),
            ((PATCHES, D), BF16),
        ],
        7000000000,
        15,
        "embed_attend",
    )
    gain_a, gain_m, final_gain = got[11:14]
    params = (gain_a, *got[7:9], gain_m, *got[9:11])
    return got[0], got[1], dict(zip(STORE_A, got[2:7])), params, final_gain


def middle_kernel(middle, gain_a, gain_m, up, down, qkv, proj, _, *rest):
    stream_o, store_m, store_a = rest[0], rest[1:4], rest[4:9]
    stream_o[...] = mlp_half(middle[...], gain_m[0:1], up.at[0], down.at[0], store_m)
    attention_half(
        stream_o[...], gain_a[1:2], qkv.at[1], proj.at[1], store_a, lambda at: None
    )


def run_middle(middle, params, after):
    gain_a, qkv, proj, gain_m, up, down = params
    got = big_kernel(
        middle_kernel,
        [(v, IN_VMEM) for v in (middle, gain_a, gain_m, up, down, qkv, proj)] + [(after, ANY_SPEC)],
        [((ROWS, D), F32)] + [STORES[k] for k in STORE_M + STORE_A],
        [],
        6000000000,
        0,
        "mlp_attend",
    )
    return got[0], dict(zip(STORE_M, got[1:4])), dict(zip(STORE_A, got[4:9]))


def pool_kernel(counts, middle, gain_m, up, down, final_gain, _, *rest):
    pooled_o, tokens_o, store_m = rest[0], rest[1], rest[2:5]
    last = mlp_half(middle[...], gain_m[1:2], up.at[1], down.at[1], store_m)
    pooled = exact_mm(camera_members(), last) * (1.0 / PATCHES)
    pooled_o[...] = pooled
    embedded = norm_rows(pooled, final_gain[...][None])
    first, second = counts[0], counts[1]
    cam = iota((SLOTS, 1), 0)
    in_first = cam < first
    in_second = (cam >= first) & (cam < first + second)
    sum_first = jnp.sum(jnp.where(in_first, embedded, 0.0), axis=0, keepdims=True)
    sum_second = jnp.sum(jnp.where(in_second, embedded, 0.0), axis=0, keepdims=True)
    row = iota((SLOTS, 1), 0)
    count_col = jnp.where(row == 0, first, second).astype(F32)
    both = jnp.where(row == 0, sum_first, jnp.where(row == 1, sum_second, 0.0))
    tokens_o[...] = (both / count_col).astype(BF16)


def run_pool(counts, middle, params, final_gain, after):
    _, _, _, gain_m, up, down = params
    got = big_kernel(
        pool_kernel,
        [(counts, SCALARS)]
        + [(v, IN_VMEM) for v in (middle, gain_m, up, down, final_gain)]
        + [(after, ANY_SPEC)],
        [((SLOTS, D), F32), ((SLOTS, D), BF16)] + [STORES[k] for k in STORE_M],
        [],
        4000000000,
        0,
        "mlp_pool",
    )
    return got[0], got[1], dict(zip(STORE_M, got[2:5]))


def camera_members():
    cam = steps_of(iota((1, ROWS), 1), PATCHES, CAM_MOST + 1)
    return jnp.where(cam == iota((SLOTS, 1), 0), 1.0, 0.0)


GRAD_COUNTS = {"second": (12, 24), "first_mlp": (12, 15), "first_attention": (0, 17)}


ROWS_D, ROWS_W = (sum(n) for n in zip(*GRAD_COUNTS.values()))


def grad_shapes(group):
    return [((4, sum(GRAD_COUNTS[group]), 16, D), BF16)] * 2


def place_of_device():
    env = lax.axis_index("env")
    return (
        lax.axis_index("grp"),
        lax.shift_right_logical(env, 3),
        lax.bitwise_and(lax.shift_right_logical(env, 1), 3),
        lax.bitwise_and(env, 1),
    )


SECOND_IN = ("second", "hidden", "down", "slope", "up", "middle", "mixed", "proj")
ATTENTION_IN = ("triple", "probs", "normed", "qkv")


def of_layer(names, refs, layer):
    refs = dict(zip(names, refs))
    return {key: ref.at[layer] if key in WEIGHTS else ref for key, ref in refs.items()}


def back_second_kernel(counts, seeds, pooled, final_gain, gain_a, gain_m, *rest):
    names = SECOND_IN + ATTENTION_IN + ("stream",)
    held, rest = of_layer(names, rest, 1), rest[len(names) :]
    keep, send, grad_o, wide_s = rest
    my_core = place_of_device()[3]
    first, second = counts[0], counts[1]
    cam = iota((SLOTS, 1), 0)
    seed = jnp.where(
        cam < first,
        seeds[0:1] / first.astype(F32),
        jnp.where(cam < first + second, seeds[1:2] / second.astype(F32), 0.0),
    )
    pooled_grad = norm_pull(pooled[...], final_gain[...][None], seed) * (1.0 / PATCHES)
    cam_row = steps_of(iota((ROWS, 1), 0), PATCHES, CAM_MOST + 1)
    member = jnp.where(cam_row == iota((1, SLOTS), 1), 1.0, 0.0)
    upstream = exact_mm(member, pooled_grad)
    middle_grad, mixed_grad = backward_mlp(
        my_core,
        upstream,
        gain_m[1:2],
        held["proj"],
        held["up"],
        held["down"],
        [held[k] for k in ("mixed", "middle", "second", "hidden", "slope")],
        keep,
        send,
    )
    grad_o[...] = backward_attention(
        my_core,
        middle_grad,
        mixed_grad,
        held["stream"],
        gain_a[1:2],
        held["qkv"],
        [held[k] for k in ("normed", "triple", "probs", "mixed")],
        (keep, send),
        27,
        wide_s,
    )


def run_back_second(counts, seeds, pooled, final_gain, stream, params, store):
    gain_a, qkv, proj, gain_m, up, down = params
    values = {"qkv": qkv, "proj": proj, "up": up, "down": down, "stream": stream}
    values.update(store)
    names = SECOND_IN + ATTENTION_IN + ("stream",)
    return big_kernel(
        back_second_kernel,
        [(counts, SCALARS)]
        + [(v, IN_VMEM) for v in (seeds, pooled, final_gain, gain_a, gain_m)]
        + [(values[k], IN_VMEM) for k in names],
        grad_shapes("second") + [((ROWS, D), F32)],
        [((ROWS, 3 * D), BF16)],
        8000000000,
        0,
        "back_second",
    )


def back_mlp_kernel(gain_m, *rest):
    names = ("stream",) + SECOND_IN
    held, rest = of_layer(names, rest, 0), rest[len(names) :]
    keep, send, middle_o, mixed_o = rest
    middle_o[...], mixed_o[...] = backward_mlp(
        place_of_device()[3],
        held["stream"][...],
        gain_m[0:1],
        held["proj"],
        held["up"],
        held["down"],
        [held[k] for k in ("mixed", "middle", "second", "hidden", "slope")],
        keep,
        send,
    )


def run_back_mlp(upstream, params, store):
    _, _, proj, gain_m, up, down = params
    values = {"proj": proj, "up": up, "down": down, "stream": upstream}
    values.update(store)
    names = ("stream",) + SECOND_IN
    return big_kernel(
        back_mlp_kernel,
        [(gain_m, IN_VMEM)] + [(values[k], IN_VMEM) for k in names],
        grad_shapes("first_mlp") + [((ROWS, D), F32), ((ROWS, D), BF16)],
        [],
        5000000000,
        0,
        "back_first_mlp",
    )


def back_attention_kernel(slot_of, tokens, middle_grad, mixed_grad, gain_a, *rest):
    names = ("mixed",) + ATTENTION_IN + ("stream", "rows")
    held, rest = of_layer(names, rest, 0), rest[len(names) :]
    keep, send, wide_s = rest
    z, x, y, my_core = place_of_device()
    device = z * 32 + x * 8 + y * 2 + my_core
    p = iota((ROWS, 1), 0)
    swap = jnp.where(p >= 128, 1, 0)
    core = jnp.where(swap == my_core, 0, 1)
    rest_p = p - swap * 128
    first = lax.shift_right_logical(rest_p, 5)
    row = lax.bitwise_and(lax.shift_right_logical(rest_p, 4), 1)
    third = lax.bitwise_and(rest_p, 3)
    to_x, to_y = jnp.where(core == 0, first, third), jnp.where(core == 0, third, first)
    to_z = lax.bitwise_and(lax.shift_right_logical(rest_p, 2), 3)
    learner = to_z * 64 + to_x * 16 + to_y * 4 + core * 2 + row
    lane = iota((1, SLOTS), 1)
    wanted = jnp.where(
        lane == 0, slot_of[device * 2], jnp.where(lane == 1, slot_of[device * 2 + 1], -1)
    )
    spread = mm(jnp.where(learner == wanted, 1.0, 0.0).astype(BF16), tokens[...]).astype(BF16)
    spots = [(ref, a, r) for ref in (keep, send) for a in range(4) for r in range(2)]
    for at, (ref, a, r) in enumerate(spots):
        ref[a, 15 + r] = spread[at * 16 : at * 16 + 16]
    stream_grad = backward_attention(
        my_core,
        middle_grad[...],
        mixed_grad[...],
        held["stream"],
        gain_a[0:1],
        held["qkv"],
        [held[k] for k in ("normed", "triple", "probs", "mixed")],
        (keep, send),
        0,
        wide_s,
    ).astype(BF16)
    for ref, core in ((keep, my_core), (send, 1 - my_core)):
        tile = mm(turned(pick(order_six(core), PATCH_DIM), held["rows"][...]), stream_grad)
        emit(tile, [(ref, a, 9 + r) for a in range(4) for r in range(6)])


def run_back_attention(slot_of, tokens, middle_grad, mixed_grad, rows, stream, params, store):
    values = {"qkv": params[1], "stream": stream, "rows": rows}
    values.update(store)
    names = ("mixed",) + ATTENTION_IN + ("stream", "rows")
    return big_kernel(
        back_attention_kernel,
        [(slot_of, SCALARS)]
        + [(v, IN_VMEM) for v in (tokens, middle_grad, mixed_grad, params[0])]
        + [(values[k], IN_VMEM) for k in names],
        grad_shapes("first_attention"),
        [((ROWS, 3 * D), BF16)],
        4000000000,
        0,
        "back_first_attention",
    )


def local_kernel(kernel, operands, outs, scratch, name):
    return pl.pallas_call(
        kernel,
        in_specs=[IN_VMEM for _ in operands],
        out_specs=[IN_VMEM for _ in outs],
        out_shape=shapes_of(outs),
        scratch_shapes=scratch,
        compiler_params=pltpu.CompilerParams(vmem_limit_bytes=SMALL_VMEM_BYTES),
        name=name,
    )(*operands)


def add_kernel(*rest):
    parts, outs = rest[:-8], rest[-8:]
    z, x, y, my_core = place_of_device()
    along = jnp.where(my_core == 0, x, y)
    at_d = at_w = 0
    for group, (count_d, count_w) in enumerate(GRAD_COUNTS.values()):
        keep, got = parts[group * 2 : group * 2 + 2]
        for step in range(4):
            place_d, place_w = lax.bitwise_and(z + step, 3), lax.bitwise_and(along + step, 3)
            if count_d:
                span = pl.ds(0, count_d)
                outs[step][pl.ds(at_d, count_d)] = keep[place_d, span] + got[place_d, span]
            span = pl.ds(count_d, count_w)
            outs[4 + step][pl.ds(at_w, count_w)] = keep[place_w, span] + got[place_w, span]
        at_d, at_w = at_d + count_d, at_w + count_w


def add_pairs(*parts):
    return local_kernel(
        add_kernel,
        parts,
        [((ROWS_D, 16, D), BF16)] * 4 + [((ROWS_W, 16, D), BF16)] * 4,
        [],
        "add_pairs",
    )


def sum_of(refs):
    total = refs[0][...].astype(F32)
    for ref in refs[1:]:
        total = total + ref[...].astype(F32)
    return total


def first_sum_kernel(*rest):
    parts, outs, (total_s, turn_d, turn_w) = rest[:8], rest[8:16], rest[16:]
    for group, at, count in ((0, 0, ROWS_D), (1, ROWS_D, ROWS_W)):
        total = sum_of(parts[group * 4 : group * 4 + 4]).reshape(count * 16, D)
        for lanes in range(3):
            total_s[lanes, pl.ds(at * 16, count * 16)] = total[:, lanes * 128 : lanes * 128 + 128]
    for b in range(16):
        for lanes in range(3):
            cols = pl.ds(lanes * 128, 128)
            turn_d[b // 4, pl.ds(b % 4 * ROWS_D, ROWS_D), cols] = total_s[
                lanes, pl.ds(b, ROWS_D, 16)
            ]
            turn_w[b // 4, pl.ds(b % 4 * ROWS_W, ROWS_W), cols] = total_s[
                lanes, pl.ds(ROWS_D * 16 + b, ROWS_W, 16)
            ]
    z, x, y, my_core = place_of_device()
    along = jnp.where(my_core == 0, x, y)
    for step in range(4):
        outs[step][...] = turn_d[lax.bitwise_and(along + step, 3)].astype(BF16)
        outs[4 + step][...] = turn_w[lax.bitwise_and(z + step, 3)].astype(BF16)


def first_sum(parts):
    return local_kernel(
        first_sum_kernel,
        parts,
        [((4 * ROWS_D, D), BF16)] * 4 + [((4 * ROWS_W, D), BF16)] * 4,
        [
            pltpu.VMEM((3, 1280, 128), F32),
            pltpu.VMEM((4, 4 * ROWS_D, D), F32),
            pltpu.VMEM((4, 4 * ROWS_W, D), F32),
        ],
        "first_sum",
    )


def second_sum_kernel(*rest):
    parts, outs, total_s = rest[:8], rest[8:12], rest[12]
    total_d, total_w = sum_of(parts[:4]), sum_of(parts[4:])
    for third in range(4):
        total_s[third, pl.ds(0, ROWS_D)] = total_d[third * ROWS_D : (third + 1) * ROWS_D]
        total_s[third, pl.ds(ROWS_D, ROWS_W)] = total_w[third * ROWS_W : (third + 1) * ROWS_W]
    _, x, y, my_core = place_of_device()
    along = jnp.where(my_core == 0, y, x)
    for step in range(4):
        outs[step][...] = total_s[lax.bitwise_and(along + step, 3)].astype(BF16)


def second_sum(parts):
    return local_kernel(
        second_sum_kernel,
        parts,
        [((ROWS_D + ROWS_W, D), BF16)] * 4,
        [pltpu.VMEM((4, ROWS_D + ROWS_W, D), F32)],
        "second_sum",
    )


def last_sum_kernel(*rest):
    parts, (tokens, patch, qkv, proj, up, down) = rest[:4], rest[4:]
    rows = sum_of(parts)
    down[:, 1], down[:, 0] = rows[0:12], rows[12:24]
    wide = rows[ROWS_D:]
    for layer, at_up, at_qkv in ((1, 0, 15), (0, 24, 39)):
        for j in range(4):
            up[:, layer, pl.ds(j * D, D)] = wide[at_up + j * 3 : at_up + j * 3 + 3]
        proj[:, layer] = wide[at_up + 12 : at_up + 15]
        for j in range(3):
            qkv[:, layer, pl.ds(j * D, D)] = wide[at_qkv + j * 3 : at_qkv + j * 3 + 3]
    patch[...] = wide[48:54]
    tokens[...] = wide[54:56].astype(BF16)


def last_sum(parts):
    return local_kernel(
        last_sum_kernel,
        parts,
        [
            ((2, D), BF16),
            ((6, D), F32),
            ((3, 2, 3 * D), F32),
            ((3, 2, D), F32),
            ((3, 2, FF), F32),
            ((12, 2, D), F32),
        ],
        [],
        "last_sum",
    )


AXES = ("grp", "env")
STEPS = (2, 1, 3)


def send_along(value, axes, step):
    pairs = []
    for device in range(128):
        z, x, y, core = device // 32, device // 8 % 4, device // 2 % 4, device % 2
        place = {"z": z, "x": x, "y": y}
        place[axes[core]] = (place[axes[core]] + step) % 4
        pairs.append((device, place["z"] * 32 + place["x"] * 8 + place["y"] * 2 + core))
    return lax.ppermute(value, AXES, pairs)


def swap_cores(value):
    return lax.ppermute(value, AXES, [(device, device ^ 1) for device in range(128)])


def exchange(pieces, axes):
    return [pieces[0]] + [send_along(pieces[step], axes, step) for step in STEPS]


def per_device(
    images,
    camera_counts,
    slot_of,
    patch_weight,
    pos_embed,
    attn_gain,
    qkv_weight,
    proj_weight,
    mlp_gain,
    up_weight,
    down_weight,
    final_gain,
    cotangent,
):
    params = (attn_gain, qkv_weight, proj_weight, mlp_gain, up_weight, down_weight)
    chip = join_cores(cotangent, swap_cores(cotangent))
    ring = exchange([chip] * 4, "zz")
    rows, stream, store_first, params, final_gain = run_embed(
        camera_counts,
        jnp.swapaxes(images, 1, 2),
        patch_weight,
        pos_embed,
        params,
        final_gain,
    )
    line = gather_ring("z", ring, final_gain)
    ring = exchange([line] * 4, "xx")
    middle_stream, store, store_second = run_middle(store_first["middle"], params, line)
    store_first.update(store)
    plane = gather_ring("x", ring, store["second"])
    ring = exchange([plane] * 4, "yy")
    pooled, tokens, store = run_pool(
        camera_counts, store_second["middle"], params, final_gain, plane
    )
    store_second.update(store)
    seeds = take_rows(slot_of, ring, pooled)
    keep_second, send, stream_grad = run_back_second(
        camera_counts,
        seeds,
        pooled,
        final_gain,
        middle_stream,
        params,
        store_second,
    )
    got_second = swap_cores(send)
    keep_mlp, send, middle_grad, mixed_grad = run_back_mlp(stream_grad, params, store_first)
    got_mlp = swap_cores(send)
    keep, send = run_back_attention(
        slot_of,
        tokens,
        middle_grad,
        mixed_grad,
        rows,
        stream,
        params,
        store_first,
    )
    got = swap_cores(send)
    pieces = add_pairs(keep_second, got_second, keep_mlp, got_mlp, keep, got)
    wide = exchange(pieces[4:], "xy")
    pieces = first_sum(exchange(pieces[:4], "zz") + wide)
    wide = exchange(pieces[4:], "zz")
    pieces = second_sum(exchange(pieces[:4], "xy") + wide)
    tokens, patch, *stacks = last_sum(exchange(pieces, "yx"))
    return (tokens, patch, *(jnp.swapaxes(stack, 0, 1) for stack in stacks))


def solution(mesh):
    placed = (
        P(("grp", "env"), None, None, None),
        P(("grp", "env")),
        P(),
        P(),
        P(),
        P(),
        P(),
        P(),
        P(),
        P(),
        P(),
        P(),
        P(("grp", "env"), None),
    )
    return jax.shard_map(
        per_device,
        mesh=mesh,
        in_specs=placed,
        out_specs=(
            P(("grp", "env"), None),
            P(("grp", "env"), None),
            P(None, ("grp", "env"), None),
            P(None, ("grp", "env"), None),
            P(None, ("grp", "env"), None),
            P(None, ("grp", "env"), None),
        ),
        check_vma=False,
    )
```

```python
from functools import partial

import jax
import jax.numpy as jnp
from jax import lax
from jax.experimental import pallas as pl
from jax.experimental.pallas import tpu as pltpu
from jax.sharding import PartitionSpec as P

F32 = jnp.float32
BF16 = jnp.bfloat16
D = 384
FF = 1536
WIDE = 768
HEADS = 6
PATCHES = 36
PATCH_DIM = 768
CAMS = 4
SLOTS = 8
CAM_MOST = 7
ROWS = 256
VMEM_BYTES = 20 * 1024 * 1024
SMALL_VMEM_BYTES = 14 * 1024 * 1024
EPS = 1e-06


def mm(left, right):
    return jnp.dot(left, right, preferred_element_type=F32)


def mm_nt(left, right):
    return lax.dot_general(left, right, (((1,), (1,)), ((), ())), preferred_element_type=F32)


def mm_tn(left, right):
    return lax.dot_general(left, right, (((0,), (0,)), ((), ())), preferred_element_type=F32)


def exact_mm(left, right):
    return jnp.dot(left, right, preferred_element_type=F32, precision=lax.Precision.HIGHEST)


def iota(shape, dim):
    return lax.broadcasted_iota(jnp.int32, shape, dim)


def steps_of(value, step, count):
    total = jnp.zeros_like(value)
    for at in range(1, count):
        total = total + jnp.where(value >= at * step, 1, 0)
    return total


def norm_rows(values, gain_row):
    centered = values - jnp.mean(values, axis=-1, keepdims=True)
    spread = jnp.mean(centered * centered, axis=-1, keepdims=True)
    return centered * lax.rsqrt(spread + EPS) * gain_row


def norm_pull(values, gain_row, upstream):
    centered = values - jnp.mean(values, axis=-1, keepdims=True)
    inv = lax.rsqrt(jnp.mean(centered * centered, axis=-1, keepdims=True) + EPS)
    hat = centered * inv
    scaled = upstream * gain_row
    return inv * (
        scaled
        - jnp.mean(scaled, axis=-1, keepdims=True)
        - hat * jnp.mean(scaled * hat, axis=-1, keepdims=True)
    )


def gelu_and_slope(before):
    size = jnp.abs(before)
    bell = jnp.exp(before * before * -0.5)
    t = 1.0 / (1.0 + (0.3275911 * 0.7071067811865476) * size)
    poly = t * (
        0.5 * 0.254829592
        + t
        * (
            0.5 * -0.284496736
            + t * (0.5 * 1.421413741 + t * (0.5 * -1.453152027 + t * (0.5 * 1.061405429)))
        )
    )
    tail = poly * bell
    below = jnp.where(before > 0, 1.0 - tail, tail)
    return before * below, below + before * bell * 0.3989422804014327


def camera_bias():
    cam_row = steps_of(iota((ROWS, 1), 0), PATCHES, CAM_MOST + 1)
    cam_col = steps_of(iota((1, ROWS), 1), PATCHES, CAM_MOST + 1)
    return jnp.where(cam_row == cam_col, 0.0, -1e30)


def head_mask(width_lanes, which):
    lane = iota((1, width_lanes), 1)
    return lane < 64 if which == 0 else lane >= 64


def attention_half(stream, gain_a, qkv, proj, store, need):
    normed_s, triple_s, probs_s, mixed_s, middle_s = store
    normed_s[...] = norm_rows(stream, gain_a).astype(BF16)
    need(0)
    triple_s[...] = mm(normed_s[...], qkv[...]).astype(BF16)
    bias = camera_bias()
    for pair in range(3):
        q = triple_s[:, pl.ds(pair * 128, 128)]
        k = triple_s[:, pl.ds(D + pair * 128, 128)]
        v = triple_s[:, pl.ds(2 * D + pair * 128, 128)]
        mixed = None
        for h in range(2):
            mask = head_mask(128, h)
            scores = mm_nt(jnp.where(mask, q * 0.125, 0.0).astype(BF16), k) + bias
            raised = jnp.exp(scores)
            probs = (raised * (1.0 / jnp.sum(raised, axis=-1, keepdims=True))).astype(BF16)
            probs_s[pair * 2 + h] = probs
            part = mm(probs, jnp.where(mask, v, 0.0).astype(BF16))
            mixed = part if mixed is None else mixed + part
        mixed_s[:, pl.ds(pair * 128, 128)] = mixed.astype(BF16)
    need(1)
    middle_s[...] = stream + mm(mixed_s[...], proj[...])


def mlp_half(middle, gain_m, up, down, store):
    second_s, hidden_s, slope_s = store
    second_s[...] = norm_rows(middle, gain_m).astype(BF16)
    total = middle
    for j in range(FF // WIDE):
        cols = pl.ds(j * WIDE, WIDE)
        hidden, slope = gelu_and_slope(mm(second_s[...], up[:, cols]))
        slope_s[:, cols] = slope.astype(BF16)
        hidden_s[:, cols] = hidden.astype(BF16)
        total = total + mm(hidden_s[:, cols], down[cols, :])
    return total


def pick(order, width=D):
    return jnp.where(order == iota((D, width), 1), 1.0, 0.0).astype(BF16)


def own_first(my_core):
    p = iota((D, 1), 0)
    swap = jnp.where(p >= D // 2, 1, 0)
    core = jnp.where(swap == my_core, 0, 1)
    return core, p - swap * (D // 2)


def order_three(my_core):
    core, rest = own_first(my_core)
    first = steps_of(rest, 48, 4)
    rest = rest - first * 48
    r = steps_of(rest, 16, 3)
    rest = rest - r * 16
    z, third = lax.shift_right_logical(rest, 2), lax.bitwise_and(rest, 3)
    x, y = jnp.where(core == 0, first, third), jnp.where(core == 0, third, first)
    return z * 96 + x * 24 + y * 6 + core * 3 + r


def chips_of(core, rest):
    second, third = lax.shift_right_logical(rest, 2), lax.bitwise_and(rest, 3)
    return jnp.where(core == 0, second * 4 + third, third * 4 + second)


def order_twelve(my_core):
    core, rest = own_first(my_core)
    r = lax.shift_right_logical(rest, 4)
    return chips_of(core, lax.bitwise_and(rest, 15)) * 24 + core * 12 + r


def order_six(core):
    p = iota((D, 1), 0)
    first = steps_of(p, 96, 4)
    rest = p - first * 96
    r = lax.shift_right_logical(rest, 4)
    rest = lax.bitwise_and(rest, 15)
    z, third = lax.shift_right_logical(rest, 2), lax.bitwise_and(rest, 3)
    x, y = jnp.where(core == 0, first, third), jnp.where(core == 0, third, first)
    return z * 192 + x * 48 + y * 12 + core * 6 + r


def turned(picks, columns):
    return mm_nt(picks, columns).astype(BF16)


def emit(tile, places):
    for at, (ref, first, q) in enumerate(places):
        ref[first, q] = tile[at * 16 : at * 16 + 16].astype(BF16)


def spots_three(refs, q_of):
    return [(ref, a, q_of(r)) for ref in refs for a in range(4) for r in range(3)]


def backward_mlp(my_core, upstream, gain_m, proj, up, down, store, keep, send):
    mixed_s, middle_s, second_s, hidden_s, slope_s = store
    both = (keep, send)
    down_in = upstream.astype(BF16)
    picks = pick(order_three(my_core))
    rows_up = turned(picks, second_s[...])
    picks_down = pick(order_twelve(my_core))
    second_grad = None
    stacked = jnp.concatenate([hidden_s[:, pl.ds(j * D, D)] for j in range(FF // D)], axis=0)
    rows = turned(picks_down, stacked)
    for j in range(FF // D):
        tile = mm(rows[:, j * ROWS : j * ROWS + ROWS], down_in)
        emit(tile, [(ref, j, r) for ref in both for r in range(12)])
    for j in range(FF // WIDE):
        cols = pl.ds(j * WIDE, WIDE)
        up_in = (slope_s[:, cols].astype(F32) * mm_nt(down_in, down[cols, :])).astype(BF16)
        tile = mm(rows_up, up_in)
        for i in range(WIDE // D):
            at = 12 + (j * (WIDE // D) + i) * 3
            emit(tile[:, i * D : i * D + D], spots_three(both, lambda r, at=at: at + r))
        part = mm_nt(up_in, up[:, cols])
        second_grad = part if second_grad is None else second_grad + part
    middle_grad = upstream + norm_pull(middle_s[...], gain_m, second_grad)
    proj_in = middle_grad.astype(BF16)
    emit(mm(turned(picks, mixed_s[...]), proj_in), spots_three(both, lambda r: 24 + r))
    return middle_grad, mm_nt(proj_in, proj[...]).astype(BF16)


def backward_attention(
    my_core, middle_grad, mixed_grad, stream_s, gain_a, qkv, store, wides, first_q, wide_s
):
    normed_s, triple_s, probs_s, mixed_s = store
    for pair in range(3):
        lanes = pl.ds(pair * 128, 128)
        q = triple_s[:, lanes] * 0.125
        k = triple_s[:, pl.ds(D + pair * 128, 128)]
        v = triple_s[:, pl.ds(2 * D + pair * 128, 128)]
        mg = mixed_grad[:, pair * 128 : pair * 128 + 128]
        product = mg.astype(F32) * mixed_s[:, lanes].astype(F32)
        dq = dk = dv = None
        for h in range(2):
            mask = head_mask(128, h)
            probs = probs_s[pair * 2 + h]
            mg_h = jnp.where(mask, mg, 0.0).astype(BF16)
            delta = jnp.sum(jnp.where(mask, product, 0.0), axis=-1, keepdims=True)
            probs_grad = mm_nt(mg_h, v)
            scores_grad = (probs.astype(F32) * (probs_grad - delta)).astype(BF16)
            part_q = mm(scores_grad, jnp.where(mask, k, 0.0).astype(BF16))
            part_k = mm_tn(scores_grad, jnp.where(mask, q, 0.0).astype(BF16))
            part_v = mm_tn(probs, mg_h)
            dq = part_q if dq is None else dq + part_q
            dk = part_k if dk is None else dk + part_k
            dv = part_v if dv is None else dv + part_v
        wide_s[:, lanes] = (dq * 0.125).astype(BF16)
        wide_s[:, pl.ds(D + pair * 128, 128)] = dk.astype(BF16)
        wide_s[:, pl.ds(2 * D + pair * 128, 128)] = dv.astype(BF16)
    rows_qkv = turned(pick(order_three(my_core)), normed_s[...])
    tile = mm(rows_qkv, wide_s[...])
    for j in range(3):
        emit(tile[:, j * D : j * D + D], spots_three(wides, lambda r, j=j: first_q + j * 3 + r))
    normed_grad = mm_nt(wide_s[...], qkv[...])
    return middle_grad + norm_pull(stream_s[...], gain_a, normed_grad)


def store_shapes():
    return [
        ((ROWS, D), BF16),
        ((ROWS, 3 * D), BF16),
        ((HEADS, ROWS, ROWS), BF16),
        ((ROWS, D), BF16),
        ((ROWS, D), F32),
        ((ROWS, D), BF16),
        ((ROWS, FF), BF16),
        ((ROWS, FF), BF16),
    ]


def whole(shape):
    return pl.BlockSpec(shape, lambda *_: (0,) * len(shape))


def shapes_of(items):
    return [jax.ShapeDtypeStruct(s, d) for s, d in items]


WEIGHTS = {
    "qkv": ((D, 3 * D), BF16),
    "proj": ((D, D), BF16),
    "up": ((D, FF), BF16),
    "down": ((FF, D), BF16),
}
STORES = dict(
    zip(
        ("normed", "triple", "probs", "mixed", "middle", "second", "hidden", "slope"),
        store_shapes(),
        strict=True,
    )
)
ANY_SPEC = pl.BlockSpec(memory_space=pl.ANY)
SCALARS = pl.BlockSpec(memory_space=pltpu.SMEM)
IN_VMEM = pl.BlockSpec(memory_space=pltpu.VMEM)
IN_HBM = pl.BlockSpec(memory_space=pltpu.HBM)


def gather_kernel(axis, *rest):
    pieces, out = rest[:4], rest[5]
    at = dict(zip("zxy", place_of_device()))[axis]
    for step, piece in zip((0, *STEPS), pieces, strict=True):
        out[lax.bitwise_and(at - step, 3)] = piece[...]


def gather_ring(axis, pieces, after):
    return local_kernel(
        partial(gather_kernel, axis),
        (*pieces, after),
        [((4, *pieces[0].shape), BF16)],
        [],
        "gather_ring",
    )[0]


def join_kernel(own, other, out):
    my_core = place_of_device()[3]
    out[my_core] = own[...]
    out[1 - my_core] = other[...]


def join_cores(own, other):
    return local_kernel(join_kernel, (own, other), [((2, 2, D), BF16)], [], "join_cores")[0]


def take_kernel(slot_of, _, *rest):
    pieces, (out, held_s) = rest[:4], rest[4:]
    z, x, y, my_core = place_of_device()
    for step, piece in zip((0, *STEPS), pieces, strict=True):
        held_s[lax.bitwise_and(y - step, 3)] = piece[...].astype(F32)
    device = z * 32 + x * 8 + y * 2 + my_core
    row = iota((2, 1), 0)
    taken = []
    for env in range(2):
        slot = slot_of[device * 2 + env]
        pair = held_s[
            lax.bitwise_and(lax.shift_right_logical(slot, 2), 3),
            lax.bitwise_and(lax.shift_right_logical(slot, 4), 3),
            lax.shift_right_logical(slot, 6),
            lax.bitwise_and(lax.shift_right_logical(slot, 1), 1),
        ]
        chosen = row == lax.bitwise_and(slot, 1)
        taken.append(jnp.sum(jnp.where(chosen, pair, 0.0), axis=0, keepdims=True))
    out[...] = jnp.where(row == 0, taken[0], taken[1])


def take_rows(slot_of, pieces, after):
    return pl.pallas_call(
        take_kernel,
        in_specs=[SCALARS, ANY_SPEC] + [IN_VMEM] * 4,
        out_specs=[IN_VMEM],
        out_shape=shapes_of([((2, D), F32)]),
        scratch_shapes=[pltpu.VMEM((4, 4, 4, 2, 2, D), F32)],
        compiler_params=pltpu.CompilerParams(vmem_limit_bytes=SMALL_VMEM_BYTES),
        name="take_rows",
    )(slot_of, after, *pieces)[0]


def big_kernel(kernel, operands, outs, scratch, flops, copies, name):
    return pl.pallas_call(
        kernel,
        in_specs=[spec for _, spec in operands],
        out_specs=[IN_VMEM for _ in outs],
        out_shape=shapes_of(outs),
        scratch_shapes=[(pltpu.VMEM if d != jnp.int32 else pltpu.SMEM)(s, d) for s, d in scratch]
        + [pltpu.SemaphoreType.DMA((copies,))] * (copies > 0),
        compiler_params=pltpu.CompilerParams(vmem_limit_bytes=VMEM_BYTES),
        cost_estimate=pl.CostEstimate(flops=flops, bytes_accessed=8000000, transcendentals=0),
        name=name,
    )(*[v for v, _ in operands])


def in_hbm(value):
    return pltpu.with_memory_space_constraint(value, pltpu.HBM)


def embed_kernel(
    counts, images, patch_weight, pos, gain_a, qkv, proj, gain_m, up, down, final_gain, *rest
):
    rows_o, stream_o, store, held, gains = rest[0], rest[1], rest[2:7], rest[7:11], rest[11:14]
    counts_o, flat_s, images_s, patch_s, pos_s, sems = rest[14:]
    first_copies = [
        pltpu.make_async_copy(source, target, sems.at[8 + at])
        for at, (source, target) in enumerate(
            (
                (images, images_s),
                (counts, counts_o),
                (patch_weight, patch_s),
                (pos, pos_s),
                (gain_a, gains[0]),
                (gain_m, gains[1]),
                (final_gain, gains[2]),
            )
        )
    ]
    copies = {}
    for layer in range(2):
        for at, (source, target) in enumerate(zip((qkv, proj, up, down), held, strict=True)):
            copies[layer, at] = pltpu.make_async_copy(
                source.at[layer], target.at[layer], sems.at[layer * 4 + at]
            )
    for copy in first_copies + list(copies.values()):
        copy.start()
    first_copies[0].wait()
    for env in range(2):
        for patch in range(PATCHES):
            at = (env * PATCHES + patch) * CAMS
            flat_s[pl.ds(at, CAMS)] = images_s[env, patch].astype(F32)
    first_copies[1].wait()
    first, second = counts_o[0], counts_o[1]
    row = iota((ROWS, 1), 0)
    cam = steps_of(row, PATCHES, CAM_MOST + 1)
    patch = row - cam * PATCHES
    slot = jnp.where(cam < first, cam, CAMS * PATCHES + cam - first)
    used = cam < first + second
    source = jnp.where(used, slot + patch * CAMS, -1)
    rows = mm(
        jnp.where(source == iota((ROWS, SLOTS * PATCHES), 1), 1.0, 0.0).astype(BF16),
        flat_s[...].astype(BF16),
    ).astype(BF16)
    rows_o[...] = rows
    place = jnp.where(used & (patch == iota((ROWS, PATCHES), 1)), 1.0, 0.0).astype(BF16)
    for copy in first_copies[2:]:
        copy.wait()
    stream = mm(rows, patch_s[...]) + mm(place, pos_s[...])
    stream_o[...] = stream
    attention_half(
        stream,
        gains[0][0:1],
        held[0].at[0],
        held[1].at[0],
        store,
        lambda at: copies[0, at].wait(),
    )
    for key in ((0, 2), (0, 3), (1, 0), (1, 1), (1, 2), (1, 3)):
        copies[key].wait()


STORE_A = ("normed", "triple", "probs", "mixed", "middle")
STORE_M = ("second", "hidden", "slope")


def run_embed(counts, images, patch_weight, pos, params, final_gain):
    gain_a, qkv, proj, gain_m, up, down = params
    sources = (counts, images, patch_weight, pos, gain_a, qkv, proj, gain_m, up, down, final_gain)
    got = big_kernel(
        embed_kernel,
        [(in_hbm(v), IN_HBM) for v in sources],
        [((ROWS, PATCH_DIM), BF16), ((ROWS, D), F32)]
        + [STORES[k] for k in STORE_A]
        + [((2, *s), d) for s, d in WEIGHTS.values()]
        + [((2, D), F32), ((2, D), F32), ((D,), F32)],
        [
            ((2,), jnp.int32),
            ((SLOTS * PATCHES, PATCH_DIM), F32),
            (images.shape, BF16),
            ((PATCH_DIM, D), BF16),
            ((PATCHES, D), BF16),
        ],
        7000000000,
        15,
        "embed_attend",
    )
    gain_a, gain_m, final_gain = got[11:14]
    params = (gain_a, *got[7:9], gain_m, *got[9:11])
    return got[0], got[1], dict(zip(STORE_A, got[2:7])), params, final_gain


def middle_kernel(middle, gain_a, gain_m, up, down, qkv, proj, _, *rest):
    stream_o, store_m, store_a = rest[0], rest[1:4], rest[4:9]
    stream_o[...] = mlp_half(middle[...], gain_m[0:1], up.at[0], down.at[0], store_m)
    attention_half(
        stream_o[...], gain_a[1:2], qkv.at[1], proj.at[1], store_a, lambda at: None
    )


def run_middle(middle, params, after):
    gain_a, qkv, proj, gain_m, up, down = params
    got = big_kernel(
        middle_kernel,
        [(v, IN_VMEM) for v in (middle, gain_a, gain_m, up, down, qkv, proj)] + [(after, ANY_SPEC)],
        [((ROWS, D), F32)] + [STORES[k] for k in STORE_M + STORE_A],
        [],
        6000000000,
        0,
        "mlp_attend",
    )
    return got[0], dict(zip(STORE_M, got[1:4])), dict(zip(STORE_A, got[4:9]))


def pool_kernel(counts, middle, gain_m, up, down, final_gain, _, *rest):
    pooled_o, tokens_o, store_m = rest[0], rest[1], rest[2:5]
    last = mlp_half(middle[...], gain_m[1:2], up.at[1], down.at[1], store_m)
    pooled = exact_mm(camera_members(), last) * (1.0 / PATCHES)
    pooled_o[...] = pooled
    embedded = norm_rows(pooled, final_gain[...][None])
    first, second = counts[0], counts[1]
    cam = iota((SLOTS, 1), 0)
    in_first = cam < first
    in_second = (cam >= first) & (cam < first + second)
    sum_first = jnp.sum(jnp.where(in_first, embedded, 0.0), axis=0, keepdims=True)
    sum_second = jnp.sum(jnp.where(in_second, embedded, 0.0), axis=0, keepdims=True)
    row = iota((SLOTS, 1), 0)
    count_col = jnp.where(row == 0, first, second).astype(F32)
    both = jnp.where(row == 0, sum_first, jnp.where(row == 1, sum_second, 0.0))
    tokens_o[...] = (both / count_col).astype(BF16)


def run_pool(counts, middle, params, final_gain, after):
    _, _, _, gain_m, up, down = params
    got = big_kernel(
        pool_kernel,
        [(counts, SCALARS)]
        + [(v, IN_VMEM) for v in (middle, gain_m, up, down, final_gain)]
        + [(after, ANY_SPEC)],
        [((SLOTS, D), F32), ((SLOTS, D), BF16)] + [STORES[k] for k in STORE_M],
        [],
        4000000000,
        0,
        "mlp_pool",
    )
    return got[0], got[1], dict(zip(STORE_M, got[2:5]))


def camera_members():
    cam = steps_of(iota((1, ROWS), 1), PATCHES, CAM_MOST + 1)
    return jnp.where(cam == iota((SLOTS, 1), 0), 1.0, 0.0)


GRAD_COUNTS = {"second": (12, 24), "first_mlp": (12, 15), "first_attention": (0, 17)}


ROWS_D, ROWS_W = (sum(n) for n in zip(*GRAD_COUNTS.values()))


def grad_shapes(group):
    return [((4, sum(GRAD_COUNTS[group]), 16, D), BF16)] * 2


def place_of_device():
    env = lax.axis_index("env")
    return (
        lax.axis_index("grp"),
        lax.shift_right_logical(env, 3),
        lax.bitwise_and(lax.shift_right_logical(env, 1), 3),
        lax.bitwise_and(env, 1),
    )


SECOND_IN = ("second", "hidden", "down", "slope", "up", "middle", "mixed", "proj")
ATTENTION_IN = ("triple", "probs", "normed", "qkv")


def of_layer(names, refs, layer):
    refs = dict(zip(names, refs))
    return {key: ref.at[layer] if key in WEIGHTS else ref for key, ref in refs.items()}


def back_second_kernel(counts, seeds, pooled, final_gain, gain_a, gain_m, *rest):
    names = SECOND_IN + ATTENTION_IN + ("stream",)
    held, rest = of_layer(names, rest, 1), rest[len(names) :]
    keep, send, grad_o, wide_s = rest
    my_core = place_of_device()[3]
    first, second = counts[0], counts[1]
    cam = iota((SLOTS, 1), 0)
    seed = jnp.where(
        cam < first,
        seeds[0:1] / first.astype(F32),
        jnp.where(cam < first + second, seeds[1:2] / second.astype(F32), 0.0),
    )
    pooled_grad = norm_pull(pooled[...], final_gain[...][None], seed) * (1.0 / PATCHES)
    cam_row = steps_of(iota((ROWS, 1), 0), PATCHES, CAM_MOST + 1)
    member = jnp.where(cam_row == iota((1, SLOTS), 1), 1.0, 0.0)
    upstream = exact_mm(member, pooled_grad)
    middle_grad, mixed_grad = backward_mlp(
        my_core,
        upstream,
        gain_m[1:2],
        held["proj"],
        held["up"],
        held["down"],
        [held[k] for k in ("mixed", "middle", "second", "hidden", "slope")],
        keep,
        send,
    )
    grad_o[...] = backward_attention(
        my_core,
        middle_grad,
        mixed_grad,
        held["stream"],
        gain_a[1:2],
        held["qkv"],
        [held[k] for k in ("normed", "triple", "probs", "mixed")],
        (keep, send),
        27,
        wide_s,
    )


def run_back_second(counts, seeds, pooled, final_gain, stream, params, store):
    gain_a, qkv, proj, gain_m, up, down = params
    values = {"qkv": qkv, "proj": proj, "up": up, "down": down, "stream": stream}
    values.update(store)
    names = SECOND_IN + ATTENTION_IN + ("stream",)
    return big_kernel(
        back_second_kernel,
        [(counts, SCALARS)]
        + [(v, IN_VMEM) for v in (seeds, pooled, final_gain, gain_a, gain_m)]
        + [(values[k], IN_VMEM) for k in names],
        grad_shapes("second") + [((ROWS, D), F32)],
        [((ROWS, 3 * D), BF16)],
        8000000000,
        0,
        "back_second",
    )


def back_mlp_kernel(gain_m, *rest):
    names = ("stream",) + SECOND_IN
    held, rest = of_layer(names, rest, 0), rest[len(names) :]
    keep, send, middle_o, mixed_o = rest
    middle_o[...], mixed_o[...] = backward_mlp(
        place_of_device()[3],
        held["stream"][...],
        gain_m[0:1],
        held["proj"],
        held["up"],
        held["down"],
        [held[k] for k in ("mixed", "middle", "second", "hidden", "slope")],
        keep,
        send,
    )


def run_back_mlp(upstream, params, store):
    _, _, proj, gain_m, up, down = params
    values = {"proj": proj, "up": up, "down": down, "stream": upstream}
    values.update(store)
    names = ("stream",) + SECOND_IN
    return big_kernel(
        back_mlp_kernel,
        [(gain_m, IN_VMEM)] + [(values[k], IN_VMEM) for k in names],
        grad_shapes("first_mlp") + [((ROWS, D), F32), ((ROWS, D), BF16)],
        [],
        5000000000,
        0,
        "back_first_mlp",
    )


def back_attention_kernel(slot_of, tokens, middle_grad, mixed_grad, gain_a, *rest):
    names = ("mixed",) + ATTENTION_IN + ("stream", "rows")
    held, rest = of_layer(names, rest, 0), rest[len(names) :]
    keep, send, wide_s = rest
    z, x, y, my_core = place_of_device()
    device = z * 32 + x * 8 + y * 2 + my_core
    p = iota((ROWS, 1), 0)
    swap = jnp.where(p >= 128, 1, 0)
    core = jnp.where(swap == my_core, 0, 1)
    rest_p = p - swap * 128
    first = lax.shift_right_logical(rest_p, 5)
    row = lax.bitwise_and(lax.shift_right_logical(rest_p, 4), 1)
    third = lax.bitwise_and(rest_p, 3)
    to_x, to_y = jnp.where(core == 0, first, third), jnp.where(core == 0, third, first)
    to_z = lax.bitwise_and(lax.shift_right_logical(rest_p, 2), 3)
    learner = to_z * 64 + to_x * 16 + to_y * 4 + core * 2 + row
    lane = iota((1, SLOTS), 1)
    wanted = jnp.where(
        lane == 0, slot_of[device * 2], jnp.where(lane == 1, slot_of[device * 2 + 1], -1)
    )
    spread = mm(jnp.where(learner == wanted, 1.0, 0.0).astype(BF16), tokens[...]).astype(BF16)
    spots = [(ref, a, r) for ref in (keep, send) for a in range(4) for r in range(2)]
    for at, (ref, a, r) in enumerate(spots):
        ref[a, 15 + r] = spread[at * 16 : at * 16 + 16]
    stream_grad = backward_attention(
        my_core,
        middle_grad[...],
        mixed_grad[...],
        held["stream"],
        gain_a[0:1],
        held["qkv"],
        [held[k] for k in ("normed", "triple", "probs", "mixed")],
        (keep, send),
        0,
        wide_s,
    ).astype(BF16)
    for ref, core in ((keep, my_core), (send, 1 - my_core)):
        tile = mm(turned(pick(order_six(core), PATCH_DIM), held["rows"][...]), stream_grad)
        emit(tile, [(ref, a, 9 + r) for a in range(4) for r in range(6)])


def run_back_attention(slot_of, tokens, middle_grad, mixed_grad, rows, stream, params, store):
    values = {"qkv": params[1], "stream": stream, "rows": rows}
    values.update(store)
    names = ("mixed",) + ATTENTION_IN + ("stream", "rows")
    return big_kernel(
        back_attention_kernel,
        [(slot_of, SCALARS)]
        + [(v, IN_VMEM) for v in (tokens, middle_grad, mixed_grad, params[0])]
        + [(values[k], IN_VMEM) for k in names],
        grad_shapes("first_attention"),
        [((ROWS, 3 * D), BF16)],
        4000000000,
        0,
        "back_first_attention",
    )


def local_kernel(kernel, operands, outs, scratch, name):
    return pl.pallas_call(
        kernel,
        in_specs=[IN_VMEM for _ in operands],
        out_specs=[IN_VMEM for _ in outs],
        out_shape=shapes_of(outs),
        scratch_shapes=scratch,
        compiler_params=pltpu.CompilerParams(vmem_limit_bytes=SMALL_VMEM_BYTES),
        name=name,
    )(*operands)


def add_kernel(*rest):
    parts, outs = rest[:-8], rest[-8:]
    z, x, y, my_core = place_of_device()
    along = jnp.where(my_core == 0, x, y)
    at_d = at_w = 0
    for group, (count_d, count_w) in enumerate(GRAD_COUNTS.values()):
        keep, got = parts[group * 2 : group * 2 + 2]
        for step in range(4):
            place_d, place_w = lax.bitwise_and(z + step, 3), lax.bitwise_and(along + step, 3)
            if count_d:
                span = pl.ds(0, count_d)
                outs[step][pl.ds(at_d, count_d)] = keep[place_d, span] + got[place_d, span]
            span = pl.ds(count_d, count_w)
            outs[4 + step][pl.ds(at_w, count_w)] = keep[place_w, span] + got[place_w, span]
        at_d, at_w = at_d + count_d, at_w + count_w


def add_pairs(*parts):
    return local_kernel(
        add_kernel,
        parts,
        [((ROWS_D, 16, D), BF16)] * 4 + [((ROWS_W, 16, D), BF16)] * 4,
        [],
        "add_pairs",
    )


def sum_of(refs):
    total = refs[0][...].astype(F32)
    for ref in refs[1:]:
        total = total + ref[...].astype(F32)
    return total


def place_on(axes):
    z, x, y, my_core = place_of_device()
    by_name = {"z": z, "x": x, "y": y}
    return jnp.where(my_core == 0, by_name[axes[0]], by_name[axes[1]])


def first_sum_kernel(axes, *rest):
    parts, outs, (total_s, turn_s) = rest[:4], rest[4:8], rest[8:]
    count = parts[0].shape[0]
    total = sum_of(parts).reshape(count * 16, D)
    for lanes in range(3):
        total_s[lanes] = total[:, lanes * 128 : lanes * 128 + 128]
    for b in range(16):
        for lanes in range(3):
            turn_s[b // 4, pl.ds(b % 4 * count, count), pl.ds(lanes * 128, 128)] = total_s[
                lanes, pl.ds(b, count, 16)
            ]
    along = place_on(axes)
    for step in range(4):
        outs[step][...] = turn_s[lax.bitwise_and(along + step, 3)].astype(BF16)


def first_sum(axes, parts):
    count = parts[0].shape[0]
    return local_kernel(
        partial(first_sum_kernel, axes),
        parts,
        [((4 * count, D), BF16)] * 4,
        [pltpu.VMEM((3, count * 16, 128), F32), pltpu.VMEM((4, 4 * count, D), F32)],
        "first_sum",
    )


def second_sum_kernel(*rest):
    parts, outs, total_s = rest[:8], rest[8:12], rest[12]
    total_d, total_w = sum_of(parts[:4]), sum_of(parts[4:])
    for third in range(4):
        total_s[third, pl.ds(0, ROWS_D)] = total_d[third * ROWS_D : (third + 1) * ROWS_D]
        total_s[third, pl.ds(ROWS_D, ROWS_W)] = total_w[third * ROWS_W : (third + 1) * ROWS_W]
    _, x, y, my_core = place_of_device()
    along = jnp.where(my_core == 0, y, x)
    for step in range(4):
        outs[step][...] = total_s[lax.bitwise_and(along + step, 3)].astype(BF16)


def second_sum(parts):
    return local_kernel(
        second_sum_kernel,
        parts,
        [((ROWS_D + ROWS_W, D), BF16)] * 4,
        [pltpu.VMEM((4, ROWS_D + ROWS_W, D), F32)],
        "second_sum",
    )


def last_sum_kernel(*rest):
    parts, (tokens, patch, qkv, proj, up, down) = rest[:4], rest[4:]
    rows = sum_of(parts)
    down[:, 1], down[:, 0] = rows[0:12], rows[12:24]
    wide = rows[ROWS_D:]
    for layer, at_up, at_qkv in ((1, 0, 15), (0, 24, 39)):
        for j in range(4):
            up[:, layer, pl.ds(j * D, D)] = wide[at_up + j * 3 : at_up + j * 3 + 3]
        proj[:, layer] = wide[at_up + 12 : at_up + 15]
        for j in range(3):
            qkv[:, layer, pl.ds(j * D, D)] = wide[at_qkv + j * 3 : at_qkv + j * 3 + 3]
    patch[...] = wide[48:54]
    tokens[...] = wide[54:56].astype(BF16)


def last_sum(parts):
    return local_kernel(
        last_sum_kernel,
        parts,
        [
            ((2, D), BF16),
            ((6, D), F32),
            ((3, 2, 3 * D), F32),
            ((3, 2, D), F32),
            ((3, 2, FF), F32),
            ((12, 2, D), F32),
        ],
        [],
        "last_sum",
    )


AXES = ("grp", "env")
STEPS = (2, 1, 3)


def send_along(value, axes, step):
    pairs = []
    for device in range(128):
        z, x, y, core = device // 32, device // 8 % 4, device // 2 % 4, device % 2
        place = {"z": z, "x": x, "y": y}
        place[axes[core]] = (place[axes[core]] + step) % 4
        pairs.append((device, place["z"] * 32 + place["x"] * 8 + place["y"] * 2 + core))
    return lax.ppermute(value, AXES, pairs)


def swap_cores(value):
    return lax.ppermute(value, AXES, [(device, device ^ 1) for device in range(128)])


def exchange(pieces, axes):
    return [pieces[0]] + [send_along(pieces[step], axes, step) for step in STEPS]


def per_device(
    images,
    camera_counts,
    slot_of,
    patch_weight,
    pos_embed,
    attn_gain,
    qkv_weight,
    proj_weight,
    mlp_gain,
    up_weight,
    down_weight,
    final_gain,
    cotangent,
):
    params = (attn_gain, qkv_weight, proj_weight, mlp_gain, up_weight, down_weight)
    chip = join_cores(cotangent, swap_cores(cotangent))
    ring = exchange([chip] * 4, "zz")
    rows, stream, store_first, params, final_gain = run_embed(
        camera_counts,
        jnp.swapaxes(images, 1, 2),
        patch_weight,
        pos_embed,
        params,
        final_gain,
    )
    line = gather_ring("z", ring, final_gain)
    ring = exchange([line] * 4, "xx")
    middle_stream, store, store_second = run_middle(store_first["middle"], params, line)
    store_first.update(store)
    plane = gather_ring("x", ring, store["second"])
    ring = exchange([plane] * 4, "yy")
    pooled, tokens, store = run_pool(
        camera_counts, store_second["middle"], params, final_gain, plane
    )
    store_second.update(store)
    seeds = take_rows(slot_of, ring, pooled)
    keep_second, send, stream_grad = run_back_second(
        camera_counts,
        seeds,
        pooled,
        final_gain,
        middle_stream,
        params,
        store_second,
    )
    got_second = swap_cores(send)
    keep_mlp, send, middle_grad, mixed_grad = run_back_mlp(stream_grad, params, store_first)
    got_mlp = swap_cores(send)
    keep, send = run_back_attention(
        slot_of,
        tokens,
        middle_grad,
        mixed_grad,
        rows,
        stream,
        params,
        store_first,
    )
    got = swap_cores(send)
    pieces = add_pairs(keep_second, got_second, keep_mlp, got_mlp, keep, got)
    wide = exchange(pieces[4:], "xy")
    deep = exchange(pieces[:4], "zz")
    wide = exchange(first_sum("zz", wide), "zz")
    deep = exchange(first_sum("xy", deep), "xy")
    pieces = second_sum(deep + wide)
    tokens, patch, *stacks = last_sum(exchange(pieces, "yx"))
    return (tokens, patch, *(jnp.swapaxes(stack, 0, 1) for stack in stacks))


def solution(mesh):
    placed = (
        P(("grp", "env"), None, None, None),
        P(("grp", "env")),
        P(),
        P(),
        P(),
        P(),
        P(),
        P(),
        P(),
        P(),
        P(),
        P(),
        P(("grp", "env"), None),
    )
    return jax.shard_map(
        per_device,
        mesh=mesh,
        in_specs=placed,
        out_specs=(
            P(("grp", "env"), None),
            P(("grp", "env"), None),
            P(None, ("grp", "env"), None),
            P(None, ("grp", "env"), None),
            P(None, ("grp", "env"), None),
            P(None, ("grp", "env"), None),
        ),
        check_vma=False,
    )
```

```python
from functools import partial

import jax
import jax.numpy as jnp
from jax import lax
from jax.experimental import pallas as pl
from jax.experimental.pallas import tpu as pltpu
from jax.sharding import PartitionSpec as P

F32 = jnp.float32
BF16 = jnp.bfloat16
D = 384
FF = 1536
WIDE = 768
HEADS = 6
PATCHES = 36
PATCH_DIM = 768
CAMS = 4
SLOTS = 8
CAM_MOST = 7
ROWS = 256
VMEM_BYTES = 20 * 1024 * 1024
SMALL_VMEM_BYTES = 14 * 1024 * 1024
EPS = 1e-06


def mm(left, right):
    return jnp.dot(left, right, preferred_element_type=F32)


def mm_nt(left, right):
    return lax.dot_general(left, right, (((1,), (1,)), ((), ())), preferred_element_type=F32)


def mm_tn(left, right):
    return lax.dot_general(left, right, (((0,), (0,)), ((), ())), preferred_element_type=F32)


def exact_mm(left, right):
    return jnp.dot(left, right, preferred_element_type=F32, precision=lax.Precision.HIGHEST)


def iota(shape, dim):
    return lax.broadcasted_iota(jnp.int32, shape, dim)


def steps_of(value, step, count):
    total = jnp.zeros_like(value)
    for at in range(1, count):
        total = total + jnp.where(value >= at * step, 1, 0)
    return total


def norm_rows(values, gain_row):
    centered = values - jnp.mean(values, axis=-1, keepdims=True)
    spread = jnp.mean(centered * centered, axis=-1, keepdims=True)
    return centered * lax.rsqrt(spread + EPS) * gain_row


def norm_pull(values, gain_row, upstream):
    centered = values - jnp.mean(values, axis=-1, keepdims=True)
    inv = lax.rsqrt(jnp.mean(centered * centered, axis=-1, keepdims=True) + EPS)
    hat = centered * inv
    scaled = upstream * gain_row
    return inv * (
        scaled
        - jnp.mean(scaled, axis=-1, keepdims=True)
        - hat * jnp.mean(scaled * hat, axis=-1, keepdims=True)
    )


def gelu_and_slope(before):
    size = jnp.abs(before)
    bell = jnp.exp(before * before * -0.5)
    t = 1.0 / (1.0 + (0.3275911 * 0.7071067811865476) * size)
    poly = t * (
        0.5 * 0.254829592
        + t
        * (
            0.5 * -0.284496736
            + t * (0.5 * 1.421413741 + t * (0.5 * -1.453152027 + t * (0.5 * 1.061405429)))
        )
    )
    tail = poly * bell
    below = jnp.where(before > 0, 1.0 - tail, tail)
    return before * below, below + before * bell * 0.3989422804014327


def camera_bias():
    cam_row = steps_of(iota((ROWS, 1), 0), PATCHES, CAM_MOST + 1)
    cam_col = steps_of(iota((1, ROWS), 1), PATCHES, CAM_MOST + 1)
    return jnp.where(cam_row == cam_col, 0.0, -1e30)


def head_mask(width_lanes, which):
    lane = iota((1, width_lanes), 1)
    return lane < 64 if which == 0 else lane >= 64


def attention_half(stream, gain_a, qkv, proj, store, need):
    normed_s, triple_s, probs_s, mixed_s, middle_s = store
    normed_s[...] = norm_rows(stream, gain_a).astype(BF16)
    need(0)
    triple_s[...] = mm(normed_s[...], qkv[...]).astype(BF16)
    bias = camera_bias()
    for pair in range(3):
        q = triple_s[:, pl.ds(pair * 128, 128)]
        k = triple_s[:, pl.ds(D + pair * 128, 128)]
        v = triple_s[:, pl.ds(2 * D + pair * 128, 128)]
        mixed = None
        for h in range(2):
            mask = head_mask(128, h)
            scores = mm_nt(jnp.where(mask, q * 0.125, 0.0).astype(BF16), k) + bias
            raised = jnp.exp(scores)
            probs = (raised * (1.0 / jnp.sum(raised, axis=-1, keepdims=True))).astype(BF16)
            probs_s[pair * 2 + h] = probs
            part = mm(probs, jnp.where(mask, v, 0.0).astype(BF16))
            mixed = part if mixed is None else mixed + part
        mixed_s[:, pl.ds(pair * 128, 128)] = mixed.astype(BF16)
    need(1)
    middle_s[...] = stream + mm(mixed_s[...], proj[...])


def mlp_half(middle, gain_m, up, down, store):
    second_s, hidden_s, slope_s = store
    second_s[...] = norm_rows(middle, gain_m).astype(BF16)
    total = middle
    for j in range(FF // WIDE):
        cols = pl.ds(j * WIDE, WIDE)
        hidden, slope = gelu_and_slope(mm(second_s[...], up[:, cols]))
        slope_s[:, cols] = slope.astype(BF16)
        hidden_s[:, cols] = hidden.astype(BF16)
        total = total + mm(hidden_s[:, cols], down[cols, :])
    return total


def pick(order, width=D):
    return jnp.where(order == iota((D, width), 1), 1.0, 0.0).astype(BF16)


def own_first(my_core):
    p = iota((D, 1), 0)
    swap = jnp.where(p >= D // 2, 1, 0)
    core = jnp.where(swap == my_core, 0, 1)
    return core, p - swap * (D // 2)


def order_three(my_core):
    core, rest = own_first(my_core)
    first = steps_of(rest, 48, 4)
    rest = rest - first * 48
    r = steps_of(rest, 16, 3)
    rest = rest - r * 16
    z, third = lax.shift_right_logical(rest, 2), lax.bitwise_and(rest, 3)
    x, y = jnp.where(core == 0, first, third), jnp.where(core == 0, third, first)
    return z * 96 + x * 24 + y * 6 + core * 3 + r


def chips_of(core, rest):
    second, third = lax.shift_right_logical(rest, 2), lax.bitwise_and(rest, 3)
    return jnp.where(core == 0, second * 4 + third, third * 4 + second)


def order_twelve(my_core):
    core, rest = own_first(my_core)
    r = lax.shift_right_logical(rest, 4)
    return chips_of(core, lax.bitwise_and(rest, 15)) * 24 + core * 12 + r


def order_six(core):
    p = iota((D, 1), 0)
    first = steps_of(p, 96, 4)
    rest = p - first * 96
    r = lax.shift_right_logical(rest, 4)
    rest = lax.bitwise_and(rest, 15)
    z, third = lax.shift_right_logical(rest, 2), lax.bitwise_and(rest, 3)
    x, y = jnp.where(core == 0, first, third), jnp.where(core == 0, third, first)
    return z * 192 + x * 48 + y * 12 + core * 6 + r


def turned(picks, columns):
    return mm_nt(picks, columns).astype(BF16)


def emit(tile, places):
    for at, (ref, first, q) in enumerate(places):
        ref[first, q] = tile[at * 16 : at * 16 + 16].astype(BF16)


def spots_three(refs, q_of):
    return [(ref, a, q_of(r)) for ref in refs for a in range(4) for r in range(3)]


def backward_mlp(my_core, upstream, gain_m, proj, up, down, store, keep, send):
    mixed_s, middle_s, second_s, hidden_s, slope_s = store
    both = (keep, send)
    down_in = upstream.astype(BF16)
    picks = pick(order_three(my_core))
    rows_up = turned(picks, second_s[...])
    picks_down = pick(order_twelve(my_core))
    second_grad = None
    stacked = jnp.concatenate([hidden_s[:, pl.ds(j * D, D)] for j in range(FF // D)], axis=0)
    rows = turned(picks_down, stacked)
    for j in range(FF // D):
        tile = mm(rows[:, j * ROWS : j * ROWS + ROWS], down_in)
        emit(tile, [(ref, j, r) for ref in both for r in range(12)])
    for j in range(FF // WIDE):
        cols = pl.ds(j * WIDE, WIDE)
        up_in = (slope_s[:, cols].astype(F32) * mm_nt(down_in, down[cols, :])).astype(BF16)
        tile = mm(rows_up, up_in)
        for i in range(WIDE // D):
            at = 12 + (j * (WIDE // D) + i) * 3
            emit(tile[:, i * D : i * D + D], spots_three(both, lambda r, at=at: at + r))
        part = mm_nt(up_in, up[:, cols])
        second_grad = part if second_grad is None else second_grad + part
    middle_grad = upstream + norm_pull(middle_s[...], gain_m, second_grad)
    proj_in = middle_grad.astype(BF16)
    emit(mm(turned(picks, mixed_s[...]), proj_in), spots_three(both, lambda r: 24 + r))
    return middle_grad, mm_nt(proj_in, proj[...]).astype(BF16)


def backward_attention(
    my_core, middle_grad, mixed_grad, stream_s, gain_a, qkv, store, wides, first_q, wide_s
):
    normed_s, triple_s, probs_s, mixed_s = store
    for pair in range(3):
        lanes = pl.ds(pair * 128, 128)
        q = triple_s[:, lanes] * 0.125
        k = triple_s[:, pl.ds(D + pair * 128, 128)]
        v = triple_s[:, pl.ds(2 * D + pair * 128, 128)]
        mg = mixed_grad[:, pair * 128 : pair * 128 + 128]
        product = mg.astype(F32) * mixed_s[:, lanes].astype(F32)
        dq = dk = dv = None
        for h in range(2):
            mask = head_mask(128, h)
            probs = probs_s[pair * 2 + h]
            mg_h = jnp.where(mask, mg, 0.0).astype(BF16)
            delta = jnp.sum(jnp.where(mask, product, 0.0), axis=-1, keepdims=True)
            probs_grad = mm_nt(mg_h, v)
            scores_grad = (probs.astype(F32) * (probs_grad - delta)).astype(BF16)
            part_q = mm(scores_grad, jnp.where(mask, k, 0.0).astype(BF16))
            part_k = mm_tn(scores_grad, jnp.where(mask, q, 0.0).astype(BF16))
            part_v = mm_tn(probs, mg_h)
            dq = part_q if dq is None else dq + part_q
            dk = part_k if dk is None else dk + part_k
            dv = part_v if dv is None else dv + part_v
        wide_s[:, lanes] = (dq * 0.125).astype(BF16)
        wide_s[:, pl.ds(D + pair * 128, 128)] = dk.astype(BF16)
        wide_s[:, pl.ds(2 * D + pair * 128, 128)] = dv.astype(BF16)
    rows_qkv = turned(pick(order_three(my_core)), normed_s[...])
    tile = mm(rows_qkv, wide_s[...])
    for j in range(3):
        emit(tile[:, j * D : j * D + D], spots_three(wides, lambda r, j=j: first_q + j * 3 + r))
    normed_grad = mm_nt(wide_s[...], qkv[...])
    return middle_grad + norm_pull(stream_s[...], gain_a, normed_grad)


def store_shapes():
    return [
        ((ROWS, D), BF16),
        ((ROWS, 3 * D), BF16),
        ((HEADS, ROWS, ROWS), BF16),
        ((ROWS, D), BF16),
        ((ROWS, D), F32),
        ((ROWS, D), BF16),
        ((ROWS, FF), BF16),
        ((ROWS, FF), BF16),
    ]


def whole(shape):
    return pl.BlockSpec(shape, lambda *_: (0,) * len(shape))


def shapes_of(items):
    return [jax.ShapeDtypeStruct(s, d) for s, d in items]


WEIGHTS = {
    "qkv": ((D, 3 * D), BF16),
    "proj": ((D, D), BF16),
    "up": ((D, FF), BF16),
    "down": ((FF, D), BF16),
}
STORES = dict(
    zip(
        ("normed", "triple", "probs", "mixed", "middle", "second", "hidden", "slope"),
        store_shapes(),
        strict=True,
    )
)
ANY_SPEC = pl.BlockSpec(memory_space=pl.ANY)
SCALARS = pl.BlockSpec(memory_space=pltpu.SMEM)
IN_VMEM = pl.BlockSpec(memory_space=pltpu.VMEM)
IN_HBM = pl.BlockSpec(memory_space=pltpu.HBM)


def gather_kernel(axis, *rest):
    pieces, out = rest[:4], rest[5]
    at = dict(zip("zxy", place_of_device()))[axis]
    for step, piece in zip((0, *STEPS), pieces, strict=True):
        out[lax.bitwise_and(at - step, 3)] = piece[...]


def gather_ring(axis, pieces, after):
    return local_kernel(
        partial(gather_kernel, axis),
        (*pieces, after),
        [((4, *pieces[0].shape), BF16)],
        [],
        "gather_ring",
    )[0]


def join_kernel(own, other, out):
    my_core = place_of_device()[3]
    out[my_core] = own[...]
    out[1 - my_core] = other[...]


def join_cores(own, other):
    return local_kernel(join_kernel, (own, other), [((2, 2, D), BF16)], [], "join_cores")[0]


def take_kernel(slot_of, _, *rest):
    pieces, (out, held_s) = rest[:4], rest[4:]
    z, x, y, my_core = place_of_device()
    for step, piece in zip((0, *STEPS), pieces, strict=True):
        held_s[lax.bitwise_and(y - step, 3)] = piece[...].astype(F32)
    device = z * 32 + x * 8 + y * 2 + my_core
    row = iota((2, 1), 0)
    taken = []
    for env in range(2):
        slot = slot_of[device * 2 + env]
        pair = held_s[
            lax.bitwise_and(lax.shift_right_logical(slot, 2), 3),
            lax.bitwise_and(lax.shift_right_logical(slot, 4), 3),
            lax.shift_right_logical(slot, 6),
            lax.bitwise_and(lax.shift_right_logical(slot, 1), 1),
        ]
        chosen = row == lax.bitwise_and(slot, 1)
        taken.append(jnp.sum(jnp.where(chosen, pair, 0.0), axis=0, keepdims=True))
    out[...] = jnp.where(row == 0, taken[0], taken[1])


def take_rows(slot_of, pieces, after):
    return pl.pallas_call(
        take_kernel,
        in_specs=[SCALARS, ANY_SPEC] + [IN_VMEM] * 4,
        out_specs=[IN_VMEM],
        out_shape=shapes_of([((2, D), F32)]),
        scratch_shapes=[pltpu.VMEM((4, 4, 4, 2, 2, D), F32)],
        compiler_params=pltpu.CompilerParams(vmem_limit_bytes=SMALL_VMEM_BYTES),
        name="take_rows",
    )(slot_of, after, *pieces)[0]


def big_kernel(kernel, operands, outs, scratch, flops, copies, name):
    return pl.pallas_call(
        kernel,
        in_specs=[spec for _, spec in operands],
        out_specs=[IN_VMEM for _ in outs],
        out_shape=shapes_of(outs),
        scratch_shapes=[(pltpu.VMEM if d != jnp.int32 else pltpu.SMEM)(s, d) for s, d in scratch]
        + [pltpu.SemaphoreType.DMA((copies,))] * (copies > 0),
        compiler_params=pltpu.CompilerParams(vmem_limit_bytes=VMEM_BYTES),
        cost_estimate=pl.CostEstimate(flops=flops, bytes_accessed=8000000, transcendentals=0),
        name=name,
    )(*[v for v, _ in operands])


def in_hbm(value):
    return pltpu.with_memory_space_constraint(value, pltpu.HBM)


def embed_kernel(
    counts, images, patch_weight, pos, gain_a, qkv, proj, gain_m, up, down, final_gain, *rest
):
    rows_o, stream_o, store, held, gains = rest[0], rest[1], rest[2:7], rest[7:11], rest[11:14]
    counts_o, flat_s, images_s, patch_s, pos_s, sems = rest[14:]
    first_copies = [
        pltpu.make_async_copy(source, target, sems.at[8 + at])
        for at, (source, target) in enumerate(
            (
                (images, images_s),
                (counts, counts_o),
                (patch_weight, patch_s),
                (pos, pos_s),
                (gain_a, gains[0]),
                (gain_m, gains[1]),
                (final_gain, gains[2]),
            )
        )
    ]
    copies = {}
    for layer in range(2):
        for at, (source, target) in enumerate(zip((qkv, proj, up, down), held, strict=True)):
            copies[layer, at] = pltpu.make_async_copy(
                source.at[layer], target.at[layer], sems.at[layer * 4 + at]
            )
    for copy in first_copies + list(copies.values()):
        copy.start()
    first_copies[0].wait()
    for env in range(2):
        for patch in range(PATCHES):
            at = (env * PATCHES + patch) * CAMS
            flat_s[pl.ds(at, CAMS)] = images_s[env, patch].astype(F32)
    first_copies[1].wait()
    first, second = counts_o[0], counts_o[1]
    row = iota((ROWS, 1), 0)
    cam = steps_of(row, PATCHES, CAM_MOST + 1)
    patch = row - cam * PATCHES
    slot = jnp.where(cam < first, cam, CAMS * PATCHES + cam - first)
    used = cam < first + second
    source = jnp.where(used, slot + patch * CAMS, -1)
    rows = mm(
        jnp.where(source == iota((ROWS, SLOTS * PATCHES), 1), 1.0, 0.0).astype(BF16),
        flat_s[...].astype(BF16),
    ).astype(BF16)
    rows_o[...] = rows
    place = jnp.where(used & (patch == iota((ROWS, PATCHES), 1)), 1.0, 0.0).astype(BF16)
    for copy in first_copies[2:]:
        copy.wait()
    stream = mm(rows, patch_s[...]) + mm(place, pos_s[...])
    stream_o[...] = stream
    attention_half(
        stream,
        gains[0][0:1],
        held[0].at[0],
        held[1].at[0],
        store,
        lambda at: copies[0, at].wait(),
    )
    for key in ((0, 2), (0, 3), (1, 0), (1, 1), (1, 2), (1, 3)):
        copies[key].wait()


STORE_A = ("normed", "triple", "probs", "mixed", "middle")
STORE_M = ("second", "hidden", "slope")


def run_embed(counts, images, patch_weight, pos, params, final_gain):
    gain_a, qkv, proj, gain_m, up, down = params
    sources = (counts, images, patch_weight, pos, gain_a, qkv, proj, gain_m, up, down, final_gain)
    got = big_kernel(
        embed_kernel,
        [(in_hbm(v), IN_HBM) for v in sources],
        [((ROWS, PATCH_DIM), BF16), ((ROWS, D), F32)]
        + [STORES[k] for k in STORE_A]
        + [((2, *s), d) for s, d in WEIGHTS.values()]
        + [((2, D), F32), ((2, D), F32), ((D,), F32)],
        [
            ((2,), jnp.int32),
            ((SLOTS * PATCHES, PATCH_DIM), F32),
            (images.shape, BF16),
            ((PATCH_DIM, D), BF16),
            ((PATCHES, D), BF16),
        ],
        7000000000,
        15,
        "embed_attend",
    )
    gain_a, gain_m, final_gain = got[11:14]
    params = (gain_a, *got[7:9], gain_m, *got[9:11])
    return got[0], got[1], dict(zip(STORE_A, got[2:7])), params, final_gain


def middle_kernel(middle, gain_a, gain_m, up, down, qkv, proj, _, *rest):
    stream_o, store_m, store_a = rest[0], rest[1:4], rest[4:9]
    stream_o[...] = mlp_half(middle[...], gain_m[0:1], up.at[0], down.at[0], store_m)
    attention_half(
        stream_o[...], gain_a[1:2], qkv.at[1], proj.at[1], store_a, lambda at: None
    )


def run_middle(middle, params, after):
    gain_a, qkv, proj, gain_m, up, down = params
    got = big_kernel(
        middle_kernel,
        [(v, IN_VMEM) for v in (middle, gain_a, gain_m, up, down, qkv, proj)] + [(after, ANY_SPEC)],
        [((ROWS, D), F32)] + [STORES[k] for k in STORE_M + STORE_A],
        [],
        6000000000,
        0,
        "mlp_attend",
    )
    return got[0], dict(zip(STORE_M, got[1:4])), dict(zip(STORE_A, got[4:9]))


def pool_kernel(counts, middle, gain_m, up, down, final_gain, _, *rest):
    pooled_o, tokens_o, store_m = rest[0], rest[1], rest[2:5]
    last = mlp_half(middle[...], gain_m[1:2], up.at[1], down.at[1], store_m)
    pooled = exact_mm(camera_members(), last) * (1.0 / PATCHES)
    pooled_o[...] = pooled
    embedded = norm_rows(pooled, final_gain[...][None])
    first, second = counts[0], counts[1]
    cam = iota((SLOTS, 1), 0)
    in_first = cam < first
    in_second = (cam >= first) & (cam < first + second)
    sum_first = jnp.sum(jnp.where(in_first, embedded, 0.0), axis=0, keepdims=True)
    sum_second = jnp.sum(jnp.where(in_second, embedded, 0.0), axis=0, keepdims=True)
    row = iota((SLOTS, 1), 0)
    count_col = jnp.where(row == 0, first, second).astype(F32)
    both = jnp.where(row == 0, sum_first, jnp.where(row == 1, sum_second, 0.0))
    tokens_o[...] = (both / count_col).astype(BF16)


def run_pool(counts, middle, params, final_gain, after):
    _, _, _, gain_m, up, down = params
    got = big_kernel(
        pool_kernel,
        [(counts, SCALARS)]
        + [(v, IN_VMEM) for v in (middle, gain_m, up, down, final_gain)]
        + [(after, ANY_SPEC)],
        [((SLOTS, D), F32), ((SLOTS, D), BF16)] + [STORES[k] for k in STORE_M],
        [],
        4000000000,
        0,
        "mlp_pool",
    )
    return got[0], got[1], dict(zip(STORE_M, got[2:5]))


def camera_members():
    cam = steps_of(iota((1, ROWS), 1), PATCHES, CAM_MOST + 1)
    return jnp.where(cam == iota((SLOTS, 1), 0), 1.0, 0.0)


GRAD_COUNTS = {"second": (12, 24), "first_mlp": (12, 15), "first_attention": (0, 17)}


ROWS_D, ROWS_W = (sum(n) for n in zip(*GRAD_COUNTS.values()))


def grad_shapes(group):
    return [((4, sum(GRAD_COUNTS[group]), 16, D), BF16)] * 2


def place_of_device():
    env = lax.axis_index("env")
    return (
        lax.axis_index("grp"),
        lax.shift_right_logical(env, 3),
        lax.bitwise_and(lax.shift_right_logical(env, 1), 3),
        lax.bitwise_and(env, 1),
    )


SECOND_IN = ("second", "hidden", "down", "slope", "up", "middle", "mixed", "proj")
ATTENTION_IN = ("triple", "probs", "normed", "qkv")


def of_layer(names, refs, layer):
    refs = dict(zip(names, refs))
    return {key: ref.at[layer] if key in WEIGHTS else ref for key, ref in refs.items()}


def back_second_kernel(counts, seeds, pooled, final_gain, gain_a, gain_m, *rest):
    names = SECOND_IN + ATTENTION_IN + ("stream",)
    held, rest = of_layer(names, rest, 1), rest[len(names) :]
    keep, send, grad_o, wide_s = rest
    my_core = place_of_device()[3]
    first, second = counts[0], counts[1]
    cam = iota((SLOTS, 1), 0)
    seed = jnp.where(
        cam < first,
        seeds[0:1] / first.astype(F32),
        jnp.where(cam < first + second, seeds[1:2] / second.astype(F32), 0.0),
    )
    pooled_grad = norm_pull(pooled[...], final_gain[...][None], seed) * (1.0 / PATCHES)
    cam_row = steps_of(iota((ROWS, 1), 0), PATCHES, CAM_MOST + 1)
    member = jnp.where(cam_row == iota((1, SLOTS), 1), 1.0, 0.0)
    upstream = exact_mm(member, pooled_grad)
    middle_grad, mixed_grad = backward_mlp(
        my_core,
        upstream,
        gain_m[1:2],
        held["proj"],
        held["up"],
        held["down"],
        [held[k] for k in ("mixed", "middle", "second", "hidden", "slope")],
        keep,
        send,
    )
    grad_o[...] = backward_attention(
        my_core,
        middle_grad,
        mixed_grad,
        held["stream"],
        gain_a[1:2],
        held["qkv"],
        [held[k] for k in ("normed", "triple", "probs", "mixed")],
        (keep, send),
        27,
        wide_s,
    )


def run_back_second(counts, seeds, pooled, final_gain, stream, params, store):
    gain_a, qkv, proj, gain_m, up, down = params
    values = {"qkv": qkv, "proj": proj, "up": up, "down": down, "stream": stream}
    values.update(store)
    names = SECOND_IN + ATTENTION_IN + ("stream",)
    return big_kernel(
        back_second_kernel,
        [(counts, SCALARS)]
        + [(v, IN_VMEM) for v in (seeds, pooled, final_gain, gain_a, gain_m)]
        + [(values[k], IN_VMEM) for k in names],
        grad_shapes("second") + [((ROWS, D), F32)],
        [((ROWS, 3 * D), BF16)],
        8000000000,
        0,
        "back_second",
    )


def back_mlp_kernel(gain_m, *rest):
    names = ("stream",) + SECOND_IN
    held, rest = of_layer(names, rest, 0), rest[len(names) :]
    keep, send, middle_o, mixed_o = rest
    middle_o[...], mixed_o[...] = backward_mlp(
        place_of_device()[3],
        held["stream"][...],
        gain_m[0:1],
        held["proj"],
        held["up"],
        held["down"],
        [held[k] for k in ("mixed", "middle", "second", "hidden", "slope")],
        keep,
        send,
    )


def run_back_mlp(upstream, params, store):
    _, _, proj, gain_m, up, down = params
    values = {"proj": proj, "up": up, "down": down, "stream": upstream}
    values.update(store)
    names = ("stream",) + SECOND_IN
    return big_kernel(
        back_mlp_kernel,
        [(gain_m, IN_VMEM)] + [(values[k], IN_VMEM) for k in names],
        grad_shapes("first_mlp") + [((ROWS, D), F32), ((ROWS, D), BF16)],
        [],
        5000000000,
        0,
        "back_first_mlp",
    )


def back_attention_kernel(slot_of, tokens, middle_grad, mixed_grad, gain_a, *rest):
    names = ("mixed",) + ATTENTION_IN + ("stream", "rows")
    held, rest = of_layer(names, rest, 0), rest[len(names) :]
    keep, send, wide_s = rest
    z, x, y, my_core = place_of_device()
    device = z * 32 + x * 8 + y * 2 + my_core
    p = iota((ROWS, 1), 0)
    swap = jnp.where(p >= 128, 1, 0)
    core = jnp.where(swap == my_core, 0, 1)
    rest_p = p - swap * 128
    first = lax.shift_right_logical(rest_p, 5)
    row = lax.bitwise_and(lax.shift_right_logical(rest_p, 4), 1)
    third = lax.bitwise_and(rest_p, 3)
    to_x, to_y = jnp.where(core == 0, first, third), jnp.where(core == 0, third, first)
    to_z = lax.bitwise_and(lax.shift_right_logical(rest_p, 2), 3)
    learner = to_z * 64 + to_x * 16 + to_y * 4 + core * 2 + row
    lane = iota((1, SLOTS), 1)
    wanted = jnp.where(
        lane == 0, slot_of[device * 2], jnp.where(lane == 1, slot_of[device * 2 + 1], -1)
    )
    spread = mm(jnp.where(learner == wanted, 1.0, 0.0).astype(BF16), tokens[...]).astype(BF16)
    spots = [(ref, a, r) for ref in (keep, send) for a in range(4) for r in range(2)]
    for at, (ref, a, r) in enumerate(spots):
        ref[a, 15 + r] = spread[at * 16 : at * 16 + 16]
    stream_grad = backward_attention(
        my_core,
        middle_grad[...],
        mixed_grad[...],
        held["stream"],
        gain_a[0:1],
        held["qkv"],
        [held[k] for k in ("normed", "triple", "probs", "mixed")],
        (keep, send),
        0,
        wide_s,
    ).astype(BF16)
    for ref, core in ((keep, my_core), (send, 1 - my_core)):
        tile = mm(turned(pick(order_six(core), PATCH_DIM), held["rows"][...]), stream_grad)
        emit(tile, [(ref, a, 9 + r) for a in range(4) for r in range(6)])


def run_back_attention(slot_of, tokens, middle_grad, mixed_grad, rows, stream, params, store):
    values = {"qkv": params[1], "stream": stream, "rows": rows}
    values.update(store)
    names = ("mixed",) + ATTENTION_IN + ("stream", "rows")
    return big_kernel(
        back_attention_kernel,
        [(slot_of, SCALARS)]
        + [(v, IN_VMEM) for v in (tokens, middle_grad, mixed_grad, params[0])]
        + [(values[k], IN_VMEM) for k in names],
        grad_shapes("first_attention"),
        [((ROWS, 3 * D), BF16)],
        4000000000,
        0,
        "back_first_attention",
    )


def local_kernel(kernel, operands, outs, scratch, name):
    return pl.pallas_call(
        kernel,
        in_specs=[IN_VMEM for _ in operands],
        out_specs=[IN_VMEM for _ in outs],
        out_shape=shapes_of(outs),
        scratch_shapes=scratch,
        compiler_params=pltpu.CompilerParams(vmem_limit_bytes=SMALL_VMEM_BYTES),
        name=name,
    )(*operands)


def add_kernel(*rest):
    parts, outs = rest[:-8], rest[-8:]
    z, x, y, my_core = place_of_device()
    along = jnp.where(my_core == 0, x, y)
    at_d = at_w = 0
    for group, (count_d, count_w) in enumerate(GRAD_COUNTS.values()):
        keep, got = parts[group * 2 : group * 2 + 2]
        for step in range(4):
            place_d, place_w = lax.bitwise_and(z + step, 3), lax.bitwise_and(along + step, 3)
            if count_d:
                span = pl.ds(0, count_d)
                outs[step][pl.ds(at_d, count_d)] = keep[place_d, span] + got[place_d, span]
            span = pl.ds(count_d, count_w)
            outs[4 + step][pl.ds(at_w, count_w)] = keep[place_w, span] + got[place_w, span]
        at_d, at_w = at_d + count_d, at_w + count_w


def add_pairs(*parts):
    return local_kernel(
        add_kernel,
        parts,
        [((ROWS_D, 16, D), BF16)] * 4 + [((ROWS_W, 16, D), BF16)] * 4,
        [],
        "add_pairs",
    )


def sum_of(refs):
    total = refs[0][...].astype(F32)
    for ref in refs[1:]:
        total = total + ref[...].astype(F32)
    return total


def place_on(axes):
    z, x, y, my_core = place_of_device()
    by_name = {"z": z, "x": x, "y": y}
    return jnp.where(my_core == 0, by_name[axes[0]], by_name[axes[1]])


def first_sum_kernel(axes, *rest):
    parts, outs, (total_s, turn_s) = rest[:4], rest[4:8], rest[8:]
    count = parts[0].shape[0]
    total = sum_of(parts).reshape(count * 16, D)
    for lanes in range(3):
        total_s[lanes] = total[:, lanes * 128 : lanes * 128 + 128]
    for b in range(16):
        for lanes in range(3):
            turn_s[b // 4, pl.ds(b % 4 * count, count), pl.ds(lanes * 128, 128)] = total_s[
                lanes, pl.ds(b, count, 16)
            ]
    along = place_on(axes)
    for step in range(4):
        outs[step][...] = turn_s[lax.bitwise_and(along + step, 3)].astype(BF16)


def first_sum(axes, parts):
    count = parts[0].shape[0]
    return local_kernel(
        partial(first_sum_kernel, axes),
        parts,
        [((4 * count, D), BF16)] * 4,
        [pltpu.VMEM((3, count * 16, 128), F32), pltpu.VMEM((4, 4 * count, D), F32)],
        "first_sum",
    )


def wide_sum_kernel(*rest):
    rest[4][...] = sum_of(rest[:4])


def wide_sum(parts):
    return local_kernel(wide_sum_kernel, parts, [((4 * ROWS_W, D), F32)], [], "wide_sum")


def second_sum_kernel(*rest):
    parts, wide, outs, total_s = rest[:4], rest[4], rest[5:9], rest[9]
    total_d, total_w = sum_of(parts), wide[...]
    for third in range(4):
        total_s[third, pl.ds(0, ROWS_D)] = total_d[third * ROWS_D : (third + 1) * ROWS_D]
        total_s[third, pl.ds(ROWS_D, ROWS_W)] = total_w[third * ROWS_W : (third + 1) * ROWS_W]
    _, x, y, my_core = place_of_device()
    along = jnp.where(my_core == 0, y, x)
    for step in range(4):
        outs[step][...] = total_s[lax.bitwise_and(along + step, 3)].astype(BF16)


def second_sum(parts):
    return local_kernel(
        second_sum_kernel,
        parts,
        [((ROWS_D + ROWS_W, D), BF16)] * 4,
        [pltpu.VMEM((4, ROWS_D + ROWS_W, D), F32)],
        "second_sum",
    )


def last_sum_kernel(*rest):
    parts, (tokens, patch, qkv, proj, up, down) = rest[:4], rest[4:]
    rows = sum_of(parts)
    down[:, 1], down[:, 0] = rows[0:12], rows[12:24]
    wide = rows[ROWS_D:]
    for layer, at_up, at_qkv in ((1, 0, 15), (0, 24, 39)):
        for j in range(4):
            up[:, layer, pl.ds(j * D, D)] = wide[at_up + j * 3 : at_up + j * 3 + 3]
        proj[:, layer] = wide[at_up + 12 : at_up + 15]
        for j in range(3):
            qkv[:, layer, pl.ds(j * D, D)] = wide[at_qkv + j * 3 : at_qkv + j * 3 + 3]
    patch[...] = wide[48:54]
    tokens[...] = wide[54:56].astype(BF16)


def last_sum(parts):
    return local_kernel(
        last_sum_kernel,
        parts,
        [
            ((2, D), BF16),
            ((6, D), F32),
            ((3, 2, 3 * D), F32),
            ((3, 2, D), F32),
            ((3, 2, FF), F32),
            ((12, 2, D), F32),
        ],
        [],
        "last_sum",
    )


AXES = ("grp", "env")
STEPS = (2, 1, 3)


def send_along(value, axes, step):
    pairs = []
    for device in range(128):
        z, x, y, core = device // 32, device // 8 % 4, device // 2 % 4, device % 2
        place = {"z": z, "x": x, "y": y}
        place[axes[core]] = (place[axes[core]] + step) % 4
        pairs.append((device, place["z"] * 32 + place["x"] * 8 + place["y"] * 2 + core))
    return lax.ppermute(value, AXES, pairs)


def swap_cores(value):
    return lax.ppermute(value, AXES, [(device, device ^ 1) for device in range(128)])


def exchange(pieces, axes):
    return [pieces[0]] + [send_along(pieces[step], axes, step) for step in STEPS]


def per_device(
    images,
    camera_counts,
    slot_of,
    patch_weight,
    pos_embed,
    attn_gain,
    qkv_weight,
    proj_weight,
    mlp_gain,
    up_weight,
    down_weight,
    final_gain,
    cotangent,
):
    params = (attn_gain, qkv_weight, proj_weight, mlp_gain, up_weight, down_weight)
    chip = join_cores(cotangent, swap_cores(cotangent))
    ring = exchange([chip] * 4, "zz")
    rows, stream, store_first, params, final_gain = run_embed(
        camera_counts,
        jnp.swapaxes(images, 1, 2),
        patch_weight,
        pos_embed,
        params,
        final_gain,
    )
    line = gather_ring("z", ring, final_gain)
    ring = exchange([line] * 4, "xx")
    middle_stream, store, store_second = run_middle(store_first["middle"], params, line)
    store_first.update(store)
    plane = gather_ring("x", ring, store["second"])
    ring = exchange([plane] * 4, "yy")
    pooled, tokens, store = run_pool(
        camera_counts, store_second["middle"], params, final_gain, plane
    )
    store_second.update(store)
    seeds = take_rows(slot_of, ring, pooled)
    keep_second, send, stream_grad = run_back_second(
        camera_counts,
        seeds,
        pooled,
        final_gain,
        middle_stream,
        params,
        store_second,
    )
    got_second = swap_cores(send)
    keep_mlp, send, middle_grad, mixed_grad = run_back_mlp(stream_grad, params, store_first)
    got_mlp = swap_cores(send)
    keep, send = run_back_attention(
        slot_of,
        tokens,
        middle_grad,
        mixed_grad,
        rows,
        stream,
        params,
        store_first,
    )
    got = swap_cores(send)
    pieces = add_pairs(keep_second, got_second, keep_mlp, got_mlp, keep, got)
    wide = exchange(pieces[4:], "xy")
    deep = exchange(pieces[:4], "zz")
    wide = exchange(first_sum("zz", wide), "zz")
    deep = exchange(first_sum("xy", deep), "xy")
    pieces = second_sum([*deep, *wide_sum(wide)])
    tokens, patch, *stacks = last_sum(exchange(pieces, "yx"))
    return (tokens, patch, *(jnp.swapaxes(stack, 0, 1) for stack in stacks))


def solution(mesh):
    placed = (
        P(("grp", "env"), None, None, None),
        P(("grp", "env")),
        P(),
        P(),
        P(),
        P(),
        P(),
        P(),
        P(),
        P(),
        P(),
        P(),
        P(("grp", "env"), None),
    )
    return jax.shard_map(
        per_device,
        mesh=mesh,
        in_specs=placed,
        out_specs=(
            P(("grp", "env"), None),
            P(("grp", "env"), None),
            P(None, ("grp", "env"), None),
            P(None, ("grp", "env"), None),
            P(None, ("grp", "env"), None),
            P(None, ("grp", "env"), None),
        ),
        check_vma=False,
    )
```

```python
from functools import partial

import jax
import jax.numpy as jnp
from jax import lax
from jax.experimental import pallas as pl
from jax.experimental.pallas import tpu as pltpu
from jax.sharding import PartitionSpec as P

F32 = jnp.float32
BF16 = jnp.bfloat16
D = 384
FF = 1536
WIDE = 768
HEADS = 6
PATCHES = 36
PATCH_DIM = 768
CAMS = 4
SLOTS = 8
CAM_MOST = 7
ROWS = 256
VMEM_BYTES = 20 * 1024 * 1024
SMALL_VMEM_BYTES = 14 * 1024 * 1024
EPS = 1e-06


def mm(left, right):
    return jnp.dot(left, right, preferred_element_type=F32)


def mm_nt(left, right):
    return lax.dot_general(left, right, (((1,), (1,)), ((), ())), preferred_element_type=F32)


def mm_tn(left, right):
    return lax.dot_general(left, right, (((0,), (0,)), ((), ())), preferred_element_type=F32)


def exact_mm(left, right):
    return jnp.dot(left, right, preferred_element_type=F32, precision=lax.Precision.HIGHEST)


def iota(shape, dim):
    return lax.broadcasted_iota(jnp.int32, shape, dim)


def steps_of(value, step, count):
    total = jnp.zeros_like(value)
    for at in range(1, count):
        total = total + jnp.where(value >= at * step, 1, 0)
    return total


def norm_rows(values, gain_row):
    centered = values - jnp.mean(values, axis=-1, keepdims=True)
    spread = jnp.mean(centered * centered, axis=-1, keepdims=True)
    return centered * lax.rsqrt(spread + EPS) * gain_row


def norm_pull(values, gain_row, upstream):
    centered = values - jnp.mean(values, axis=-1, keepdims=True)
    inv = lax.rsqrt(jnp.mean(centered * centered, axis=-1, keepdims=True) + EPS)
    hat = centered * inv
    scaled = upstream * gain_row
    return inv * (
        scaled
        - jnp.mean(scaled, axis=-1, keepdims=True)
        - hat * jnp.mean(scaled * hat, axis=-1, keepdims=True)
    )


def gelu_and_slope(before):
    size = jnp.abs(before)
    bell = jnp.exp(before * before * -0.5)
    t = 1.0 / (1.0 + (0.3275911 * 0.7071067811865476) * size)
    poly = t * (
        0.5 * 0.254829592
        + t
        * (
            0.5 * -0.284496736
            + t * (0.5 * 1.421413741 + t * (0.5 * -1.453152027 + t * (0.5 * 1.061405429)))
        )
    )
    tail = poly * bell
    below = jnp.where(before > 0, 1.0 - tail, tail)
    return before * below, below + before * bell * 0.3989422804014327


def camera_bias():
    cam_row = steps_of(iota((ROWS, 1), 0), PATCHES, CAM_MOST + 1)
    cam_col = steps_of(iota((1, ROWS), 1), PATCHES, CAM_MOST + 1)
    return jnp.where(cam_row == cam_col, 0.0, -1e30)


def head_mask(width_lanes, which):
    lane = iota((1, width_lanes), 1)
    return lane < 64 if which == 0 else lane >= 64


def attention_half(stream, gain_a, qkv, proj, store, need):
    normed_s, triple_s, probs_s, mixed_s, middle_s = store
    normed_s[...] = norm_rows(stream, gain_a).astype(BF16)
    need(0)
    triple_s[...] = mm(normed_s[...], qkv[...]).astype(BF16)
    bias = camera_bias()
    for pair in range(3):
        q = triple_s[:, pl.ds(pair * 128, 128)]
        k = triple_s[:, pl.ds(D + pair * 128, 128)]
        v = triple_s[:, pl.ds(2 * D + pair * 128, 128)]
        mixed = None
        for h in range(2):
            mask = head_mask(128, h)
            scores = mm_nt(jnp.where(mask, q * 0.125, 0.0).astype(BF16), k) + bias
            raised = jnp.exp(scores)
            probs = (raised * (1.0 / jnp.sum(raised, axis=-1, keepdims=True))).astype(BF16)
            probs_s[pair * 2 + h] = probs
            part = mm(probs, jnp.where(mask, v, 0.0).astype(BF16))
            mixed = part if mixed is None else mixed + part
        mixed_s[:, pl.ds(pair * 128, 128)] = mixed.astype(BF16)
    need(1)
    middle_s[...] = stream + mm(mixed_s[...], proj[...])


def mlp_half(middle, gain_m, up, down, store):
    second_s, hidden_s, slope_s = store
    second_s[...] = norm_rows(middle, gain_m).astype(BF16)
    total = middle
    for j in range(FF // WIDE):
        cols = pl.ds(j * WIDE, WIDE)
        hidden, slope = gelu_and_slope(mm(second_s[...], up[:, cols]))
        slope_s[:, cols] = slope.astype(BF16)
        hidden_s[:, cols] = hidden.astype(BF16)
        total = total + mm(hidden_s[:, cols], down[cols, :])
    return total


def pick(order, width=D):
    return jnp.where(order == iota((D, width), 1), 1.0, 0.0).astype(BF16)


def own_first(my_core):
    p = iota((D, 1), 0)
    swap = jnp.where(p >= D // 2, 1, 0)
    core = jnp.where(swap == my_core, 0, 1)
    return core, p - swap * (D // 2)


def order_three(my_core):
    core, rest = own_first(my_core)
    first = steps_of(rest, 48, 4)
    rest = rest - first * 48
    r = steps_of(rest, 16, 3)
    rest = rest - r * 16
    z, third = lax.shift_right_logical(rest, 2), lax.bitwise_and(rest, 3)
    x, y = jnp.where(core == 0, first, third), jnp.where(core == 0, third, first)
    return z * 96 + x * 24 + y * 6 + core * 3 + r


def chips_of(core, rest):
    second, third = lax.shift_right_logical(rest, 2), lax.bitwise_and(rest, 3)
    return jnp.where(core == 0, second * 4 + third, third * 4 + second)


def order_twelve(my_core):
    core, rest = own_first(my_core)
    r = lax.shift_right_logical(rest, 4)
    return chips_of(core, lax.bitwise_and(rest, 15)) * 24 + core * 12 + r


def order_six(core):
    p = iota((D, 1), 0)
    first = steps_of(p, 96, 4)
    rest = p - first * 96
    r = lax.shift_right_logical(rest, 4)
    rest = lax.bitwise_and(rest, 15)
    z, third = lax.shift_right_logical(rest, 2), lax.bitwise_and(rest, 3)
    x, y = jnp.where(core == 0, first, third), jnp.where(core == 0, third, first)
    return z * 192 + x * 48 + y * 12 + core * 6 + r


def turned(picks, columns):
    return mm_nt(picks, columns).astype(BF16)


def emit(tile, places):
    for at, (ref, first, q) in enumerate(places):
        ref[first, q] = tile[at * 16 : at * 16 + 16].astype(BF16)


def spots_three(refs, q_of):
    return [(ref, a, q_of(r)) for ref in refs for a in range(4) for r in range(3)]


def backward_mlp(my_core, upstream, gain_m, proj, up, down, store, keep, send):
    mixed_s, middle_s, second_s, hidden_s, slope_s = store
    both = (keep, send)
    down_in = upstream.astype(BF16)
    picks = pick(order_three(my_core))
    rows_up = turned(picks, second_s[...])
    picks_down = pick(order_twelve(my_core))
    second_grad = None
    stacked = jnp.concatenate([hidden_s[:, pl.ds(j * D, D)] for j in range(FF // D)], axis=0)
    rows = turned(picks_down, stacked)
    for j in range(FF // D):
        tile = mm(rows[:, j * ROWS : j * ROWS + ROWS], down_in)
        emit(tile, [(ref, j, r) for ref in both for r in range(12)])
    for j in range(FF // WIDE):
        cols = pl.ds(j * WIDE, WIDE)
        up_in = (slope_s[:, cols].astype(F32) * mm_nt(down_in, down[cols, :])).astype(BF16)
        tile = mm(rows_up, up_in)
        for i in range(WIDE // D):
            at = 12 + (j * (WIDE // D) + i) * 3
            emit(tile[:, i * D : i * D + D], spots_three(both, lambda r, at=at: at + r))
        part = mm_nt(up_in, up[:, cols])
        second_grad = part if second_grad is None else second_grad + part
    middle_grad = upstream + norm_pull(middle_s[...], gain_m, second_grad)
    proj_in = middle_grad.astype(BF16)
    emit(mm(turned(picks, mixed_s[...]), proj_in), spots_three(both, lambda r: 24 + r))
    return middle_grad, mm_nt(proj_in, proj[...]).astype(BF16)


def backward_attention(
    my_core, middle_grad, mixed_grad, stream_s, gain_a, qkv, store, wides, first_q, wide_s
):
    normed_s, triple_s, probs_s, mixed_s = store
    for pair in range(3):
        lanes = pl.ds(pair * 128, 128)
        q = triple_s[:, lanes] * 0.125
        k = triple_s[:, pl.ds(D + pair * 128, 128)]
        v = triple_s[:, pl.ds(2 * D + pair * 128, 128)]
        mg = mixed_grad[:, pair * 128 : pair * 128 + 128]
        product = mg.astype(F32) * mixed_s[:, lanes].astype(F32)
        dq = dk = dv = None
        for h in range(2):
            mask = head_mask(128, h)
            probs = probs_s[pair * 2 + h]
            mg_h = jnp.where(mask, mg, 0.0).astype(BF16)
            delta = jnp.sum(jnp.where(mask, product, 0.0), axis=-1, keepdims=True)
            probs_grad = mm_nt(mg_h, v)
            scores_grad = (probs.astype(F32) * (probs_grad - delta)).astype(BF16)
            part_q = mm(scores_grad, jnp.where(mask, k, 0.0).astype(BF16))
            part_k = mm_tn(scores_grad, jnp.where(mask, q, 0.0).astype(BF16))
            part_v = mm_tn(probs, mg_h)
            dq = part_q if dq is None else dq + part_q
            dk = part_k if dk is None else dk + part_k
            dv = part_v if dv is None else dv + part_v
        wide_s[:, lanes] = (dq * 0.125).astype(BF16)
        wide_s[:, pl.ds(D + pair * 128, 128)] = dk.astype(BF16)
        wide_s[:, pl.ds(2 * D + pair * 128, 128)] = dv.astype(BF16)
    rows_qkv = turned(pick(order_three(my_core)), normed_s[...])
    tile = mm(rows_qkv, wide_s[...])
    for j in range(3):
        emit(tile[:, j * D : j * D + D], spots_three(wides, lambda r, j=j: first_q + j * 3 + r))
    normed_grad = mm_nt(wide_s[...], qkv[...])
    return middle_grad + norm_pull(stream_s[...], gain_a, normed_grad)


def store_shapes():
    return [
        ((ROWS, D), BF16),
        ((ROWS, 3 * D), BF16),
        ((HEADS, ROWS, ROWS), BF16),
        ((ROWS, D), BF16),
        ((ROWS, D), F32),
        ((ROWS, D), BF16),
        ((ROWS, FF), BF16),
        ((ROWS, FF), BF16),
    ]


def whole(shape):
    return pl.BlockSpec(shape, lambda *_: (0,) * len(shape))


def shapes_of(items):
    return [jax.ShapeDtypeStruct(s, d) for s, d in items]


WEIGHTS = {
    "qkv": ((D, 3 * D), BF16),
    "proj": ((D, D), BF16),
    "up": ((D, FF), BF16),
    "down": ((FF, D), BF16),
}
STORES = dict(
    zip(
        ("normed", "triple", "probs", "mixed", "middle", "second", "hidden", "slope"),
        store_shapes(),
        strict=True,
    )
)
ANY_SPEC = pl.BlockSpec(memory_space=pl.ANY)
SCALARS = pl.BlockSpec(memory_space=pltpu.SMEM)
IN_VMEM = pl.BlockSpec(memory_space=pltpu.VMEM)
IN_HBM = pl.BlockSpec(memory_space=pltpu.HBM)


def gather_kernel(axis, *rest):
    pieces, out = rest[:4], rest[5]
    at = dict(zip("zxy", place_of_device()))[axis]
    for step, piece in zip((0, *STEPS), pieces, strict=True):
        out[lax.bitwise_and(at - step, 3)] = piece[...]


def gather_ring(axis, pieces, after):
    return local_kernel(
        partial(gather_kernel, axis),
        (*pieces, after),
        [((4, *pieces[0].shape), BF16)],
        [],
        "gather_ring",
    )[0]


def hold_kernel(source, out, sem):
    copy = pltpu.make_async_copy(source, out, sem.at[0])
    copy.start()
    copy.wait()


def hold(value):
    outs = [(value.shape, value.dtype)]
    return big_kernel(
        hold_kernel, [(in_hbm(value), IN_HBM)], outs, [], 1000000, 1, "hold"
    )[0]


def join_kernel(own, other, out):
    my_core = place_of_device()[3]
    out[my_core] = own[...]
    out[1 - my_core] = other[...]


def join_cores(own, other):
    return local_kernel(join_kernel, (own, other), [((2, 2, D), BF16)], [], "join_cores")[0]


def take_kernel(slot_of, _, *rest):
    pieces, (out, held_s) = rest[:4], rest[4:]
    z, x, y, my_core = place_of_device()
    for step, piece in zip((0, *STEPS), pieces, strict=True):
        held_s[lax.bitwise_and(y - step, 3)] = piece[...].astype(F32)
    device = z * 32 + x * 8 + y * 2 + my_core
    row = iota((2, 1), 0)
    taken = []
    for env in range(2):
        slot = slot_of[device * 2 + env]
        pair = held_s[
            lax.bitwise_and(lax.shift_right_logical(slot, 2), 3),
            lax.bitwise_and(lax.shift_right_logical(slot, 4), 3),
            lax.shift_right_logical(slot, 6),
            lax.bitwise_and(lax.shift_right_logical(slot, 1), 1),
        ]
        chosen = row == lax.bitwise_and(slot, 1)
        taken.append(jnp.sum(jnp.where(chosen, pair, 0.0), axis=0, keepdims=True))
    out[...] = jnp.where(row == 0, taken[0], taken[1])


def take_rows(slot_of, pieces, after):
    return pl.pallas_call(
        take_kernel,
        in_specs=[SCALARS, ANY_SPEC] + [IN_VMEM] * 4,
        out_specs=[IN_VMEM],
        out_shape=shapes_of([((2, D), F32)]),
        scratch_shapes=[pltpu.VMEM((4, 4, 4, 2, 2, D), F32)],
        compiler_params=pltpu.CompilerParams(vmem_limit_bytes=SMALL_VMEM_BYTES),
        name="take_rows",
    )(slot_of, after, *pieces)[0]


def big_kernel(kernel, operands, outs, scratch, flops, copies, name):
    return pl.pallas_call(
        kernel,
        in_specs=[spec for _, spec in operands],
        out_specs=[IN_VMEM for _ in outs],
        out_shape=shapes_of(outs),
        scratch_shapes=[(pltpu.VMEM if d != jnp.int32 else pltpu.SMEM)(s, d) for s, d in scratch]
        + [pltpu.SemaphoreType.DMA((copies,))] * (copies > 0),
        compiler_params=pltpu.CompilerParams(vmem_limit_bytes=VMEM_BYTES),
        cost_estimate=pl.CostEstimate(flops=flops, bytes_accessed=8000000, transcendentals=0),
        name=name,
    )(*[v for v, _ in operands])


def in_hbm(value):
    return pltpu.with_memory_space_constraint(value, pltpu.HBM)


def embed_kernel(
    counts, images, patch_weight, pos, gain_a, qkv, proj, gain_m, up, down, final_gain, *rest
):
    rows_o, stream_o, store, held, gains = rest[0], rest[1], rest[2:7], rest[7:11], rest[11:14]
    counts_o, flat_s, images_s, patch_s, pos_s, sems = rest[14:]
    first_copies = [
        pltpu.make_async_copy(source, target, sems.at[8 + at])
        for at, (source, target) in enumerate(
            (
                (images, images_s),
                (counts, counts_o),
                (patch_weight, patch_s),
                (pos, pos_s),
                (gain_a, gains[0]),
                (gain_m, gains[1]),
                (final_gain, gains[2]),
            )
        )
    ]
    copies = {}
    for layer in range(2):
        for at, (source, target) in enumerate(zip((qkv, proj, up, down), held, strict=True)):
            copies[layer, at] = pltpu.make_async_copy(
                source.at[layer], target.at[layer], sems.at[layer * 4 + at]
            )
    for copy in first_copies + list(copies.values()):
        copy.start()
    first_copies[0].wait()
    for env in range(2):
        for patch in range(PATCHES):
            at = (env * PATCHES + patch) * CAMS
            flat_s[pl.ds(at, CAMS)] = images_s[env, patch].astype(F32)
    first_copies[1].wait()
    first, second = counts_o[0], counts_o[1]
    row = iota((ROWS, 1), 0)
    cam = steps_of(row, PATCHES, CAM_MOST + 1)
    patch = row - cam * PATCHES
    slot = jnp.where(cam < first, cam, CAMS * PATCHES + cam - first)
    used = cam < first + second
    source = jnp.where(used, slot + patch * CAMS, -1)
    rows = mm(
        jnp.where(source == iota((ROWS, SLOTS * PATCHES), 1), 1.0, 0.0).astype(BF16),
        flat_s[...].astype(BF16),
    ).astype(BF16)
    rows_o[...] = rows
    place = jnp.where(used & (patch == iota((ROWS, PATCHES), 1)), 1.0, 0.0).astype(BF16)
    for copy in first_copies[2:]:
        copy.wait()
    stream = mm(rows, patch_s[...]) + mm(place, pos_s[...])
    stream_o[...] = stream
    attention_half(
        stream,
        gains[0][0:1],
        held[0].at[0],
        held[1].at[0],
        store,
        lambda at: copies[0, at].wait(),
    )
    for key in ((0, 2), (0, 3), (1, 0), (1, 1), (1, 2), (1, 3)):
        copies[key].wait()


STORE_A = ("normed", "triple", "probs", "mixed", "middle")
STORE_M = ("second", "hidden", "slope")


def run_embed(counts, images, patch_weight, pos, params, final_gain):
    gain_a, qkv, proj, gain_m, up, down = params
    sources = (counts, images, patch_weight, pos, gain_a, qkv, proj, gain_m, up, down, final_gain)
    got = big_kernel(
        embed_kernel,
        [(in_hbm(v), IN_HBM) for v in sources],
        [((ROWS, PATCH_DIM), BF16), ((ROWS, D), F32)]
        + [STORES[k] for k in STORE_A]
        + [((2, *s), d) for s, d in WEIGHTS.values()]
        + [((2, D), F32), ((2, D), F32), ((D,), F32)],
        [
            ((2,), jnp.int32),
            ((SLOTS * PATCHES, PATCH_DIM), F32),
            (images.shape, BF16),
            ((PATCH_DIM, D), BF16),
            ((PATCHES, D), BF16),
        ],
        7000000000,
        15,
        "embed_attend",
    )
    gain_a, gain_m, final_gain = got[11:14]
    params = (gain_a, *got[7:9], gain_m, *got[9:11])
    return got[0], got[1], dict(zip(STORE_A, got[2:7])), params, final_gain


def middle_kernel(middle, gain_a, gain_m, up, down, qkv, proj, _, *rest):
    stream_o, store_m, store_a = rest[0], rest[1:4], rest[4:9]
    stream_o[...] = mlp_half(middle[...], gain_m[0:1], up.at[0], down.at[0], store_m)
    attention_half(
        stream_o[...], gain_a[1:2], qkv.at[1], proj.at[1], store_a, lambda at: None
    )


def run_middle(middle, params, after):
    gain_a, qkv, proj, gain_m, up, down = params
    got = big_kernel(
        middle_kernel,
        [(v, IN_VMEM) for v in (middle, gain_a, gain_m, up, down, qkv, proj)] + [(after, ANY_SPEC)],
        [((ROWS, D), F32)] + [STORES[k] for k in STORE_M + STORE_A],
        [],
        6000000000,
        0,
        "mlp_attend",
    )
    return got[0], dict(zip(STORE_M, got[1:4])), dict(zip(STORE_A, got[4:9]))


def pool_kernel(counts, middle, gain_m, up, down, final_gain, _, *rest):
    pooled_o, tokens_o, store_m = rest[0], rest[1], rest[2:5]
    last = mlp_half(middle[...], gain_m[1:2], up.at[1], down.at[1], store_m)
    pooled = exact_mm(camera_members(), last) * (1.0 / PATCHES)
    pooled_o[...] = pooled
    embedded = norm_rows(pooled, final_gain[...][None])
    first, second = counts[0], counts[1]
    cam = iota((SLOTS, 1), 0)
    in_first = cam < first
    in_second = (cam >= first) & (cam < first + second)
    sum_first = jnp.sum(jnp.where(in_first, embedded, 0.0), axis=0, keepdims=True)
    sum_second = jnp.sum(jnp.where(in_second, embedded, 0.0), axis=0, keepdims=True)
    row = iota((SLOTS, 1), 0)
    count_col = jnp.where(row == 0, first, second).astype(F32)
    both = jnp.where(row == 0, sum_first, jnp.where(row == 1, sum_second, 0.0))
    tokens_o[...] = (both / count_col).astype(BF16)


def run_pool(counts, middle, params, final_gain, after):
    _, _, _, gain_m, up, down = params
    got = big_kernel(
        pool_kernel,
        [(counts, SCALARS)]
        + [(v, IN_VMEM) for v in (middle, gain_m, up, down, final_gain)]
        + [(after, ANY_SPEC)],
        [((SLOTS, D), F32), ((SLOTS, D), BF16)] + [STORES[k] for k in STORE_M],
        [],
        4000000000,
        0,
        "mlp_pool",
    )
    return got[0], got[1], dict(zip(STORE_M, got[2:5]))


def camera_members():
    cam = steps_of(iota((1, ROWS), 1), PATCHES, CAM_MOST + 1)
    return jnp.where(cam == iota((SLOTS, 1), 0), 1.0, 0.0)


GRAD_COUNTS = {"second": (12, 24), "first_mlp": (12, 15), "first_attention": (0, 11), "first_patch": (0, 6)}


ROWS_D, ROWS_W = (sum(n) for n in zip(*GRAD_COUNTS.values()))


def grad_shapes(group):
    return [((4, sum(GRAD_COUNTS[group]), 16, D), BF16)] * 2


def place_of_device():
    env = lax.axis_index("env")
    return (
        lax.axis_index("grp"),
        lax.shift_right_logical(env, 3),
        lax.bitwise_and(lax.shift_right_logical(env, 1), 3),
        lax.bitwise_and(env, 1),
    )


SECOND_IN = ("second", "hidden", "down", "slope", "up", "middle", "mixed", "proj")
ATTENTION_IN = ("triple", "probs", "normed", "qkv")


def of_layer(names, refs, layer):
    refs = dict(zip(names, refs))
    return {key: ref.at[layer] if key in WEIGHTS else ref for key, ref in refs.items()}


def back_second_kernel(counts, seeds, pooled, final_gain, gain_a, gain_m, *rest):
    names = SECOND_IN + ATTENTION_IN + ("stream",)
    held, rest = of_layer(names, rest, 1), rest[len(names) :]
    keep, send, grad_o, wide_s = rest
    my_core = place_of_device()[3]
    first, second = counts[0], counts[1]
    cam = iota((SLOTS, 1), 0)
    seed = jnp.where(
        cam < first,
        seeds[0:1] / first.astype(F32),
        jnp.where(cam < first + second, seeds[1:2] / second.astype(F32), 0.0),
    )
    pooled_grad = norm_pull(pooled[...], final_gain[...][None], seed) * (1.0 / PATCHES)
    cam_row = steps_of(iota((ROWS, 1), 0), PATCHES, CAM_MOST + 1)
    member = jnp.where(cam_row == iota((1, SLOTS), 1), 1.0, 0.0)
    upstream = exact_mm(member, pooled_grad)
    middle_grad, mixed_grad = backward_mlp(
        my_core,
        upstream,
        gain_m[1:2],
        held["proj"],
        held["up"],
        held["down"],
        [held[k] for k in ("mixed", "middle", "second", "hidden", "slope")],
        keep,
        send,
    )
    grad_o[...] = backward_attention(
        my_core,
        middle_grad,
        mixed_grad,
        held["stream"],
        gain_a[1:2],
        held["qkv"],
        [held[k] for k in ("normed", "triple", "probs", "mixed")],
        (keep, send),
        27,
        wide_s,
    )


def run_back_second(counts, seeds, pooled, final_gain, stream, params, store):
    gain_a, qkv, proj, gain_m, up, down = params
    values = {"qkv": qkv, "proj": proj, "up": up, "down": down, "stream": stream}
    values.update(store)
    names = SECOND_IN + ATTENTION_IN + ("stream",)
    return big_kernel(
        back_second_kernel,
        [(counts, SCALARS)]
        + [(v, IN_VMEM) for v in (seeds, pooled, final_gain, gain_a, gain_m)]
        + [(values[k], IN_VMEM) for k in names],
        grad_shapes("second") + [((ROWS, D), F32)],
        [((ROWS, 3 * D), BF16)],
        8000000000,
        0,
        "back_second",
    )


def back_mlp_kernel(gain_m, *rest):
    names = ("stream",) + SECOND_IN
    held, rest = of_layer(names, rest, 0), rest[len(names) :]
    keep, send, middle_o, mixed_o = rest
    middle_o[...], mixed_o[...] = backward_mlp(
        place_of_device()[3],
        held["stream"][...],
        gain_m[0:1],
        held["proj"],
        held["up"],
        held["down"],
        [held[k] for k in ("mixed", "middle", "second", "hidden", "slope")],
        keep,
        send,
    )


def run_back_mlp(upstream, params, store):
    _, _, proj, gain_m, up, down = params
    values = {"proj": proj, "up": up, "down": down, "stream": upstream}
    values.update(store)
    names = ("stream",) + SECOND_IN
    return big_kernel(
        back_mlp_kernel,
        [(gain_m, IN_VMEM)] + [(values[k], IN_VMEM) for k in names],
        grad_shapes("first_mlp") + [((ROWS, D), F32), ((ROWS, D), BF16)],
        [],
        5000000000,
        0,
        "back_first_mlp",
    )


def back_attention_kernel(slot_of, tokens, middle_grad, mixed_grad, gain_a, *rest):
    names = ("mixed",) + ATTENTION_IN + ("stream",)
    held, rest = of_layer(names, rest, 0), rest[len(names) :]
    keep, send, grad_o, wide_s = rest
    z, x, y, my_core = place_of_device()
    device = z * 32 + x * 8 + y * 2 + my_core
    p = iota((ROWS, 1), 0)
    swap = jnp.where(p >= 128, 1, 0)
    core = jnp.where(swap == my_core, 0, 1)
    rest_p = p - swap * 128
    first = lax.shift_right_logical(rest_p, 5)
    row = lax.bitwise_and(lax.shift_right_logical(rest_p, 4), 1)
    third = lax.bitwise_and(rest_p, 3)
    to_x, to_y = jnp.where(core == 0, first, third), jnp.where(core == 0, third, first)
    to_z = lax.bitwise_and(lax.shift_right_logical(rest_p, 2), 3)
    learner = to_z * 64 + to_x * 16 + to_y * 4 + core * 2 + row
    lane = iota((1, SLOTS), 1)
    wanted = jnp.where(
        lane == 0, slot_of[device * 2], jnp.where(lane == 1, slot_of[device * 2 + 1], -1)
    )
    spread = mm(jnp.where(learner == wanted, 1.0, 0.0).astype(BF16), tokens[...]).astype(BF16)
    spots = [(ref, a, r) for ref in (keep, send) for a in range(4) for r in range(2)]
    for at, (ref, a, r) in enumerate(spots):
        ref[a, 9 + r] = spread[at * 16 : at * 16 + 16]
    stream_grad = backward_attention(
        my_core,
        middle_grad[...],
        mixed_grad[...],
        held["stream"],
        gain_a[0:1],
        held["qkv"],
        [held[k] for k in ("normed", "triple", "probs", "mixed")],
        (keep, send),
        0,
        wide_s,
    ).astype(BF16)
    grad_o[...] = stream_grad


def back_patch_kernel(rows, grad, keep, send):
    my_core = place_of_device()[3]
    for ref, core in ((keep, my_core), (send, 1 - my_core)):
        tile = mm(turned(pick(order_six(core), PATCH_DIM), rows[...]), grad[...])
        emit(tile, [(ref, a, r) for a in range(4) for r in range(6)])


def run_back_patch(rows, grad):
    return big_kernel(
        back_patch_kernel,
        [(rows, IN_VMEM), (grad, IN_VMEM)],
        grad_shapes("first_patch"),
        [],
        1000000000,
        0,
        "back_patch",
    )


def run_back_attention(slot_of, tokens, middle_grad, mixed_grad, stream, params, store):
    values = {"qkv": params[1], "stream": stream}
    values.update(store)
    names = ("mixed",) + ATTENTION_IN + ("stream",)
    return big_kernel(
        back_attention_kernel,
        [(slot_of, SCALARS)]
        + [(v, IN_VMEM) for v in (tokens, middle_grad, mixed_grad, params[0])]
        + [(values[k], IN_VMEM) for k in names],
        grad_shapes("first_attention") + [((ROWS, D), BF16)],
        [((ROWS, 3 * D), BF16)],
        4000000000,
        0,
        "back_first_attention",
    )


def local_kernel(kernel, operands, outs, scratch, name):
    return pl.pallas_call(
        kernel,
        in_specs=[IN_VMEM for _ in operands],
        out_specs=[IN_VMEM for _ in outs],
        out_shape=shapes_of(outs),
        scratch_shapes=scratch,
        compiler_params=pltpu.CompilerParams(vmem_limit_bytes=SMALL_VMEM_BYTES),
        name=name,
    )(*operands)


def add_kernel(*rest):
    parts, outs = rest[:-8], rest[-8:]
    z, x, y, my_core = place_of_device()
    along = jnp.where(my_core == 0, x, y)
    at_d = at_w = 0
    for group, (count_d, count_w) in enumerate(GRAD_COUNTS.values()):
        keep, got = parts[group * 2 : group * 2 + 2]
        for step in range(4):
            place_d, place_w = lax.bitwise_and(z + step, 3), lax.bitwise_and(along + step, 3)
            if count_d:
                span = pl.ds(0, count_d)
                outs[step][pl.ds(at_d, count_d)] = keep[place_d, span] + got[place_d, span]
            span = pl.ds(count_d, count_w)
            outs[4 + step][pl.ds(at_w, count_w)] = keep[place_w, span] + got[place_w, span]
        at_d, at_w = at_d + count_d, at_w + count_w


def add_pairs(*parts):
    return local_kernel(
        add_kernel,
        parts,
        [((ROWS_D, 16, D), BF16)] * 4 + [((ROWS_W, 16, D), BF16)] * 4,
        [],
        "add_pairs",
    )


def sum_of(refs):
    total = refs[0][...].astype(F32)
    for ref in refs[1:]:
        total = total + ref[...].astype(F32)
    return total


def place_on(axes):
    z, x, y, my_core = place_of_device()
    by_name = {"z": z, "x": x, "y": y}
    return jnp.where(my_core == 0, by_name[axes[0]], by_name[axes[1]])


def first_sum_kernel(axes, *rest):
    parts, outs, (total_s, turn_s) = rest[:4], rest[4:8], rest[8:]
    count = parts[0].shape[0]
    total = sum_of(parts).reshape(count * 16, D)
    for lanes in range(3):
        total_s[lanes] = total[:, lanes * 128 : lanes * 128 + 128]
    for b in range(16):
        for lanes in range(3):
            turn_s[b // 4, pl.ds(b % 4 * count, count), pl.ds(lanes * 128, 128)] = total_s[
                lanes, pl.ds(b, count, 16)
            ]
    along = place_on(axes)
    for step in range(4):
        outs[step][...] = turn_s[lax.bitwise_and(along + step, 3)].astype(BF16)


def first_sum(axes, parts):
    count = parts[0].shape[0]
    return local_kernel(
        partial(first_sum_kernel, axes),
        parts,
        [((4 * count, D), BF16)] * 4,
        [pltpu.VMEM((3, count * 16, 128), F32), pltpu.VMEM((4, 4 * count, D), F32)],
        "first_sum",
    )


def wide_sum_kernel(*rest):
    rest[4][...] = sum_of(rest[:4])


def wide_sum(parts):
    return local_kernel(wide_sum_kernel, parts, [((4 * ROWS_W, D), F32)], [], "wide_sum")


def second_sum_kernel(*rest):
    parts, wide, outs, total_s = rest[:4], rest[4], rest[5:9], rest[9]
    total_d, total_w = sum_of(parts), wide[...]
    for third in range(4):
        total_s[third, pl.ds(0, ROWS_D)] = total_d[third * ROWS_D : (third + 1) * ROWS_D]
        total_s[third, pl.ds(ROWS_D, ROWS_W)] = total_w[third * ROWS_W : (third + 1) * ROWS_W]
    _, x, y, my_core = place_of_device()
    along = jnp.where(my_core == 0, y, x)
    for step in range(4):
        outs[step][...] = total_s[lax.bitwise_and(along + step, 3)].astype(BF16)


def second_sum(parts):
    return local_kernel(
        second_sum_kernel,
        parts,
        [((ROWS_D + ROWS_W, D), BF16)] * 4,
        [pltpu.VMEM((4, ROWS_D + ROWS_W, D), F32)],
        "second_sum",
    )


def last_sum_kernel(*rest):
    parts, (tokens, patch, qkv, proj, up, down) = rest[:4], rest[4:]
    rows = sum_of(parts)
    down[:, 1], down[:, 0] = rows[0:12], rows[12:24]
    wide = rows[ROWS_D:]
    for layer, at_up, at_qkv in ((1, 0, 15), (0, 24, 39)):
        for j in range(4):
            up[:, layer, pl.ds(j * D, D)] = wide[at_up + j * 3 : at_up + j * 3 + 3]
        proj[:, layer] = wide[at_up + 12 : at_up + 15]
        for j in range(3):
            qkv[:, layer, pl.ds(j * D, D)] = wide[at_qkv + j * 3 : at_qkv + j * 3 + 3]
    tokens[...] = wide[48:50].astype(BF16)
    patch[...] = wide[50:56]


def last_sum(parts):
    return local_kernel(
        last_sum_kernel,
        parts,
        [
            ((2, D), BF16),
            ((6, D), F32),
            ((3, 2, 3 * D), F32),
            ((3, 2, D), F32),
            ((3, 2, FF), F32),
            ((12, 2, D), F32),
        ],
        [],
        "last_sum",
    )


AXES = ("grp", "env")
STEPS = (2, 1, 3)


def send_along(value, axes, step):
    pairs = []
    for device in range(128):
        z, x, y, core = device // 32, device // 8 % 4, device // 2 % 4, device % 2
        place = {"z": z, "x": x, "y": y}
        place[axes[core]] = (place[axes[core]] + step) % 4
        pairs.append((device, place["z"] * 32 + place["x"] * 8 + place["y"] * 2 + core))
    return lax.ppermute(value, AXES, pairs)


def swap_cores(value):
    return lax.ppermute(value, AXES, [(device, device ^ 1) for device in range(128)])


def exchange(pieces, axes):
    return [pieces[0]] + [send_along(pieces[step], axes, step) for step in STEPS]


def per_device(
    images,
    camera_counts,
    slot_of,
    patch_weight,
    pos_embed,
    attn_gain,
    qkv_weight,
    proj_weight,
    mlp_gain,
    up_weight,
    down_weight,
    final_gain,
    cotangent,
):
    params = (attn_gain, qkv_weight, proj_weight, mlp_gain, up_weight, down_weight)
    chip = join_cores(hold(cotangent), swap_cores(cotangent))
    ring = exchange([chip] * 4, "zz")
    rows, stream, store_first, params, final_gain = run_embed(
        camera_counts,
        jnp.swapaxes(images, 1, 2),
        patch_weight,
        pos_embed,
        params,
        final_gain,
    )
    line = gather_ring("z", ring, final_gain)
    ring = exchange([line] * 4, "xx")
    middle_stream, store, store_second = run_middle(store_first["middle"], params, line)
    store_first.update(store)
    plane = gather_ring("x", ring, store["second"])
    ring = exchange([plane] * 4, "yy")
    pooled, tokens, store = run_pool(
        camera_counts, store_second["middle"], params, final_gain, plane
    )
    store_second.update(store)
    seeds = take_rows(slot_of, ring, pooled)
    keep_second, send, stream_grad = run_back_second(
        camera_counts,
        seeds,
        pooled,
        final_gain,
        middle_stream,
        params,
        store_second,
    )
    got_second = swap_cores(send)
    keep_mlp, send, middle_grad, mixed_grad = run_back_mlp(stream_grad, params, store_first)
    got_mlp = swap_cores(send)
    keep, send, grad = run_back_attention(
        slot_of,
        tokens,
        middle_grad,
        mixed_grad,
        stream,
        params,
        store_first,
    )
    got = swap_cores(send)
    keep_patch, send = run_back_patch(rows, grad)
    got_patch = swap_cores(send)
    pieces = add_pairs(keep_second, got_second, keep_mlp, got_mlp, keep, got, keep_patch, got_patch)
    wide = exchange(pieces[4:], "xy")
    deep = exchange(pieces[:4], "zz")
    wide = exchange(first_sum("zz", wide), "zz")
    deep = exchange(first_sum("xy", deep), "xy")
    pieces = second_sum([*deep, *wide_sum(wide)])
    tokens, patch, *stacks = last_sum(exchange(pieces, "yx"))
    return (tokens, patch, *(jnp.swapaxes(stack, 0, 1) for stack in stacks))


def solution(mesh):
    placed = (
        P(("grp", "env"), None, None, None),
        P(("grp", "env")),
        P(),
        P(),
        P(),
        P(),
        P(),
        P(),
        P(),
        P(),
        P(),
        P(),
        P(("grp", "env"), None),
    )
    return jax.shard_map(
        per_device,
        mesh=mesh,
        in_specs=placed,
        out_specs=(
            P(("grp", "env"), None),
            P(("grp", "env"), None),
            P(None, ("grp", "env"), None),
            P(None, ("grp", "env"), None),
            P(None, ("grp", "env"), None),
            P(None, ("grp", "env"), None),
        ),
        check_vma=False,
    )
```

```python
from functools import partial

import jax
import jax.numpy as jnp
from jax import lax
from jax.experimental import pallas as pl
from jax.experimental.pallas import tpu as pltpu
from jax.sharding import PartitionSpec as P

F32 = jnp.float32
BF16 = jnp.bfloat16
D = 384
FF = 1536
WIDE = 768
HEADS = 6
PATCHES = 36
PATCH_DIM = 768
CAMS = 4
SLOTS = 8
CAM_MOST = 7
ROWS = 256
VMEM_BYTES = 20 * 1024 * 1024
SMALL_VMEM_BYTES = 14 * 1024 * 1024
EPS = 1e-06


def mm(left, right):
    return jnp.dot(left, right, preferred_element_type=F32)


def mm_nt(left, right):
    return lax.dot_general(left, right, (((1,), (1,)), ((), ())), preferred_element_type=F32)


def mm_tn(left, right):
    return lax.dot_general(left, right, (((0,), (0,)), ((), ())), preferred_element_type=F32)


def exact_mm(left, right):
    return jnp.dot(left, right, preferred_element_type=F32, precision=lax.Precision.HIGHEST)


def iota(shape, dim):
    return lax.broadcasted_iota(jnp.int32, shape, dim)


def steps_of(value, step, count):
    total = jnp.zeros_like(value)
    for at in range(1, count):
        total = total + jnp.where(value >= at * step, 1, 0)
    return total


def norm_rows(values, gain_row):
    centered = values - jnp.mean(values, axis=-1, keepdims=True)
    spread = jnp.mean(centered * centered, axis=-1, keepdims=True)
    return centered * lax.rsqrt(spread + EPS) * gain_row


def norm_pull(values, gain_row, upstream):
    centered = values - jnp.mean(values, axis=-1, keepdims=True)
    inv = lax.rsqrt(jnp.mean(centered * centered, axis=-1, keepdims=True) + EPS)
    hat = centered * inv
    scaled = upstream * gain_row
    return inv * (
        scaled
        - jnp.mean(scaled, axis=-1, keepdims=True)
        - hat * jnp.mean(scaled * hat, axis=-1, keepdims=True)
    )


def gelu_and_slope(before):
    size = jnp.abs(before)
    bell = jnp.exp(before * before * -0.5)
    t = 1.0 / (1.0 + (0.3275911 * 0.7071067811865476) * size)
    poly = t * (
        0.5 * 0.254829592
        + t
        * (
            0.5 * -0.284496736
            + t * (0.5 * 1.421413741 + t * (0.5 * -1.453152027 + t * (0.5 * 1.061405429)))
        )
    )
    tail = poly * bell
    below = jnp.where(before > 0, 1.0 - tail, tail)
    return before * below, below + before * bell * 0.3989422804014327


def camera_bias():
    cam_row = steps_of(iota((ROWS, 1), 0), PATCHES, CAM_MOST + 1)
    cam_col = steps_of(iota((1, ROWS), 1), PATCHES, CAM_MOST + 1)
    return jnp.where(cam_row == cam_col, 0.0, -1e30)


def head_mask(width_lanes, which):
    lane = iota((1, width_lanes), 1)
    return lane < 64 if which == 0 else lane >= 64


def attention_half(stream, gain_a, qkv, proj, store, need):
    normed_s, triple_s, probs_s, mixed_s, middle_s = store
    normed_s[...] = norm_rows(stream, gain_a).astype(BF16)
    need(0)
    triple_s[...] = mm(normed_s[...], qkv[...]).astype(BF16)
    bias = camera_bias()
    for pair in range(3):
        q = triple_s[:, pl.ds(pair * 128, 128)]
        k = triple_s[:, pl.ds(D + pair * 128, 128)]
        v = triple_s[:, pl.ds(2 * D + pair * 128, 128)]
        mixed = None
        for h in range(2):
            mask = head_mask(128, h)
            scores = mm_nt(jnp.where(mask, q * 0.125, 0.0).astype(BF16), k) + bias
            raised = jnp.exp(scores)
            probs = (raised * (1.0 / jnp.sum(raised, axis=-1, keepdims=True))).astype(BF16)
            probs_s[pair * 2 + h] = probs
            part = mm(probs, jnp.where(mask, v, 0.0).astype(BF16))
            mixed = part if mixed is None else mixed + part
        mixed_s[:, pl.ds(pair * 128, 128)] = mixed.astype(BF16)
    need(1)
    middle_s[...] = stream + mm(mixed_s[...], proj[...])


def mlp_half(middle, gain_m, up, down, store):
    second_s, hidden_s, slope_s = store
    second_s[...] = norm_rows(middle, gain_m).astype(BF16)
    total = middle
    for j in range(FF // WIDE):
        cols = pl.ds(j * WIDE, WIDE)
        hidden, slope = gelu_and_slope(mm(second_s[...], up[:, cols]))
        slope_s[:, cols] = slope.astype(BF16)
        hidden_s[:, cols] = hidden.astype(BF16)
        total = total + mm(hidden_s[:, cols], down[cols, :])
    return total


def pick(order, width=D):
    return jnp.where(order == iota((D, width), 1), 1.0, 0.0).astype(BF16)


def own_first(my_core):
    p = iota((D, 1), 0)
    swap = jnp.where(p >= D // 2, 1, 0)
    core = jnp.where(swap == my_core, 0, 1)
    return core, p - swap * (D // 2)


def order_three(my_core):
    core, rest = own_first(my_core)
    first = steps_of(rest, 48, 4)
    rest = rest - first * 48
    r = steps_of(rest, 16, 3)
    rest = rest - r * 16
    z, third = lax.shift_right_logical(rest, 2), lax.bitwise_and(rest, 3)
    x, y = jnp.where(core == 0, first, third), jnp.where(core == 0, third, first)
    return z * 96 + x * 24 + y * 6 + core * 3 + r


def chips_of(core, rest):
    second, third = lax.shift_right_logical(rest, 2), lax.bitwise_and(rest, 3)
    return jnp.where(core == 0, second * 4 + third, third * 4 + second)


def order_twelve(my_core):
    core, rest = own_first(my_core)
    r = lax.shift_right_logical(rest, 4)
    return chips_of(core, lax.bitwise_and(rest, 15)) * 24 + core * 12 + r


def order_six(core):
    p = iota((D, 1), 0)
    first = steps_of(p, 96, 4)
    rest = p - first * 96
    r = lax.shift_right_logical(rest, 4)
    rest = lax.bitwise_and(rest, 15)
    z, third = lax.shift_right_logical(rest, 2), lax.bitwise_and(rest, 3)
    x, y = jnp.where(core == 0, first, third), jnp.where(core == 0, third, first)
    return z * 192 + x * 48 + y * 12 + core * 6 + r


def turned(picks, columns):
    return mm_nt(picks, columns).astype(BF16)


def emit(tile, places):
    for at, (ref, first, q) in enumerate(places):
        ref[first, q] = tile[at * 16 : at * 16 + 16].astype(BF16)


def spots_three(refs, q_of):
    return [(ref, a, q_of(r)) for ref in refs for a in range(4) for r in range(3)]


def backward_mlp(my_core, upstream, gain_m, proj, up, down, store, keep, send):
    mixed_s, middle_s, second_s, hidden_s, slope_s = store
    both = (keep, send)
    down_in = upstream.astype(BF16)
    picks = pick(order_three(my_core))
    rows_up = turned(picks, second_s[...])
    picks_down = pick(order_twelve(my_core))
    second_grad = None
    stacked = jnp.concatenate([hidden_s[:, pl.ds(j * D, D)] for j in range(FF // D)], axis=0)
    rows = turned(picks_down, stacked)
    for j in range(FF // D):
        tile = mm(rows[:, j * ROWS : j * ROWS + ROWS], down_in)
        emit(tile, [(ref, j, r) for ref in both for r in range(12)])
    for j in range(FF // WIDE):
        cols = pl.ds(j * WIDE, WIDE)
        up_in = (slope_s[:, cols].astype(F32) * mm_nt(down_in, down[cols, :])).astype(BF16)
        tile = mm(rows_up, up_in)
        for i in range(WIDE // D):
            at = 12 + (j * (WIDE // D) + i) * 3
            emit(tile[:, i * D : i * D + D], spots_three(both, lambda r, at=at: at + r))
        part = mm_nt(up_in, up[:, cols])
        second_grad = part if second_grad is None else second_grad + part
    middle_grad = upstream + norm_pull(middle_s[...], gain_m, second_grad)
    proj_in = middle_grad.astype(BF16)
    emit(mm(turned(picks, mixed_s[...]), proj_in), spots_three(both, lambda r: 24 + r))
    return middle_grad, mm_nt(proj_in, proj[...]).astype(BF16)


def backward_attention(
    my_core, middle_grad, mixed_grad, stream_s, gain_a, qkv, store, wides, first_q, wide_s
):
    normed_s, triple_s, probs_s, mixed_s = store
    for pair in range(3):
        lanes = pl.ds(pair * 128, 128)
        q = triple_s[:, lanes] * 0.125
        k = triple_s[:, pl.ds(D + pair * 128, 128)]
        v = triple_s[:, pl.ds(2 * D + pair * 128, 128)]
        mg = mixed_grad[:, pair * 128 : pair * 128 + 128]
        product = mg.astype(F32) * mixed_s[:, lanes].astype(F32)
        dq = dk = dv = None
        for h in range(2):
            mask = head_mask(128, h)
            probs = probs_s[pair * 2 + h]
            mg_h = jnp.where(mask, mg, 0.0).astype(BF16)
            delta = jnp.sum(jnp.where(mask, product, 0.0), axis=-1, keepdims=True)
            probs_grad = mm_nt(mg_h, v)
            scores_grad = (probs.astype(F32) * (probs_grad - delta)).astype(BF16)
            part_q = mm(scores_grad, jnp.where(mask, k, 0.0).astype(BF16))
            part_k = mm_tn(scores_grad, jnp.where(mask, q, 0.0).astype(BF16))
            part_v = mm_tn(probs, mg_h)
            dq = part_q if dq is None else dq + part_q
            dk = part_k if dk is None else dk + part_k
            dv = part_v if dv is None else dv + part_v
        wide_s[:, lanes] = (dq * 0.125).astype(BF16)
        wide_s[:, pl.ds(D + pair * 128, 128)] = dk.astype(BF16)
        wide_s[:, pl.ds(2 * D + pair * 128, 128)] = dv.astype(BF16)
    rows_qkv = turned(pick(order_three(my_core)), normed_s[...])
    tile = mm(rows_qkv, wide_s[...])
    for j in range(3):
        emit(tile[:, j * D : j * D + D], spots_three(wides, lambda r, j=j: first_q + j * 3 + r))
    normed_grad = mm_nt(wide_s[...], qkv[...])
    return middle_grad + norm_pull(stream_s[...], gain_a, normed_grad)


def store_shapes():
    return [
        ((ROWS, D), BF16),
        ((ROWS, 3 * D), BF16),
        ((HEADS, ROWS, ROWS), BF16),
        ((ROWS, D), BF16),
        ((ROWS, D), F32),
        ((ROWS, D), BF16),
        ((ROWS, FF), BF16),
        ((ROWS, FF), BF16),
    ]


def whole(shape):
    return pl.BlockSpec(shape, lambda *_: (0,) * len(shape))


def shapes_of(items):
    return [jax.ShapeDtypeStruct(s, d) for s, d in items]


WEIGHTS = {
    "qkv": ((D, 3 * D), BF16),
    "proj": ((D, D), BF16),
    "up": ((D, FF), BF16),
    "down": ((FF, D), BF16),
}
STORES = dict(
    zip(
        ("normed", "triple", "probs", "mixed", "middle", "second", "hidden", "slope"),
        store_shapes(),
        strict=True,
    )
)
ANY_SPEC = pl.BlockSpec(memory_space=pl.ANY)
SCALARS = pl.BlockSpec(memory_space=pltpu.SMEM)
IN_VMEM = pl.BlockSpec(memory_space=pltpu.VMEM)
IN_HBM = pl.BlockSpec(memory_space=pltpu.HBM)


def gather_kernel(axis, *rest):
    pieces, out = rest[:4], rest[5]
    at = dict(zip("zxy", place_of_device()))[axis]
    for step, piece in zip((0, *STEPS), pieces, strict=True):
        out[lax.bitwise_and(at - step, 3)] = piece[...]


def gather_ring(axis, pieces, after):
    return local_kernel(
        partial(gather_kernel, axis),
        (*pieces, after),
        [((4, *pieces[0].shape), BF16)],
        [],
        "gather_ring",
    )[0]


def hold_kernel(source, out, sem):
    copy = pltpu.make_async_copy(source, out, sem.at[0])
    copy.start()
    copy.wait()


def hold(value):
    outs = [(value.shape, value.dtype)]
    return big_kernel(
        hold_kernel, [(in_hbm(value), IN_HBM)], outs, [], 1000000, 1, "hold"
    )[0]


def join_kernel(own, other, out):
    my_core = place_of_device()[3]
    out[my_core] = own[...]
    out[1 - my_core] = other[...]


def join_cores(own, other):
    return local_kernel(join_kernel, (own, other), [((2, 2, D), BF16)], [], "join_cores")[0]


def take_kernel(slot_of, _, *rest):
    pieces, (out, held_s) = rest[:4], rest[4:]
    z, x, y, my_core = place_of_device()
    for step, piece in zip((0, *STEPS), pieces, strict=True):
        held_s[lax.bitwise_and(y - step, 3)] = piece[...]
    device = z * 32 + x * 8 + y * 2 + my_core
    row = iota((2, 1), 0)
    taken = []
    for env in range(2):
        slot = slot_of[device * 2 + env]
        pair = held_s[
            lax.bitwise_and(lax.shift_right_logical(slot, 2), 3),
            lax.bitwise_and(lax.shift_right_logical(slot, 4), 3),
            lax.shift_right_logical(slot, 6),
            lax.bitwise_and(lax.shift_right_logical(slot, 1), 1),
        ].astype(F32)
        chosen = row == lax.bitwise_and(slot, 1)
        taken.append(jnp.sum(jnp.where(chosen, pair, 0.0), axis=0, keepdims=True))
    out[...] = jnp.where(row == 0, taken[0], taken[1])


def take_rows(slot_of, pieces, after):
    return pl.pallas_call(
        take_kernel,
        in_specs=[SCALARS, ANY_SPEC] + [IN_VMEM] * 4,
        out_specs=[IN_VMEM],
        out_shape=shapes_of([((2, D), F32)]),
        scratch_shapes=[pltpu.VMEM((4, 4, 4, 2, 2, D), BF16)],
        compiler_params=pltpu.CompilerParams(vmem_limit_bytes=SMALL_VMEM_BYTES),
        name="take_rows",
    )(slot_of, after, *pieces)[0]


def big_kernel(kernel, operands, outs, scratch, flops, copies, name):
    return pl.pallas_call(
        kernel,
        in_specs=[spec for _, spec in operands],
        out_specs=[IN_VMEM for _ in outs],
        out_shape=shapes_of(outs),
        scratch_shapes=[(pltpu.VMEM if d != jnp.int32 else pltpu.SMEM)(s, d) for s, d in scratch]
        + [pltpu.SemaphoreType.DMA((copies,))] * (copies > 0),
        compiler_params=pltpu.CompilerParams(vmem_limit_bytes=VMEM_BYTES),
        cost_estimate=pl.CostEstimate(flops=flops, bytes_accessed=8000000, transcendentals=0),
        name=name,
    )(*[v for v, _ in operands])


def in_hbm(value):
    return pltpu.with_memory_space_constraint(value, pltpu.HBM)


def embed_kernel(
    counts, images, patch_weight, pos, gain_a, qkv, proj, gain_m, up, down, final_gain, *rest
):
    rows_o, stream_o, store, held, gains = rest[0], rest[1], rest[2:7], rest[7:11], rest[11:14]
    counts_o, flat_s, images_s, patch_s, pos_s, sems = rest[14:]
    first_copies = [
        pltpu.make_async_copy(source, target, sems.at[8 + at])
        for at, (source, target) in enumerate(
            (
                (images, images_s),
                (counts, counts_o),
                (patch_weight, patch_s),
                (pos, pos_s),
                (gain_a, gains[0]),
                (gain_m, gains[1]),
                (final_gain, gains[2]),
            )
        )
    ]
    copies = {}
    for layer in range(2):
        for at, (source, target) in enumerate(zip((qkv, proj, up, down), held, strict=True)):
            copies[layer, at] = pltpu.make_async_copy(
                source.at[layer], target.at[layer], sems.at[layer * 4 + at]
            )
    for copy in first_copies + list(copies.values()):
        copy.start()
    first_copies[0].wait()
    for env in range(2):
        for patch in range(PATCHES):
            at = (env * PATCHES + patch) * CAMS
            flat_s[pl.ds(at, CAMS)] = images_s[env, patch].astype(F32)
    first_copies[1].wait()
    first, second = counts_o[0], counts_o[1]
    row = iota((ROWS, 1), 0)
    cam = steps_of(row, PATCHES, CAM_MOST + 1)
    patch = row - cam * PATCHES
    slot = jnp.where(cam < first, cam, CAMS * PATCHES + cam - first)
    used = cam < first + second
    source = jnp.where(used, slot + patch * CAMS, -1)
    rows = mm(
        jnp.where(source == iota((ROWS, SLOTS * PATCHES), 1), 1.0, 0.0).astype(BF16),
        flat_s[...].astype(BF16),
    ).astype(BF16)
    rows_o[...] = rows
    place = jnp.where(used & (patch == iota((ROWS, PATCHES), 1)), 1.0, 0.0).astype(BF16)
    for copy in first_copies[2:]:
        copy.wait()
    stream = mm(rows, patch_s[...]) + mm(place, pos_s[...])
    stream_o[...] = stream
    attention_half(
        stream,
        gains[0][0:1],
        held[0].at[0],
        held[1].at[0],
        store,
        lambda at: copies[0, at].wait(),
    )
    for key in ((0, 2), (0, 3), (1, 0), (1, 1), (1, 2), (1, 3)):
        copies[key].wait()


STORE_A = ("normed", "triple", "probs", "mixed", "middle")
STORE_M = ("second", "hidden", "slope")


def run_embed(counts, images, patch_weight, pos, params, final_gain):
    gain_a, qkv, proj, gain_m, up, down = params
    sources = (counts, images, patch_weight, pos, gain_a, qkv, proj, gain_m, up, down, final_gain)
    got = big_kernel(
        embed_kernel,
        [(in_hbm(v), IN_HBM) for v in sources],
        [((ROWS, PATCH_DIM), BF16), ((ROWS, D), F32)]
        + [STORES[k] for k in STORE_A]
        + [((2, *s), d) for s, d in WEIGHTS.values()]
        + [((2, D), F32), ((2, D), F32), ((D,), F32)],
        [
            ((2,), jnp.int32),
            ((SLOTS * PATCHES, PATCH_DIM), F32),
            (images.shape, BF16),
            ((PATCH_DIM, D), BF16),
            ((PATCHES, D), BF16),
        ],
        7000000000,
        15,
        "embed_attend",
    )
    gain_a, gain_m, final_gain = got[11:14]
    params = (gain_a, *got[7:9], gain_m, *got[9:11])
    return got[0], got[1], dict(zip(STORE_A, got[2:7])), params, final_gain


def middle_kernel(middle, gain_a, gain_m, up, down, qkv, proj, _, *rest):
    stream_o, store_m, store_a = rest[0], rest[1:4], rest[4:9]
    stream_o[...] = mlp_half(middle[...], gain_m[0:1], up.at[0], down.at[0], store_m)
    attention_half(
        stream_o[...], gain_a[1:2], qkv.at[1], proj.at[1], store_a, lambda at: None
    )


def run_middle(middle, params, after):
    gain_a, qkv, proj, gain_m, up, down = params
    got = big_kernel(
        middle_kernel,
        [(v, IN_VMEM) for v in (middle, gain_a, gain_m, up, down, qkv, proj)] + [(after, ANY_SPEC)],
        [((ROWS, D), F32)] + [STORES[k] for k in STORE_M + STORE_A],
        [],
        6000000000,
        0,
        "mlp_attend",
    )
    return got[0], dict(zip(STORE_M, got[1:4])), dict(zip(STORE_A, got[4:9]))


def pool_kernel(counts, middle, gain_m, up, down, final_gain, _, *rest):
    pooled_o, tokens_o, store_m = rest[0], rest[1], rest[2:5]
    last = mlp_half(middle[...], gain_m[1:2], up.at[1], down.at[1], store_m)
    pooled = exact_mm(camera_members(), last) * (1.0 / PATCHES)
    pooled_o[...] = pooled
    embedded = norm_rows(pooled, final_gain[...][None])
    first, second = counts[0], counts[1]
    cam = iota((SLOTS, 1), 0)
    in_first = cam < first
    in_second = (cam >= first) & (cam < first + second)
    sum_first = jnp.sum(jnp.where(in_first, embedded, 0.0), axis=0, keepdims=True)
    sum_second = jnp.sum(jnp.where(in_second, embedded, 0.0), axis=0, keepdims=True)
    row = iota((SLOTS, 1), 0)
    count_col = jnp.where(row == 0, first, second).astype(F32)
    both = jnp.where(row == 0, sum_first, jnp.where(row == 1, sum_second, 0.0))
    tokens_o[...] = (both / count_col).astype(BF16)


def run_pool(counts, middle, params, final_gain, after):
    _, _, _, gain_m, up, down = params
    got = big_kernel(
        pool_kernel,
        [(counts, SCALARS)]
        + [(v, IN_VMEM) for v in (middle, gain_m, up, down, final_gain)]
        + [(after, ANY_SPEC)],
        [((SLOTS, D), F32), ((SLOTS, D), BF16)] + [STORES[k] for k in STORE_M],
        [],
        4000000000,
        0,
        "mlp_pool",
    )
    return got[0], got[1], dict(zip(STORE_M, got[2:5]))


def camera_members():
    cam = steps_of(iota((1, ROWS), 1), PATCHES, CAM_MOST + 1)
    return jnp.where(cam == iota((SLOTS, 1), 0), 1.0, 0.0)


GRAD_COUNTS = {"second": (12, 24), "first_mlp": (12, 15), "first_attention": (0, 11), "first_patch": (0, 6)}


ROWS_D, ROWS_W = (sum(n) for n in zip(*GRAD_COUNTS.values()))


def grad_shapes(group):
    return [((4, sum(GRAD_COUNTS[group]), 16, D), BF16)] * 2


def place_of_device():
    env = lax.axis_index("env")
    return (
        lax.axis_index("grp"),
        lax.shift_right_logical(env, 3),
        lax.bitwise_and(lax.shift_right_logical(env, 1), 3),
        lax.bitwise_and(env, 1),
    )


SECOND_IN = ("second", "hidden", "down", "slope", "up", "middle", "mixed", "proj")
ATTENTION_IN = ("triple", "probs", "normed", "qkv")


def of_layer(names, refs, layer):
    refs = dict(zip(names, refs))
    return {key: ref.at[layer] if key in WEIGHTS else ref for key, ref in refs.items()}


def back_second_kernel(counts, seeds, pooled, final_gain, gain_a, gain_m, *rest):
    names = SECOND_IN + ATTENTION_IN + ("stream",)
    held, rest = of_layer(names, rest, 1), rest[len(names) :]
    keep, send, grad_o, wide_s = rest
    my_core = place_of_device()[3]
    first, second = counts[0], counts[1]
    cam = iota((SLOTS, 1), 0)
    seed = jnp.where(
        cam < first,
        seeds[0:1] / first.astype(F32),
        jnp.where(cam < first + second, seeds[1:2] / second.astype(F32), 0.0),
    )
    pooled_grad = norm_pull(pooled[...], final_gain[...][None], seed) * (1.0 / PATCHES)
    cam_row = steps_of(iota((ROWS, 1), 0), PATCHES, CAM_MOST + 1)
    member = jnp.where(cam_row == iota((1, SLOTS), 1), 1.0, 0.0)
    upstream = exact_mm(member, pooled_grad)
    middle_grad, mixed_grad = backward_mlp(
        my_core,
        upstream,
        gain_m[1:2],
        held["proj"],
        held["up"],
        held["down"],
        [held[k] for k in ("mixed", "middle", "second", "hidden", "slope")],
        keep,
        send,
    )
    grad_o[...] = backward_attention(
        my_core,
        middle_grad,
        mixed_grad,
        held["stream"],
        gain_a[1:2],
        held["qkv"],
        [held[k] for k in ("normed", "triple", "probs", "mixed")],
        (keep, send),
        27,
        wide_s,
    )


def run_back_second(counts, seeds, pooled, final_gain, stream, params, store):
    gain_a, qkv, proj, gain_m, up, down = params
    values = {"qkv": qkv, "proj": proj, "up": up, "down": down, "stream": stream}
    values.update(store)
    names = SECOND_IN + ATTENTION_IN + ("stream",)
    return big_kernel(
        back_second_kernel,
        [(counts, SCALARS)]
        + [(v, IN_VMEM) for v in (seeds, pooled, final_gain, gain_a, gain_m)]
        + [(values[k], IN_VMEM) for k in names],
        grad_shapes("second") + [((ROWS, D), F32)],
        [((ROWS, 3 * D), BF16)],
        8000000000,
        0,
        "back_second",
    )


def back_mlp_kernel(gain_m, *rest):
    names = ("stream",) + SECOND_IN
    held, rest = of_layer(names, rest, 0), rest[len(names) :]
    keep, send, middle_o, mixed_o = rest
    middle_o[...], mixed_o[...] = backward_mlp(
        place_of_device()[3],
        held["stream"][...],
        gain_m[0:1],
        held["proj"],
        held["up"],
        held["down"],
        [held[k] for k in ("mixed", "middle", "second", "hidden", "slope")],
        keep,
        send,
    )


def run_back_mlp(upstream, params, store):
    _, _, proj, gain_m, up, down = params
    values = {"proj": proj, "up": up, "down": down, "stream": upstream}
    values.update(store)
    names = ("stream",) + SECOND_IN
    return big_kernel(
        back_mlp_kernel,
        [(gain_m, IN_VMEM)] + [(values[k], IN_VMEM) for k in names],
        grad_shapes("first_mlp") + [((ROWS, D), F32), ((ROWS, D), BF16)],
        [],
        5000000000,
        0,
        "back_first_mlp",
    )


def back_attention_kernel(slot_of, tokens, middle_grad, mixed_grad, gain_a, *rest):
    names = ("mixed",) + ATTENTION_IN + ("stream",)
    held, rest = of_layer(names, rest, 0), rest[len(names) :]
    keep, send, grad_o, wide_s = rest
    z, x, y, my_core = place_of_device()
    device = z * 32 + x * 8 + y * 2 + my_core
    p = iota((ROWS, 1), 0)
    swap = jnp.where(p >= 128, 1, 0)
    core = jnp.where(swap == my_core, 0, 1)
    rest_p = p - swap * 128
    first = lax.shift_right_logical(rest_p, 5)
    row = lax.bitwise_and(lax.shift_right_logical(rest_p, 4), 1)
    third = lax.bitwise_and(rest_p, 3)
    to_x, to_y = jnp.where(core == 0, first, third), jnp.where(core == 0, third, first)
    to_z = lax.bitwise_and(lax.shift_right_logical(rest_p, 2), 3)
    learner = to_z * 64 + to_x * 16 + to_y * 4 + core * 2 + row
    lane = iota((1, SLOTS), 1)
    wanted = jnp.where(
        lane == 0, slot_of[device * 2], jnp.where(lane == 1, slot_of[device * 2 + 1], -1)
    )
    spread = mm(jnp.where(learner == wanted, 1.0, 0.0).astype(BF16), tokens[...]).astype(BF16)
    spots = [(ref, a, r) for ref in (keep, send) for a in range(4) for r in range(2)]
    for at, (ref, a, r) in enumerate(spots):
        ref[a, 9 + r] = spread[at * 16 : at * 16 + 16]
    stream_grad = backward_attention(
        my_core,
        middle_grad[...],
        mixed_grad[...],
        held["stream"],
        gain_a[0:1],
        held["qkv"],
        [held[k] for k in ("normed", "triple", "probs", "mixed")],
        (keep, send),
        0,
        wide_s,
    ).astype(BF16)
    grad_o[...] = stream_grad


def back_patch_kernel(rows, grad, keep, send):
    my_core = place_of_device()[3]
    for ref, core in ((keep, my_core), (send, 1 - my_core)):
        tile = mm(turned(pick(order_six(core), PATCH_DIM), rows[...]), grad[...])
        emit(tile, [(ref, a, r) for a in range(4) for r in range(6)])


def run_back_patch(rows, grad):
    return big_kernel(
        back_patch_kernel,
        [(rows, IN_VMEM), (grad, IN_VMEM)],
        grad_shapes("first_patch"),
        [],
        1000000000,
        0,
        "back_patch",
    )


def run_back_attention(slot_of, tokens, middle_grad, mixed_grad, stream, params, store):
    values = {"qkv": params[1], "stream": stream}
    values.update(store)
    names = ("mixed",) + ATTENTION_IN + ("stream",)
    return big_kernel(
        back_attention_kernel,
        [(slot_of, SCALARS)]
        + [(v, IN_VMEM) for v in (tokens, middle_grad, mixed_grad, params[0])]
        + [(values[k], IN_VMEM) for k in names],
        grad_shapes("first_attention") + [((ROWS, D), BF16)],
        [((ROWS, 3 * D), BF16)],
        4000000000,
        0,
        "back_first_attention",
    )


def local_kernel(kernel, operands, outs, scratch, name):
    return pl.pallas_call(
        kernel,
        in_specs=[IN_VMEM for _ in operands],
        out_specs=[IN_VMEM for _ in outs],
        out_shape=shapes_of(outs),
        scratch_shapes=scratch,
        compiler_params=pltpu.CompilerParams(vmem_limit_bytes=SMALL_VMEM_BYTES),
        name=name,
    )(*operands)


def add_kernel(*rest):
    parts, outs = rest[:-8], rest[-8:]
    z, x, y, my_core = place_of_device()
    along = jnp.where(my_core == 0, x, y)
    at_d = at_w = 0
    for group, (count_d, count_w) in enumerate(GRAD_COUNTS.values()):
        keep, got = parts[group * 2 : group * 2 + 2]
        for step in range(4):
            place_d, place_w = lax.bitwise_and(z + step, 3), lax.bitwise_and(along + step, 3)
            if count_d:
                span = pl.ds(0, count_d)
                outs[step][pl.ds(at_d, count_d)] = keep[place_d, span] + got[place_d, span]
            span = pl.ds(count_d, count_w)
            outs[4 + step][pl.ds(at_w, count_w)] = keep[place_w, span] + got[place_w, span]
        at_d, at_w = at_d + count_d, at_w + count_w


def add_pairs(*parts):
    return local_kernel(
        add_kernel,
        parts,
        [((ROWS_D, 16, D), BF16)] * 4 + [((ROWS_W, 16, D), BF16)] * 4,
        [],
        "add_pairs",
    )


def sum_of(refs):
    total = refs[0][...].astype(F32)
    for ref in refs[1:]:
        total = total + ref[...].astype(F32)
    return total


def place_on(axes):
    z, x, y, my_core = place_of_device()
    by_name = {"z": z, "x": x, "y": y}
    return jnp.where(my_core == 0, by_name[axes[0]], by_name[axes[1]])


def first_sum_kernel(axes, *rest):
    parts, outs, total_s = rest[:4], rest[4:8], rest[8]
    count = parts[0].shape[0]
    total = sum_of(parts).reshape(count * 16, D)
    for lanes in range(3):
        total_s[lanes] = total[:, lanes * 128 : lanes * 128 + 128]
    along = place_on(axes)
    for step in range(4):
        second = lax.bitwise_and(along + step, 3)
        for lanes in range(3):
            rows = [total_s[lanes, pl.ds(second * 4 + third, count, 16)] for third in range(4)]
            outs[step][:, pl.ds(lanes * 128, 128)] = jnp.concatenate(rows, axis=0).astype(BF16)


def first_sum(axes, parts):
    count = parts[0].shape[0]
    return local_kernel(
        partial(first_sum_kernel, axes),
        parts,
        [((4 * count, D), BF16)] * 4,
        [pltpu.VMEM((3, count * 16, 128), F32)],
        "first_sum",
    )


def wide_sum_kernel(*rest):
    rest[4][...] = sum_of(rest[:4])


def wide_sum(parts):
    return local_kernel(wide_sum_kernel, parts, [((4 * ROWS_W, D), F32)], [], "wide_sum")


def second_sum_kernel(*rest):
    parts, wide, outs, total_s = rest[:4], rest[4], rest[5:9], rest[9]
    total_d, total_w = sum_of(parts), wide[...]
    for third in range(4):
        total_s[third, pl.ds(0, ROWS_D)] = total_d[third * ROWS_D : (third + 1) * ROWS_D]
        total_s[third, pl.ds(ROWS_D, ROWS_W)] = total_w[third * ROWS_W : (third + 1) * ROWS_W]
    _, x, y, my_core = place_of_device()
    along = jnp.where(my_core == 0, y, x)
    for step in range(4):
        outs[step][...] = total_s[lax.bitwise_and(along + step, 3)].astype(BF16)


def second_sum(parts):
    return local_kernel(
        second_sum_kernel,
        parts,
        [((ROWS_D + ROWS_W, D), BF16)] * 4,
        [pltpu.VMEM((4, ROWS_D + ROWS_W, D), F32)],
        "second_sum",
    )


def last_sum_kernel(*rest):
    parts, (tokens, patch, qkv, proj, up, down) = rest[:4], rest[4:]
    rows = sum_of(parts)
    down[:, 1], down[:, 0] = rows[0:12], rows[12:24]
    wide = rows[ROWS_D:]
    for layer, at_up, at_qkv in ((1, 0, 15), (0, 24, 39)):
        for j in range(4):
            up[:, layer, pl.ds(j * D, D)] = wide[at_up + j * 3 : at_up + j * 3 + 3]
        proj[:, layer] = wide[at_up + 12 : at_up + 15]
        for j in range(3):
            qkv[:, layer, pl.ds(j * D, D)] = wide[at_qkv + j * 3 : at_qkv + j * 3 + 3]
    tokens[...] = wide[48:50].astype(BF16)
    patch[...] = wide[50:56]


def last_sum(parts):
    return local_kernel(
        last_sum_kernel,
        parts,
        [
            ((2, D), BF16),
            ((6, D), F32),
            ((3, 2, 3 * D), F32),
            ((3, 2, D), F32),
            ((3, 2, FF), F32),
            ((12, 2, D), F32),
        ],
        [],
        "last_sum",
    )


AXES = ("grp", "env")
STEPS = (2, 1, 3)


def send_along(value, axes, step):
    pairs = []
    for device in range(128):
        z, x, y, core = device // 32, device // 8 % 4, device // 2 % 4, device % 2
        place = {"z": z, "x": x, "y": y}
        place[axes[core]] = (place[axes[core]] + step) % 4
        pairs.append((device, place["z"] * 32 + place["x"] * 8 + place["y"] * 2 + core))
    return lax.ppermute(value, AXES, pairs)


def swap_cores(value):
    return lax.ppermute(value, AXES, [(device, device ^ 1) for device in range(128)])


def exchange(pieces, axes):
    return [pieces[0]] + [send_along(pieces[step], axes, step) for step in STEPS]


def per_device(
    images,
    camera_counts,
    slot_of,
    patch_weight,
    pos_embed,
    attn_gain,
    qkv_weight,
    proj_weight,
    mlp_gain,
    up_weight,
    down_weight,
    final_gain,
    cotangent,
):
    params = (attn_gain, qkv_weight, proj_weight, mlp_gain, up_weight, down_weight)
    chip = join_cores(hold(cotangent), swap_cores(cotangent))
    ring = exchange([chip] * 4, "zz")
    rows, stream, store_first, params, final_gain = run_embed(
        camera_counts,
        jnp.swapaxes(images, 1, 2),
        patch_weight,
        pos_embed,
        params,
        final_gain,
    )
    line = gather_ring("z", ring, final_gain)
    ring = exchange([line] * 4, "xx")
    middle_stream, store, store_second = run_middle(store_first["middle"], params, line)
    store_first.update(store)
    plane = gather_ring("x", ring, store["second"])
    ring = exchange([plane] * 4, "yy")
    pooled, tokens, store = run_pool(
        camera_counts, store_second["middle"], params, final_gain, plane
    )
    store_second.update(store)
    seeds = take_rows(slot_of, ring, pooled)
    keep_second, send, stream_grad = run_back_second(
        camera_counts,
        seeds,
        pooled,
        final_gain,
        middle_stream,
        params,
        store_second,
    )
    got_second = swap_cores(send)
    keep_mlp, send, middle_grad, mixed_grad = run_back_mlp(stream_grad, params, store_first)
    got_mlp = swap_cores(send)
    keep, send, grad = run_back_attention(
        slot_of,
        tokens,
        middle_grad,
        mixed_grad,
        stream,
        params,
        store_first,
    )
    got = swap_cores(send)
    keep_patch, send = run_back_patch(rows, grad)
    got_patch = swap_cores(send)
    pieces = add_pairs(keep_second, got_second, keep_mlp, got_mlp, keep, got, keep_patch, got_patch)
    wide = exchange(pieces[4:], "xy")
    deep = exchange(pieces[:4], "zz")
    wide = exchange(first_sum("zz", wide), "zz")
    deep = exchange(first_sum("xy", deep), "xy")
    pieces = second_sum([*deep, *wide_sum(wide)])
    tokens, patch, *stacks = last_sum(exchange(pieces, "yx"))
    return (tokens, patch, *(jnp.swapaxes(stack, 0, 1) for stack in stacks))


def solution(mesh):
    placed = (
        P(("grp", "env"), None, None, None),
        P(("grp", "env")),
        P(),
        P(),
        P(),
        P(),
        P(),
        P(),
        P(),
        P(),
        P(),
        P(),
        P(("grp", "env"), None),
    )
    return jax.shard_map(
        per_device,
        mesh=mesh,
        in_specs=placed,
        out_specs=(
            P(("grp", "env"), None),
            P(("grp", "env"), None),
            P(None, ("grp", "env"), None),
            P(None, ("grp", "env"), None),
            P(None, ("grp", "env"), None),
            P(None, ("grp", "env"), None),
        ),
        check_vma=False,
    )
```
